32 devices in a mesh: region: 16 (over z, y, x), tile: 2 (over core).
Axes of the slice: x: 2, y: 2, z: 4, core: 2. Of those that a mesh axis runs over, the one named last changes fastest.
Arguments:
- innovations: float32 [64, 16384], P(None, ('region', 'tile')), may hold values from -6 to 6
- obs_geometry: float32 [3, 16384], P(None, ('region', 'tile')), may hold values from 0 to 32, as said below
- obs_error: float32 [16384], P(('region', 'tile')), may hold values from 0.25 to 1
- tile_owner: int32 [16, 7], P('region'), may hold values from -1 to 1, as said below
Outputs:
- weights: float32 [64, 16384], P(None, ('region', 'tile'))
- residual: float32 [64, 16384], P(None, ('region', 'tile'))
The draws below stay inside these ranges and needn't reach their ends.
Inputs may be any that keep to these rules, and one draw needn't show every extreme that they name: tile_owner[i, k] names the device along tile that computes the tile of regions i and i + k, or is -1 where that pair is not listed. A region lists the offsets 0 to e - 1 for some e of 1 to 7, and i + k is a region for every listed pair. No device owns more than 4 tiles of its region, and some device owns exactly 4. `obs_geometry`: the standard deviations lie between 0.5 and 2. The operator A built from these positions and the listed tiles is symmetric positive definite.
All inputs are finite; a program needn't handle non-finite values.
Results may differ from the reference program's by a relative error of at most 0.0098.
Values may be sent and summed in bfloat16 or wider, within the bound.
No kernel may reach another device: no remote copies, remote signals or barrier semaphores. Data moves between devices by JAX's collectives and lax.ppermute only.
A program may use at most 128 MiB of HBM per device.

```python
import math
import jax
import jax.numpy as jnp
from jax import lax

OBS_REG = 1024
COLS = 64
REACH = 7
ITERS = 2
REGIONS = 16
OBS = 16384
N_TILE = 2


def region_layout(key):
    folded = jax.random.fold_in(key, 7311)
    subkeys = jax.random.split(folded, 4)
    drawn = jax.random.randint(subkeys[0], (REGIONS,), 5, REACH + 1)
    drawn = drawn.at[0].set(REACH)
    regions = jnp.arange(REGIONS, dtype=jnp.int32)
    extent = jnp.minimum(drawn, REGIONS - regions)
    return (extent, drawn, subkeys)


def draw_tile_owner(key, part):
    extent, drawn, subkeys = region_layout(key)
    heaviest = jax.random.randint(subkeys[1], (REGIONS,), 0, N_TILE)
    heaviest = heaviest.at[0].set(N_TILE - 1)
    lowest = jnp.maximum(1, extent - 4)
    highest = jnp.minimum(4, extent)
    heavy_count = jax.random.randint(subkeys[2], (REGIONS,), lowest, highest + 1)
    heavy_count = heavy_count.at[0].set(4)
    rotation = jax.random.randint(subkeys[3], (REGIONS,), 0, N_TILE - 1)
    offsets = jnp.arange(REACH, dtype=jnp.int32)[None, :]
    beyond = offsets - heavy_count[:, None]
    others = (heaviest[:, None] + 1 + (beyond + rotation[:, None]) % (N_TILE - 1)) % N_TILE
    owning = jnp.where(offsets < heavy_count[:, None], heaviest[:, None], others)
    return jnp.where(offsets < extent[:, None], owning, -1).astype(jnp.int32)


def draw_obs_geometry(key, part):
    extent, drawn, subkeys = region_layout(key)
    pieces = jax.random.split(jax.random.fold_in(key, 977), 3)
    along_x = jax.random.uniform(pieces[0], (REGIONS, OBS_REG), jnp.float32)
    across_y = jax.random.uniform(pieces[1], (REGIONS, OBS_REG), jnp.float32)
    regions = jnp.arange(REGIONS).astype(jnp.float32)[:, None]
    span_x = 0.5 * drawn.astype(jnp.float32)[:, None] - 1.0
    position_x = 0.5 * regions + along_x * span_x
    position_y = across_y * (OBS_REG / 32.0)
    spread = jax.random.uniform(pieces[2], (REGIONS, OBS_REG), jnp.float32, 0.8, 1.25)
    return jnp.stack([position_x.reshape(-1), position_y.reshape(-1), spread.reshape(-1)]).astype(jnp.float32)


def shard_levels(stream_key, shape, shards, smallest, high):
    loudness = 1.0
    for dim, shards_of in shards:
        steps = jax.random.uniform(jax.random.fold_in(jax.random.fold_in(stream_key, 6), dim), (shards_of,), jnp.float32, smallest / len(shards), high / len(shards))
        loudness = loudness * jnp.repeat(jnp.exp(steps), shape[dim] // shards_of).reshape((-1,) + (1,) * (len(shape) - 1 - dim))
    return loudness


def scatter_about(rng, shape, scale, limit, cuts=(), kind=jnp.bfloat16):
    result = jax.random.normal(rng, shape, jnp.float32) * scale
    if len(cuts) > 0:
        result = shard_levels(rng, shape, cuts, -0.22, 0.18) * result
    return jnp.clip(result, min=-limit, max=limit).astype(kind)


def setup_inputs(seed: int = 0) -> dict:
    splits = jax.random.split(jax.random.key(seed), 5)
    return {
        "innovations": scatter_about(splits[0], (COLS, OBS), 1.0, 6.0, ((1, 32),), jnp.float32),
        "obs_geometry": draw_obs_geometry(jax.random.fold_in(splits[4], 71), 0),
        "obs_error": jnp.clip(jnp.exp(math.log(1.0) - 1.3862944 * jax.random.uniform(splits[2], (OBS,), jnp.float32) ** shard_levels(splits[2], (OBS,), ((0, 32),), -0.2, 0.2)), 0.25, 1.0),
        "tile_owner": draw_tile_owner(jax.random.fold_in(splits[4], 71), 0),
    }


gc_length = 0.5

def gaspari_cohn(distance):
    scaled = distance / gc_length
    bounded = jnp.maximum(scaled, 1.0)
    near_part = (((-0.25 * scaled + 0.5) * scaled + 0.625) * scaled - 5.0 / 3.0) * scaled * scaled + 1.0
    far_part = ((((scaled / 12.0 - 0.5) * scaled + 0.625) * scaled + 5.0 / 3.0) * scaled - 5.0) * scaled + 4.0 - 2.0 / (3.0 * bounded)
    return jnp.where(scaled <= 1.0, near_part, jnp.where(scaled <= 2.0, far_part, 0.0))

def build_tile(home_rows, far_rows):
    across_x = home_rows[0][:, None] - far_rows[0][None, :]
    across_y = home_rows[1][:, None] - far_rows[1][None, :]
    distance = jnp.sqrt(across_x * across_x + across_y * across_y)
    return (home_rows[2][:, None] * far_rows[2][None, :] * gaspari_cohn(distance)).astype(jnp.bfloat16)

def gram_matrix(left_rows, right_rows):
    return jnp.dot(left_rows.astype(jnp.float32), right_rows.T.astype(jnp.float32), precision=lax.Precision.HIGHEST, preferred_element_type=jnp.float32)

def gram_solve(gram_value, target):
    symmetric = 0.5 * (gram_value + gram_value.T)
    factor = jnp.linalg.cholesky(symmetric)
    interim = lax.linalg.triangular_solve(factor, target, left_side=True, lower=True)
    return lax.linalg.triangular_solve(factor, interim, left_side=True, lower=True, transpose_a=True)

def apply_operator(direction, places, obs_error, tile_owner):
    rounded = direction.astype(jnp.bfloat16)
    blocks = jnp.transpose(rounded.reshape(COLS, REGIONS, OBS_REG), (1, 0, 2))

    def region_step(summed, region):
        for offset in range(REACH):
            partner = jnp.minimum(region + offset, REGIONS - 1).astype(jnp.int32)
            listed = tile_owner[region, offset] >= 0

            def add_tile(current, partner=partner, offset=offset):
                tile_block = build_tile(places[region], places[partner])
                to_home = lax.dot_general(blocks[partner].astype(jnp.float32), tile_block.astype(jnp.float32), (((1,), (1,)), ((), ())), preferred_element_type=jnp.float32)
                current = current.at[region].add(to_home)
                if offset > 0:
                    to_partner = jnp.dot(blocks[region].astype(jnp.float32), tile_block.astype(jnp.float32), preferred_element_type=jnp.float32)
                    current = current.at[partner].add(to_partner)
                return current

            def keep_summed(current):
                return current
            summed = lax.cond(listed, add_tile, keep_summed, summed)
        return (summed, None)
    summed, unused = lax.scan(region_step, jnp.zeros((REGIONS, COLS, OBS_REG), jnp.float32), jnp.arange(REGIONS, dtype=jnp.int32))
    coupled = jnp.transpose(summed, (1, 0, 2)).reshape(COLS, OBS)
    return obs_error[None, :] * direction + coupled

def reference(innovations, obs_geometry, obs_error, tile_owner):
    places = jnp.transpose(obs_geometry.reshape(3, REGIONS, OBS_REG), (1, 0, 2))
    weights = jnp.zeros_like(innovations)
    residual = innovations
    direction = innovations
    squares = gram_matrix(residual, residual)
    for iteration in range(ITERS):
        image_block = apply_operator(direction, places, obs_error, tile_owner)
        curvature = gram_matrix(direction, image_block)
        step_size = gram_solve(curvature, squares)
        weights = weights + jnp.dot(step_size.T, direction, precision=lax.Precision.HIGHEST)
        residual = residual - jnp.dot(step_size.T, image_block, precision=lax.Precision.HIGHEST)
        if iteration + 1 < ITERS:
            next_squares = gram_matrix(residual, residual)
            conjugacy = gram_solve(squares, next_squares)
            direction = residual + jnp.dot(conjugacy.T, direction, precision=lax.Precision.HIGHEST)
            squares = next_squares
    return (weights, residual)
```

```python
import functools

import jax
import jax.numpy as jnp
from jax import lax
from jax.experimental import pallas as pl
from jax.experimental.pallas import tpu as pltpu
from jax.sharding import PartitionSpec as P

CUTOFF = 1.001
LANES = 128
ROWS = 64
BATCH = 4
GROUP = 4
RING = 4
VMEM = 60 * 1024 * 1024
HIGHEST = lax.Precision.HIGHEST


def whole_vmem(count):
    return [pl.BlockSpec(memory_space=pltpu.VMEM)] * count


def dot_nt(left, right, precision=None):
    return lax.dot_general(
        left, right, (((1,), (1,)), ((), ())), precision=precision, preferred_element_type=jnp.float32
    )


def dot_nn(left, right, precision=None):
    return lax.dot_general(
        left, right, (((1,), (0,)), ((), ())), precision=precision, preferred_element_type=jnp.float32
    )


def three_parts(value):
    high = value.astype(jnp.bfloat16)
    rest = value - high.astype(jnp.float32)
    middle = rest.astype(jnp.bfloat16)
    low = (rest - middle.astype(jnp.float32)).astype(jnp.bfloat16)
    return high, middle, low


def exchange(block, offsets, axis):
    count = lax.axis_size(axis)
    gathered = block[None]
    bit = count // 2
    while bit:
        other = lax.ppermute(gathered, axis, [(i, i ^ bit) for i in range(count)])
        gathered = jnp.concatenate([gathered, other], axis=0)
        bit //= 2
    return gathered


def slot_offsets(count):
    offsets = [0]
    bit = count // 2
    while bit:
        offsets = offsets + [o ^ bit for o in offsets]
        bit //= 2
    return offsets


def sum_over(block, axis):
    count = lax.axis_size(axis)
    bit = 1
    while bit < count:
        block = block + lax.ppermute(block, axis, [(i, i ^ bit) for i in range(count)])
        bit *= 2
    return block


def fill_order(rank, order_ref):
    n = order_ref.shape[0]
    step = 64

    def fill(block, carry):
        start = pl.multiple_of(block * step, step)
        place = (start + lax.broadcasted_iota(jnp.int32, (step, n), 0)).astype(jnp.float32)
        order_ref[pl.ds(start, step), :] = jnp.where(place == rank, 1.0, 0.0).astype(jnp.bfloat16)
        return carry

    lax.fori_loop(0, n // step, fill, 0)


def sort_kernel(places_ref, y_ref, block_ref, places_out, block_out, rounded_out, rank_out, order_ref):
    n = places_ref.shape[1]
    step = 64
    y_row = places_ref[1:2, :]
    index_row = lax.broadcasted_iota(jnp.int32, (step, n), 1)

    def count(block, total):
        start = pl.multiple_of(block * step, step)
        y_column = y_ref[pl.ds(start, step), :]
        index_column = start + lax.broadcasted_iota(jnp.int32, (step, n), 0)
        before = (y_column < y_row) | ((y_column == y_row) & (index_column < index_row))
        return total + jnp.sum(jnp.where(before, 1.0, 0.0).reshape(step // 8, 8, n), axis=0)

    total = lax.fori_loop(0, n // step, count, jnp.zeros((8, n), jnp.float32))
    rank = jnp.sum(total, axis=0, keepdims=True)
    rank_out[...] = rank
    fill_order(rank, order_ref)
    order = order_ref[...]
    places_out[...] = sum(dot_nt(part, order) for part in reversed(three_parts(places_ref[...])))
    sorted_block = sum(dot_nt(part, order) for part in reversed(three_parts(block_ref[...])))
    block_out[...] = sorted_block
    rounded_out[...] = sorted_block.astype(jnp.bfloat16)


def sort_region(places, block):
    n = places.shape[1]
    columns = block.shape[0]
    return pl.pallas_call(
        sort_kernel,
        out_shape=(
            jax.ShapeDtypeStruct(places.shape, jnp.float32),
            jax.ShapeDtypeStruct(block.shape, jnp.float32),
            jax.ShapeDtypeStruct(block.shape, jnp.bfloat16),
            jax.ShapeDtypeStruct((1, n), jnp.float32),
        ),
        in_specs=whole_vmem(3),
        out_specs=tuple(whole_vmem(4)),
        scratch_shapes=[pltpu.VMEM((n, n), jnp.bfloat16)],
        compiler_params=pltpu.CompilerParams(vmem_limit_bytes=VMEM),
        cost_estimate=pl.CostEstimate(
            flops=6 * n * n * (columns + 8), bytes_accessed=4 * n * n, transcendentals=0
        ),
        name="sort_region",
    )(places, places[1][:, None], block)


def unsort_kernel(rank_ref, block_ref, block_out, order_ref):
    fill_order(rank_ref[...], order_ref)
    order = order_ref[...]
    block_out[...] = sum(dot_nn(part, order) for part in reversed(three_parts(block_ref[...])))


def unsort(rank, block):
    n = block.shape[1]
    return pl.pallas_call(
        unsort_kernel,
        out_shape=jax.ShapeDtypeStruct(block.shape, jnp.float32),
        in_specs=whole_vmem(2),
        out_specs=whole_vmem(1)[0],
        scratch_shapes=[pltpu.VMEM((n, n), jnp.bfloat16)],
        compiler_params=pltpu.CompilerParams(vmem_limit_bytes=VMEM),
        cost_estimate=pl.CostEstimate(
            flops=6 * n * n * block.shape[0], bytes_accessed=4 * n * n, transcendentals=0
        ),
        name="unsort",
    )(rank, block)


def plan_blocks(own, everyone, listed, most):
    n = own.shape[1]
    slots = everyone.shape[0]
    chunks = n // LANES
    y = everyone[:, 1, :].reshape(slots * chunks, LANES)
    y_own = own[1].reshape(n // ROWS, ROWS)
    near = (y[None, :, 0] <= y_own[:, -1:] + CUTOFF) & (y[None, :, -1] >= y_own[:, :1] - CUTOFF)
    active = near & jnp.repeat(listed, chunks)[None, :]
    total = slots * chunks
    index = jnp.arange(total, dtype=jnp.int32)
    counted = active.astype(jnp.int32)
    place = jnp.sum(
        jnp.where(index[None, :, None] < index[None, None, :], counted[:, :, None], 0), axis=1
    )
    length = most * chunks
    spot = jnp.arange(length, dtype=jnp.int32)
    hit = active[:, :, None] & (place[:, :, None] == spot[None, None, :])
    ids = jnp.sum(jnp.where(hit, index[None, :, None] + 1, 0), axis=1) - 1
    batches = (jnp.sum(counted, axis=1) + BATCH - 1) // BATCH
    blocks = jnp.arange(n // ROWS, dtype=jnp.int32)
    base = jnp.sum(jnp.where(blocks[None, :] < blocks[:, None], batches[None, :], 0), axis=1)
    return ids.reshape(-1), jnp.concatenate([batches, base])


def gaspari_cohn(squared):
    squared = jnp.maximum(squared, 1e-12)
    inverse = lax.rsqrt(squared)
    scaled = squared * inverse
    near = (((-0.25 * scaled + 0.5) * scaled + 0.625) * scaled - 5.0 / 3.0) * squared + 1.0
    left = jnp.maximum(2.0 - scaled, 0.0)
    left = left * left
    far = (left * left) * ((scaled + 2.0) * scaled - 0.5) * (inverse * (1.0 / 12.0))
    return jnp.where(scaled <= 1.0, near, far)


def build_kernel(length, ids_ref, plan_ref, own_ref, all_ref, tiles_ref, wide_ref, ring_ref, sems):
    n = own_ref.shape[1]
    blocks = n // ROWS
    chunks = n // LANES
    column = jnp.transpose(own_ref[...])
    for row in range(3):
        wide_ref[row] = jnp.broadcast_to(column[:, row : row + 1], (n, LANES))

    def copy_out(slot, batch):
        return pltpu.make_async_copy(ring_ref.at[slot], tiles_ref.at[batch], sems.at[slot])

    def build_block(block, carry):
        start = pl.multiple_of(block * ROWS, ROWS)
        base = plan_ref[blocks + block]

        def build_batch(step, inner):
            batch = base + step
            slot = lax.rem(batch, RING)

            @pl.when(batch >= RING)
            def _():
                copy_out(slot, batch).wait()

            for part in range(BATCH):
                entry = ids_ref[block * length + step * BATCH + part]
                chunk = jnp.maximum(entry, 0)
                place = chunk // chunks
                lane = pl.multiple_of((chunk - place * chunks) * LANES, LANES)
                far = all_ref[place, :, pl.ds(lane, LANES)]
                across_x = 2.0 * wide_ref[0, pl.ds(start, ROWS), :] - 2.0 * far[0:1, :]
                across_y = 2.0 * wide_ref[1, pl.ds(start, ROWS), :] - 2.0 * far[1:2, :]
                value = gaspari_cohn(across_x * across_x + across_y * across_y)
                spread = jnp.where(entry >= 0, far[2:3, :], 0.0)
                value = wide_ref[2, pl.ds(start, ROWS), :] * spread * value
                ring_ref[slot, :, part * LANES : (part + 1) * LANES] = value.astype(jnp.bfloat16)
            copy_out(slot, batch).start()
            return inner

        return lax.fori_loop(0, plan_ref[block], build_batch, carry)

    lax.fori_loop(0, blocks, build_block, 0)
    total = plan_ref[blocks - 1] + plan_ref[2 * blocks - 1]
    for slot in range(RING):

        @pl.when(slot < total)
        def _():
            copy_out(slot, slot).wait()


def build_tiles(ids, plan, own, everyone, length, capacity):
    n = own.shape[1]
    smem = pl.BlockSpec(memory_space=pltpu.SMEM)
    return pl.pallas_call(
        functools.partial(build_kernel, length),
        out_shape=jax.ShapeDtypeStruct((capacity, ROWS, BATCH * LANES), jnp.bfloat16),
        in_specs=[smem, smem] + whole_vmem(2),
        out_specs=pl.BlockSpec(memory_space=pl.ANY),
        scratch_shapes=[
            pltpu.VMEM((3, n, LANES), jnp.float32),
            pltpu.VMEM((RING, ROWS, BATCH * LANES), jnp.bfloat16),
            pltpu.SemaphoreType.DMA((RING,)),
        ],
        compiler_params=pltpu.CompilerParams(vmem_limit_bytes=VMEM),
        cost_estimate=pl.CostEstimate(
            flops=40 * 3 * n * n, bytes_accessed=8 * n * n, transcendentals=3 * n * n
        ),
        name="build_tiles",
    )(ids, plan, own, everyone)


def apply_kernel(
    length, ids_ref, plan_ref, tiles_ref, all_ref, block_ref, scale_ref, out_ref, rounded_ref,
    held_ref, total_ref, sems,
):
    columns, n = block_ref.shape
    blocks = n // ROWS
    chunks = n // LANES
    total = plan_ref[blocks - 1] + plan_ref[2 * blocks - 1]
    groups = (total + GROUP - 1) // GROUP

    def copy_in(group):
        start = group * GROUP
        return pltpu.make_async_copy(
            tiles_ref.at[pl.ds(start, GROUP)], held_ref.at[pl.ds(start, GROUP)], sems.at[group]
        )

    def start_copy(group, carry):
        copy_in(group).start()
        return carry

    lax.fori_loop(0, groups, start_copy, 0)

    def apply_block(block, carry):
        base = plan_ref[blocks + block]

        def apply_batch(step, value):
            batch = base + step

            @pl.when(lax.rem(batch, GROUP) == 0)
            def _():
                copy_in(batch // GROUP).wait()

            parts = []
            for part in range(BATCH):
                chunk = jnp.maximum(ids_ref[block * length + step * BATCH + part], 0)
                place = chunk // chunks
                lane = pl.multiple_of((chunk - place * chunks) * LANES, LANES)
                parts.append(all_ref[place, :, pl.ds(lane, LANES)])
            return value + dot_nt(held_ref[batch], jnp.concatenate(parts, axis=1))

        value = lax.fori_loop(
            0, plan_ref[block], apply_batch, jnp.zeros((ROWS, columns), jnp.float32)
        )
        total_ref[pl.ds(pl.multiple_of(block * ROWS, ROWS), ROWS), :] = value
        return carry

    lax.fori_loop(0, blocks, apply_block, 0)
    result = jnp.transpose(total_ref[...]) + scale_ref[...] * block_ref[...]
    out_ref[...] = result
    rounded_ref[...] = result.astype(jnp.bfloat16)


def apply_tiles(ids, plan, tiles, everyone, block, scale, length):
    columns, n = block.shape
    smem = pl.BlockSpec(memory_space=pltpu.SMEM)
    return pl.pallas_call(
        functools.partial(apply_kernel, length),
        out_shape=(
            jax.ShapeDtypeStruct(block.shape, jnp.float32),
            jax.ShapeDtypeStruct(block.shape, jnp.bfloat16),
        ),
        in_specs=[smem, smem, pl.BlockSpec(memory_space=pl.ANY)] + whole_vmem(3),
        out_specs=tuple(whole_vmem(2)),
        scratch_shapes=[
            pltpu.VMEM(tiles.shape, jnp.bfloat16),
            pltpu.VMEM((n, columns), jnp.float32),
            pltpu.SemaphoreType.DMA((tiles.shape[0] // GROUP,)),
        ],
        compiler_params=pltpu.CompilerParams(vmem_limit_bytes=VMEM),
        cost_estimate=pl.CostEstimate(
            flops=6 * n * n * columns, bytes_accessed=8 * n * n, transcendentals=0
        ),
        name="apply_tiles",
    )(ids, plan, tiles, everyone, block, scale)


def solve_positive(matrix, target):
    n = matrix.shape[0]
    table = jnp.concatenate([0.5 * (matrix + jnp.transpose(matrix)), target], axis=1)
    bands = [table[k : k + 8, :] for k in range(0, n, 8)]
    row_index = lax.broadcasted_iota(jnp.int32, (8, 1), 0)
    for k in range(0, n, 2):
        own, row = k // 8, k % 8
        firsts = [band[:, k : k + 1] for band in bands]
        seconds = [band[:, k + 1 : k + 2] for band in bands]
        a, b = firsts[own][row : row + 1, :], seconds[own][row : row + 1, :]
        c, d = firsts[own][row + 1 : row + 2, :], seconds[own][row + 1 : row + 2, :]
        determinant = a * d - b * c
        inverse = lax.rsqrt(determinant)
        inverse = inverse * inverse
        inverse = inverse * (2.0 - determinant * inverse)
        upper, lower = bands[own][row : row + 1, :], bands[own][row + 1 : row + 2, :]
        new_upper = (d * upper - b * lower) * inverse
        new_lower = (a * lower - c * upper) * inverse
        bands = [
            band - (first * new_upper + second * new_lower)
            for band, first, second in zip(bands, firsts, seconds)
        ]
        bands[own] = jnp.where(
            row_index == row, new_upper, jnp.where(row_index == row + 1, new_lower, bands[own])
        )
    return jnp.concatenate([band[:, n:] for band in bands], axis=0)


def gram_kernel(left_ref, right_ref, out_ref):
    left, right = left_ref[...], right_ref[...]
    out_ref[0] = dot_nt(left, left, HIGHEST)
    out_ref[1] = dot_nt(left, right, HIGHEST)
    out_ref[2] = dot_nt(right, right, HIGHEST)


def gram_matrices(left, right):
    n = left.shape[0]
    return pl.pallas_call(
        gram_kernel,
        out_shape=jax.ShapeDtypeStruct((3, n, n), jnp.float32),
        in_specs=whole_vmem(2),
        out_specs=whole_vmem(1)[0],
        name="gram_matrices",
    )(left, right)


def cross_kernel(left_ref, right_ref, out_ref):
    out_ref[...] = dot_nt(left_ref[...], right_ref[...], HIGHEST)


def cross_gram(left, right):
    return pl.pallas_call(
        cross_kernel,
        out_shape=jax.ShapeDtypeStruct((left.shape[0], right.shape[0]), jnp.float32),
        in_specs=whole_vmem(2),
        out_specs=whole_vmem(1)[0],
        name="cross_gram",
    )(left, right)


def first_kernel(grams_ref, out_ref):
    squares, mixed, images = grams_ref[0], grams_ref[1], grams_ref[2]
    n = squares.shape[0]
    step = solve_positive(mixed, squares)
    step_t = jnp.transpose(step)
    cross = dot_nn(mixed, step, HIGHEST)
    after = squares - cross - jnp.transpose(cross) + dot_nn(step_t, dot_nn(images, step, HIGHEST), HIGHEST)
    turn = solve_positive(squares, after)
    eye = (
        lax.broadcasted_iota(jnp.int32, (n, n), 0) == lax.broadcasted_iota(jnp.int32, (n, n), 1)
    ).astype(jnp.float32)
    lead = eye + jnp.transpose(turn)
    part = dot_nn(lead, dot_nn(images, step, HIGHEST), HIGHEST)
    known = dot_nt(dot_nn(lead, mixed, HIGHEST), lead, HIGHEST) - part - jnp.transpose(part)
    out_ref[0] = step_t
    out_ref[1] = lead
    out_ref[2] = after
    out_ref[3] = known


def first_step(grams):
    n = grams.shape[1]
    return pl.pallas_call(
        first_kernel,
        out_shape=jax.ShapeDtypeStruct((4, n, n), jnp.float32),
        in_specs=whole_vmem(1),
        out_specs=whole_vmem(1)[0],
        name="first_step",
    )(grams)


def last_kernel(first_ref, cross_ref, start_ref, image_ref, second_ref, weights_ref, residual_ref):
    step_t, lead, after, known = first_ref[0], first_ref[1], first_ref[2], first_ref[3]
    curvature = known + dot_nt(dot_nn(step_t, cross_ref[...], HIGHEST), step_t, HIGHEST)
    last_t = jnp.transpose(solve_positive(curvature, after))
    outer = step_t + dot_nn(last_t, lead, HIGHEST)
    inner = dot_nn(last_t, step_t, HIGHEST)
    start, image = start_ref[...], image_ref[...]
    weights_ref[...] = dot_nn(outer, start, HIGHEST) - dot_nn(inner, image, HIGHEST)
    residual_ref[...] = start - dot_nn(outer, image, HIGHEST) + dot_nn(inner, second_ref[...], HIGHEST)


def last_step(first, cross, start, image, second):
    return pl.pallas_call(
        last_kernel,
        out_shape=(jax.ShapeDtypeStruct(start.shape, jnp.float32),) * 2,
        in_specs=whole_vmem(5),
        out_specs=tuple(whole_vmem(2)),
        name="last_step",
    )(first, cross, start, image, second)


def shards(innovations, obs_geometry, obs_error, tile_owner):
    regions = lax.axis_size("region")
    reach = tile_owner.shape[1]
    here = lax.axis_index("region")
    offsets = slot_offsets(regions)

    def to_columns(block):
        return lax.all_to_all(block, "tile", 0, 1, tiled=True)

    def to_rows(block):
        return lax.all_to_all(block, "tile", 1, 0, tiled=True)

    places = lax.all_gather(
        jnp.concatenate([obs_geometry, obs_error[None, :]], axis=0), "tile", axis=1, tiled=True
    )
    n = places.shape[1]
    chunks = n // LANES
    places, start, rounded, rank = sort_region(places, to_columns(innovations))
    scale = places[3:4]

    flags = jnp.where(tile_owner[0] >= 0, 1.0, 0.0).astype(jnp.float32)
    flag_row = jnp.zeros((1, n), jnp.float32).at[0, :reach].set(flags)
    message = jnp.concatenate([places[:3], flag_row], axis=0)
    everyone = exchange(message, offsets, "region")
    region = here ^ jnp.array(offsets, jnp.int32)
    distance = region - here
    ahead = jnp.arange(reach, dtype=jnp.int32)
    own_flag = jnp.sum(jnp.where(distance[:, None] == ahead[None, :], flags[None, :], 0.0), axis=1)
    far_flag = jnp.sum(
        jnp.where(-distance[:, None] == ahead[None, :], everyone[:, 3, :reach], 0.0), axis=1
    )
    listed = (own_flag + far_flag) > 0.5

    most = min(regions, 2 * reach - 1)
    length = -(-most * chunks // BATCH) * BATCH
    capacity = (n // ROWS) * (length // BATCH)
    capacity = -(-capacity // GROUP) * GROUP
    ids, plan = plan_blocks(places, everyone, listed, most)
    tiles = build_tiles(ids, plan, places, everyone, length, capacity)

    apply = functools.partial(apply_tiles, ids, plan, tiles, length=length)
    image, image_rounded = apply(exchange(rounded, offsets, "region"), start, scale)
    image_all = lax.all_gather(image, "tile", axis=0, tiled=True)
    image_rows = to_rows(unsort(rank, image))
    grams = lax.psum(gram_matrices(innovations, image_rows), ("region", "tile"))

    second, _ = apply(exchange(image_rounded, offsets, "region"), image, scale)
    cross = sum_over(cross_gram(image_all, second), "region")
    cross = lax.all_gather(cross, "tile", axis=1, tiled=True)
    second_rows = to_rows(unsort(rank, second))
    first = first_step(grams)
    return last_step(first, cross, innovations, image_rows, second_rows)


def solution(mesh):
    return jax.shard_map(
        shards,
        mesh=mesh,
        in_specs=(
            P(None, ("region", "tile")),
            P(None, ("region", "tile")),
            P(("region", "tile")),
            P("region", None),
        ),
        out_specs=(P(None, ("region", "tile")), P(None, ("region", "tile"))),
        check_vma=False,
    )
```

```python
import functools

import jax
import jax.numpy as jnp
from jax import lax
from jax.experimental import pallas as pl
from jax.experimental.pallas import tpu as pltpu
from jax.sharding import PartitionSpec as P

CUTOFF = 1.001
LANES = 128
PLANE = 4
ROWS = 64
BATCH = 4
GROUP = 4
UNROLL = 4
RING = 4
VMEM = 60 * 1024 * 1024
HIGHEST = lax.Precision.HIGHEST


def whole_vmem(count):
    return [pl.BlockSpec(memory_space=pltpu.VMEM)] * count


def dot_nt(left, right, precision=None):
    return lax.dot_general(
        left, right, (((1,), (1,)), ((), ())), precision=precision, preferred_element_type=jnp.float32
    )


def dot_nn(left, right, precision=None):
    return lax.dot_general(
        left, right, (((1,), (0,)), ((), ())), precision=precision, preferred_element_type=jnp.float32
    )


def three_parts(value):
    high = value.astype(jnp.bfloat16)
    rest = value - high.astype(jnp.float32)
    middle = rest.astype(jnp.bfloat16)
    low = (rest - middle.astype(jnp.float32)).astype(jnp.bfloat16)
    return high, middle, low


def partners(axis, bit):
    return [(i, i ^ bit) for i in range(lax.axis_size(axis))]


def swap_all(block, axis, join):
    bit = 1
    while bit < lax.axis_size(axis):
        block = jnp.concatenate([block, lax.ppermute(block, axis, partners(axis, bit))], axis=join)
        bit *= 2
    return block


def from_ahead(block, distance):
    count = lax.axis_size("region")
    route = [(i + distance, i) for i in range(count) if 0 <= i + distance < count]
    return lax.ppermute(block, "region", route)


def window_regions(reach):
    here = lax.axis_index("region")
    place, base = here % PLANE, here // PLANE * PLANE
    within = jnp.arange(PLANE, dtype=jnp.int32)
    pieces = [base + (place ^ within)]
    for step in range(1, (reach - 2) // PLANE + 2):
        keep = min(PLANE, reach - 1 - (step - 1) * PLANE)
        for sign in (1, -1):
            first = jnp.where(sign > 0, 0, PLANE - keep)
            order = within if keep == PLANE else (within[:keep] ^ (place & (keep - 1)))
            found = (place ^ within) if keep == PLANE else first + order
            pieces.append(base + sign * step * PLANE + found)
    return jnp.concatenate(pieces)


def window(block, reach):
    place = lax.axis_index("region") % PLANE
    block = block[None]
    bit = 1
    while bit < PLANE:
        block = jnp.concatenate([block, lax.ppermute(block, "region", partners("region", bit))], axis=0)
        bit *= 2
    pieces = [block]
    for step in range(1, (reach - 2) // PLANE + 2):
        keep = min(PLANE, reach - 1 - (step - 1) * PLANE)
        for sign in (1, -1):
            sent = block
            if keep < PLANE:
                first = 0 if sign > 0 else PLANE - keep
                sent = lax.dynamic_slice_in_dim(block, (place ^ first) // keep * keep, keep, axis=0)
            pieces.append(from_ahead(sent, sign * step * PLANE))
    return pieces


def sum_over(block, axis):
    count = lax.axis_size(axis)
    bit = 1
    while bit < count:
        block = block + lax.ppermute(block, axis, [(i, i ^ bit) for i in range(count)])
        bit *= 2
    return block


def stacked_parts(value):
    return jnp.concatenate([part.astype(jnp.float32) for part in three_parts(value)], axis=0).astype(
        jnp.bfloat16
    )


def add_parts(value):
    rows = value.shape[0] // 3
    return (value[2 * rows :] + value[rows : 2 * rows]) + value[:rows]


def fill_order(first, rank, order_ref, row, count):
    step = 64

    def fill(block, carry):
        start = pl.multiple_of(block * step, step)
        place = first + start + lax.broadcasted_iota(jnp.int32, (step, rank.shape[1]), 0)
        order_ref[pl.ds(pl.multiple_of(row + start, step), step), :] = jnp.where(
            place == rank, 1.0, 0.0
        ).astype(jnp.bfloat16)
        return carry

    lax.fori_loop(0, count // step, fill, 0)


def sort_kernel(first_ref, places_ref, column_ref, block_ref, places_out, block_out, rounded_out, rank_out, order_ref):
    n = places_ref.shape[1]
    local = block_out.shape[1]
    step = 64
    y_row, index_row = places_ref[1:2, :], places_ref[4:5, :]

    def count(block, total):
        start = pl.multiple_of(block * step, step)
        y_column = jnp.broadcast_to(column_ref[pl.ds(start, step), 0:1], (step, n))
        index_column = jnp.broadcast_to(column_ref[pl.ds(start, step), 1:2], (step, n))
        before = (y_column < y_row) | ((y_column == y_row) & (index_column < index_row))
        return total + jnp.sum(jnp.where(before, 1.0, 0.0).reshape(step // 8, 8, n), axis=0)

    total = lax.fori_loop(0, n // step, count, jnp.zeros((8, n), jnp.float32))
    rank = jnp.sum(total, axis=0, keepdims=True).astype(jnp.int32)
    rank_out[...] = rank[:, :local]
    fill_order(first_ref[0], rank, order_ref, 0, local)
    order = order_ref[...]
    places_out[...] = add_parts(dot_nt(stacked_parts(places_ref[...]), order))
    sorted_block = add_parts(dot_nt(stacked_parts(block_ref[...]), order))
    block_out[...] = sorted_block
    rounded_out[...] = sorted_block.astype(jnp.bfloat16)


def sort_region(first, places, block, local):
    n = places.shape[1]
    columns = block.shape[0]
    return pl.pallas_call(
        sort_kernel,
        out_shape=(
            jax.ShapeDtypeStruct((places.shape[0], local), jnp.float32),
            jax.ShapeDtypeStruct((columns, local), jnp.float32),
            jax.ShapeDtypeStruct((columns, local), jnp.bfloat16),
            jax.ShapeDtypeStruct((1, local), jnp.int32),
        ),
        in_specs=[pl.BlockSpec(memory_space=pltpu.SMEM)] + whole_vmem(3),
        out_specs=tuple(whole_vmem(4)),
        scratch_shapes=[pltpu.VMEM((local, n), jnp.bfloat16)],
        compiler_params=pltpu.CompilerParams(vmem_limit_bytes=VMEM),
        cost_estimate=pl.CostEstimate(
            flops=6 * n * local * (columns + 8), bytes_accessed=4 * n * local, transcendentals=0
        ),
        name="sort_region",
    )(first[:1], places, jnp.stack([places[1], places[4]], axis=1), block)


def unsort_kernel(first_ref, rank_ref, block_ref, block_out, order_ref):
    n, local = order_ref.shape
    for slot in range(n // local):
        fill_order(first_ref[slot], rank_ref[...], order_ref, slot * local, local)
    block_out[...] = add_parts(dot_nn(stacked_parts(block_ref[...]), order_ref[...]))


def unsort(first, rank, block):
    n = block.shape[1]
    local = rank.shape[1]
    return pl.pallas_call(
        unsort_kernel,
        out_shape=jax.ShapeDtypeStruct((block.shape[0], local), jnp.float32),
        in_specs=[pl.BlockSpec(memory_space=pltpu.SMEM)] + whole_vmem(2),
        out_specs=whole_vmem(1)[0],
        scratch_shapes=[pltpu.VMEM((n, local), jnp.bfloat16)],
        compiler_params=pltpu.CompilerParams(vmem_limit_bytes=VMEM),
        cost_estimate=pl.CostEstimate(
            flops=6 * n * local * block.shape[0], bytes_accessed=4 * n * local, transcendentals=0
        ),
        name="unsort",
    )(first, rank, block)


def plan_blocks(own, everyone, listed, length):
    n = own.shape[1]
    slots = everyone.shape[0]
    chunks = everyone.shape[2] // LANES
    y = everyone[:, 1, :].reshape(slots * chunks, LANES)
    y_own = own[1].reshape(n // ROWS, ROWS)
    near = (y[None, :, 0] <= y_own[:, -1:] + CUTOFF) & (y[None, :, -1] >= y_own[:, :1] - CUTOFF)
    active = near & jnp.broadcast_to(listed[:, None], (slots, chunks)).reshape(1, slots * chunks)
    total = slots * chunks
    index = jnp.arange(total, dtype=jnp.int32)
    counted = active.astype(jnp.int32)
    place = jnp.sum(
        jnp.where(index[None, :, None] < index[None, None, :], counted[:, :, None], 0), axis=1
    )
    spot = jnp.arange(length, dtype=jnp.int32)
    hit = active[:, :, None] & (place[:, :, None] == spot[None, None, :])
    ids = jnp.sum(jnp.where(hit, index[None, :, None] + 1, 0), axis=1) - 1
    batches = (jnp.sum(counted, axis=1) + BATCH - 1) // BATCH
    blocks = jnp.arange(n // ROWS, dtype=jnp.int32)
    base = jnp.sum(jnp.where(blocks[None, :] < blocks[:, None], batches[None, :], 0), axis=1)
    return ids.reshape(-1), jnp.concatenate([batches, base])


def gaspari_cohn(squared):
    squared = jnp.maximum(squared, 1e-12)
    inverse = lax.rsqrt(squared)
    scaled = squared * inverse
    near = (((-0.25 * scaled + 0.5) * scaled + 0.625) * scaled - 5.0 / 3.0) * squared + 1.0
    left = jnp.maximum(2.0 - scaled, 0.0)
    left = left * left
    far = (left * left) * ((scaled + 2.0) * scaled - 0.5) * (inverse * (1.0 / 12.0))
    return jnp.where(scaled <= 1.0, near, far)


def build_kernel(length, ids_ref, plan_ref, own_ref, all_ref, tiles_ref, wide_ref, ring_ref, sems):
    n = own_ref.shape[1]
    blocks = n // ROWS
    chunks = all_ref.shape[2] // LANES
    column = jnp.transpose(own_ref[...])
    for row in range(3):
        scale = 2.0 if row < 2 else 1.0
        wide_ref[row] = jnp.broadcast_to(scale * column[:, row : row + 1], (n, LANES))

    def copy_out(slot, batch):
        return pltpu.make_async_copy(ring_ref.at[slot], tiles_ref.at[batch], sems.at[slot])

    def build_block(block, carry):
        start = pl.multiple_of(block * ROWS, ROWS)
        base = plan_ref[blocks + block]

        def build_batch(step, inner):
            batch = base + step
            slot = lax.rem(batch, RING)

            @pl.when(batch >= RING)
            def _():
                copy_out(slot, batch).wait()

            for part in range(BATCH):
                entry = ids_ref[block * length + step * BATCH + part]
                chunk = jnp.maximum(entry, 0)
                place = chunk // chunks
                lane = pl.multiple_of((chunk - place * chunks) * LANES, LANES)
                far = all_ref[place, :, pl.ds(lane, LANES)]
                across_x = wide_ref[0, pl.ds(start, ROWS), :] - 2.0 * far[0:1, :]
                across_y = wide_ref[1, pl.ds(start, ROWS), :] - 2.0 * far[1:2, :]
                value = gaspari_cohn(across_x * across_x + across_y * across_y)
                spread = jnp.where(entry >= 0, far[2:3, :], 0.0)
                value = wide_ref[2, pl.ds(start, ROWS), :] * spread * value
                ring_ref[slot, :, part * LANES : (part + 1) * LANES] = value.astype(jnp.bfloat16)
            copy_out(slot, batch).start()
            return inner

        return lax.fori_loop(0, plan_ref[block], build_batch, carry)

    lax.fori_loop(0, blocks, build_block, 0)
    total = plan_ref[blocks - 1] + plan_ref[2 * blocks - 1]
    for slot in range(RING):

        @pl.when(slot < total)
        def _():
            copy_out(slot, slot).wait()


def build_tiles(ids, plan, own, everyone, length, capacity):
    n = own.shape[1]
    smem = pl.BlockSpec(memory_space=pltpu.SMEM)
    return pl.pallas_call(
        functools.partial(build_kernel, length),
        out_shape=jax.ShapeDtypeStruct((capacity, ROWS, BATCH * LANES), jnp.bfloat16),
        in_specs=[smem, smem] + whole_vmem(2),
        out_specs=pl.BlockSpec(memory_space=pl.ANY),
        scratch_shapes=[
            pltpu.VMEM((3, n, LANES), jnp.float32),
            pltpu.VMEM((RING, ROWS, BATCH * LANES), jnp.bfloat16),
            pltpu.SemaphoreType.DMA((RING,)),
        ],
        compiler_params=pltpu.CompilerParams(vmem_limit_bytes=VMEM),
        cost_estimate=pl.CostEstimate(
            flops=40 * 3 * n * n, bytes_accessed=8 * n * n, transcendentals=3 * n * n
        ),
        name="build_tiles",
    )(ids, plan, own, everyone)


def apply_kernel(length, wanted, ids_ref, plan_ref, tiles_ref, *refs):
    *piece_refs, block_ref, scale_ref, out_ref, rounded_ref, gram_ref = refs[:-5]
    held_ref, all_ref, total_ref, sems, piece_sems = refs[-5:]
    columns, n = block_ref.shape
    blocks = n // ROWS
    chunks = n // LANES
    slots = all_ref.shape[1]

    def pieces():
        half = all_ref.shape[0] // 2
        slot = 0
        for index in range(0, len(piece_refs), 2):
            count = piece_refs[index].shape[1]
            for part in range(2):
                yield pltpu.make_async_copy(
                    piece_refs[index + part],
                    all_ref.at[pl.ds(part * half, half), pl.ds(slot, count)],
                    piece_sems.at[index + part],
                )
            slot += count

    for copy in pieces():
        copy.start()
    total = plan_ref[blocks - 1] + plan_ref[2 * blocks - 1]
    groups = (total + GROUP - 1) // GROUP

    def copy_in(group):
        start = group * GROUP
        return pltpu.make_async_copy(
            tiles_ref.at[pl.ds(start, GROUP)], held_ref.at[pl.ds(start, GROUP)], sems.at[group]
        )

    def start_copy(group, carry):
        copy_in(group).start()
        return carry

    lax.fori_loop(0, groups, start_copy, 0)
    for copy in pieces():
        copy.wait()

    def apply_block(block, carry):
        base = plan_ref[blocks + block]

        batches = plan_ref[block]

        def apply_batches(turn, value):
            for inner in range(UNROLL):
                step = turn * UNROLL + inner
                batch = base + jnp.minimum(step, batches - 1)

                @pl.when((lax.rem(batch, GROUP) == 0) & (step < batches))
                def _(batch=batch):
                    copy_in(batch // GROUP).wait()

            sides, tiles = [], []
            for inner in range(UNROLL):
                step = turn * UNROLL + inner
                tiles.append(held_ref[base + jnp.minimum(step, batches - 1)])
                for part in range(BATCH):
                    entry = ids_ref[block * length + jnp.minimum(step, batches - 1) * BATCH + part]
                    chunk = jnp.maximum(entry, 0)
                    place = chunk // chunks
                    lane = pl.multiple_of((chunk - place * chunks) * LANES, LANES)
                    tile = place // slots
                    side = all_ref[tile, place - tile * slots, :, pl.ds(lane, LANES)]
                    sides.append(jnp.where(step < batches, side, jnp.zeros_like(side)))
            return value + dot_nt(jnp.concatenate(tiles, axis=1), jnp.concatenate(sides, axis=1))

        value = lax.fori_loop(
            0,
            (batches + UNROLL - 1) // UNROLL,
            apply_batches,
            jnp.zeros((ROWS, columns), jnp.float32),
        )
        total_ref[pl.ds(pl.multiple_of(block * ROWS, ROWS), ROWS), :] = value
        return carry

    lax.fori_loop(0, blocks, apply_block, 0)
    block = block_ref[...]
    result = jnp.transpose(total_ref[...]) + scale_ref[...] * block
    out_ref[...] = result
    rounded_ref[...] = result.astype(jnp.bfloat16)
    pairs = {"squares": (block, block), "mixed": (block, result), "images": (result, result)}
    for index, name in enumerate(wanted):
        gram_ref[index] = dot_nt(*pairs[name], HIGHEST)


def apply_tiles(ids, plan, tiles, pieces, block, scale, length, wanted):
    columns, n = block.shape
    smem = pl.BlockSpec(memory_space=pltpu.SMEM)
    anywhere = pl.BlockSpec(memory_space=pl.ANY)
    tile_slots = 2 * pieces[0].shape[0]
    slots = sum(piece.shape[1] for piece in pieces) // 2
    return pl.pallas_call(
        functools.partial(apply_kernel, length, wanted),
        out_shape=(
            jax.ShapeDtypeStruct(block.shape, jnp.float32),
            jax.ShapeDtypeStruct(block.shape, jnp.bfloat16),
            jax.ShapeDtypeStruct((len(wanted), columns, columns), jnp.float32),
        ),
        in_specs=[smem, smem, anywhere] + [anywhere] * len(pieces) + whole_vmem(2),
        out_specs=tuple(whole_vmem(3)),
        scratch_shapes=[
            pltpu.VMEM(tiles.shape, jnp.bfloat16),
            pltpu.VMEM((tile_slots, slots, columns, n), jnp.bfloat16),
            pltpu.VMEM((n, columns), jnp.float32),
            pltpu.SemaphoreType.DMA((tiles.shape[0] // GROUP,)),
            pltpu.SemaphoreType.DMA((len(pieces),)),
        ],
        compiler_params=pltpu.CompilerParams(vmem_limit_bytes=VMEM),
        cost_estimate=pl.CostEstimate(
            flops=6 * n * n * columns, bytes_accessed=8 * n * n, transcendentals=0
        ),
        name="apply_tiles",
    )(ids, plan, tiles, *pieces, block, scale)


def reciprocal(value):
    inverse = lax.rsqrt(value)
    inverse = inverse * inverse
    return inverse * (2.0 - value * inverse)


def small_product(left, right):
    return [[sum(l * r[j] for l, r in zip(row, right)) for j in range(len(right[0]))] for row in left]


def small_difference(left, right):
    return [[l - r for l, r in zip(*rows)] for rows in zip(left, right)]


def small_inverse(matrix):
    (a, b), (c, d) = matrix
    scale = reciprocal(a * d - b * c)
    return [[d * scale, -b * scale], [-c * scale, a * scale]]


def solve_positive(matrix, target):
    n = matrix.shape[0]
    table = jnp.concatenate([0.5 * (matrix + jnp.transpose(matrix)), target], axis=1)
    bands = [table[k : k + 8, :] for k in range(0, n, 8)]
    row_index = lax.broadcasted_iota(jnp.int32, bands[0].shape, 0)
    for k in range(0, n, 4):
        own, row = k // 8, k % 8
        columns = [
            [jnp.broadcast_to(band[:, k + j : k + j + 1], band.shape) for band in bands] for j in range(4)
        ]
        pivot = [[columns[j][own][row + i : row + i + 1] for j in range(4)] for i in range(4)]
        upper, lower = pivot[:2], pivot[2:]
        top = small_inverse([r[:2] for r in upper])
        factor = small_product([r[:2] for r in lower], top)
        right = [r[2:] for r in upper]
        rest = small_inverse(small_difference([r[2:] for r in lower], small_product(factor, right)))
        rows = [[bands[own][row + i : row + i + 1]] for i in range(4)]
        last = small_product(rest, small_difference(rows[2:], small_product(factor, rows[:2])))
        first = small_product(top, small_difference(rows[:2], small_product(right, last)))
        new = [r[0] for r in first + last]
        bands = [
            band - ((columns[0][i] * new[0] + columns[1][i] * new[1]) + (columns[2][i] * new[2] + columns[3][i] * new[3]))
            for i, band in enumerate(bands)
        ]
        for i in range(4):
            bands[own] = jnp.where(row_index == row + i, new[i], bands[own])
    return jnp.concatenate([band[:, n:] for band in bands], axis=0)


def first_kernel(grams_ref, out_ref):
    squares, mixed, images = grams_ref[0], grams_ref[1], grams_ref[2]
    n = squares.shape[0]
    step = solve_positive(mixed, squares)
    step_t = jnp.transpose(step)
    cross = dot_nn(mixed, step, HIGHEST)
    after = squares - cross - jnp.transpose(cross) + dot_nn(step_t, dot_nn(images, step, HIGHEST), HIGHEST)
    turn = solve_positive(squares, after)
    eye = (
        lax.broadcasted_iota(jnp.int32, (n, n), 0) == lax.broadcasted_iota(jnp.int32, (n, n), 1)
    ).astype(jnp.float32)
    lead = eye + jnp.transpose(turn)
    part = dot_nn(lead, dot_nn(images, step, HIGHEST), HIGHEST)
    known = dot_nt(dot_nn(lead, mixed, HIGHEST), lead, HIGHEST) - part - jnp.transpose(part)
    out_ref[0] = step_t
    out_ref[1] = lead
    out_ref[2] = after
    out_ref[3] = known


def first_step(grams):
    n = grams.shape[1]
    return pl.pallas_call(
        first_kernel,
        out_shape=jax.ShapeDtypeStruct((4, n, n), jnp.float32),
        in_specs=whole_vmem(1),
        out_specs=whole_vmem(1)[0],
        name="first_step",
    )(grams)


def last_kernel(first_ref, cross_ref, start_ref, images_ref, weights_ref, residual_ref):
    step_t, lead, after, known = first_ref[0], first_ref[1], first_ref[2], first_ref[3]
    n = step_t.shape[0]
    curvature = known + dot_nt(dot_nn(step_t, cross_ref[...], HIGHEST), step_t, HIGHEST)
    last_t = jnp.transpose(solve_positive(curvature, after))
    outer = step_t + dot_nn(last_t, lead, HIGHEST)
    inner = dot_nn(last_t, step_t, HIGHEST)
    start, image = start_ref[...], images_ref[:n, :]
    weights_ref[...] = dot_nn(outer, start, HIGHEST) - dot_nn(inner, image, HIGHEST)
    residual_ref[...] = start - dot_nn(outer, image, HIGHEST) + dot_nn(inner, images_ref[n:, :], HIGHEST)


def last_step(first, cross, start, images):
    return pl.pallas_call(
        last_kernel,
        out_shape=(jax.ShapeDtypeStruct(start.shape, jnp.float32),) * 2,
        in_specs=whole_vmem(4),
        out_specs=tuple(whole_vmem(2)),
        name="last_step",
    )(first, cross, start, images)


def shards(innovations, obs_geometry, obs_error, tile_owner):
    tiles_axis = lax.axis_size("tile")
    reach = tile_owner.shape[1]
    here, tile = lax.axis_index("region"), lax.axis_index("tile")
    columns, local = innovations.shape
    first = (tile ^ jnp.arange(tiles_axis, dtype=jnp.int32)) * local

    index = (first[0] + jnp.arange(local, dtype=jnp.int32)).astype(jnp.float32)
    places = jnp.concatenate([obs_geometry, obs_error[None, :], index[None, :]], axis=0)
    places = swap_all(places, "tile", 1)
    own, start, rounded, rank = sort_region(first, places, swap_all(innovations, "tile", 1), local)
    scale = own[3:4]

    flags = jnp.where(tile_owner[0] >= 0, 1.0, 0.0).astype(jnp.float32)
    flag_row = jnp.concatenate([flags, jnp.zeros((local - reach,), jnp.float32)])[None, :]
    message = swap_all(jnp.concatenate([own[:3], flag_row], axis=0)[None], "tile", 0)
    everyone = jnp.concatenate(window(message, reach), axis=0)
    slots = everyone.shape[0]
    region = window_regions(reach)
    distance = region - here
    ahead = jnp.arange(reach, dtype=jnp.int32)
    own_flag = jnp.sum(jnp.where(distance[:, None] == ahead[None, :], flags[None, :], 0.0), axis=1)
    far_flag = jnp.sum(
        jnp.where(-distance[:, None] == ahead[None, :], everyone[:, 0, 3, :reach], 0.0), axis=1
    )
    inside = (region >= 0) & (region < lax.axis_size("region"))
    listed = jnp.tile(inside & ((own_flag + far_flag) > 0.5), tiles_axis)
    everyone = jnp.swapaxes(everyone, 0, 1).reshape(tiles_axis * slots, 4, local)

    most = min(lax.axis_size("region"), 2 * reach - 1) * tiles_axis * (local // LANES)
    length = -(-most // BATCH) * BATCH
    capacity = (local // ROWS) * (length // BATCH)
    capacity = -(-capacity // GROUP) * GROUP
    ids, plan = plan_blocks(own, everyone, listed, length)
    tiles = build_tiles(ids, plan, own, everyone, length, capacity)

    def apply(rounded, block, wanted):
        pieces = []
        for piece in window(rounded, reach):
            piece = piece[None]
            bit = 1
            while 2 * bit < tiles_axis:
                piece = jnp.concatenate([piece, lax.ppermute(piece, "tile", partners("tile", bit))], axis=0)
                bit *= 2
            pieces += [piece, lax.ppermute(piece, "tile", partners("tile", bit))]
        return apply_tiles(ids, plan, tiles, pieces, block, scale, length, wanted)

    image, image_rounded, grams = apply(rounded, start, ("squares", "mixed", "images"))
    grams = sum_over(sum_over(grams, "tile"), "region")
    second, _, cross = apply(image_rounded, image, ("mixed",))
    cross = sum_over(sum_over(cross[0], "tile"), "region")
    images = swap_all(jnp.concatenate([image, second], axis=0), "tile", 1)
    images = unsort(first, rank, images)
    return last_step(first_step(grams), cross, innovations, images)


def solution(mesh):
    return jax.shard_map(
        shards,
        mesh=mesh,
        in_specs=(
            P(None, ("region", "tile")),
            P(None, ("region", "tile")),
            P(("region", "tile")),
            P("region", None),
        ),
        out_specs=(P(None, ("region", "tile")), P(None, ("region", "tile"))),
        check_vma=False,
    )
```

```python
import functools

import jax
import jax.numpy as jnp
from jax import lax
from jax.experimental import pallas as pl
from jax.experimental.pallas import tpu as pltpu
from jax.sharding import PartitionSpec as P

CUTOFF = 1.001
LANES = 128
ROWS = 64
BATCH = 4
UNROLL = 4
RING = 8
VMEM = 48 * 1024 * 1024
EXTRA = 16
HIGHEST = lax.Precision.HIGHEST


def whole_vmem(count):
    return [pl.BlockSpec(memory_space=pltpu.VMEM)] * count


def dot_nt(left, right, precision=None):
    return lax.dot_general(
        left, right, (((1,), (1,)), ((), ())), precision=precision, preferred_element_type=jnp.float32
    )


def dot_nn(left, right, precision=None):
    return lax.dot_general(
        left, right, (((1,), (0,)), ((), ())), precision=precision, preferred_element_type=jnp.float32
    )


def three_parts(value):
    high = value.astype(jnp.bfloat16)
    rest = value - high.astype(jnp.float32)
    middle = rest.astype(jnp.bfloat16)
    low = (rest - middle.astype(jnp.float32)).astype(jnp.bfloat16)
    return high, middle, low


def halves(block, axis):
    count = lax.axis_size(axis)
    block = block[None]
    bit = 1
    while 2 * bit < count:
        block = jnp.concatenate([block, swapped(block, axis, bit)], axis=0)
        bit *= 2
    return block, swapped(block, axis, bit)


def swapped(block, axis, bit):
    return lax.ppermute(block, axis, [(i, i ^ bit) for i in range(lax.axis_size(axis))])


def sum_over(block, axis):
    bit = 1
    while bit < lax.axis_size(axis):
        block = block + swapped(block, axis, bit)
        bit *= 2
    return block


def region_orders(count):
    bits = []
    bit = count // 2
    while bit:
        bits.append(bit)
        bit //= 2
    return bits, bits[:1] + bits[-1:] + bits[1:-1] if len(bits) > 2 else bits[::-1]


def slot_offsets(count):
    table = []
    for bits in region_orders(count):
        offsets = [0]
        for bit in bits:
            offsets = offsets + [offset ^ bit for offset in offsets]
        table.append(offsets)
    return jnp.array(table, jnp.int32)


def exchange(block):
    regions, tiles = lax.axis_size("region"), lax.axis_size("tile")
    block = block[None]
    for even, odd in zip(*region_orders(regions)):
        route = [
            (region * tiles + tile, (region ^ (odd if tile % 2 else even)) * tiles + tile)
            for region in range(regions)
            for tile in range(tiles)
        ]
        other = lax.ppermute(block, ("region", "tile"), route)
        if 2 * block.shape[0] == regions:
            return block, other
        block = jnp.concatenate([block, other], axis=0)


def stacked_parts(value):
    return jnp.concatenate([part.astype(jnp.float32) for part in three_parts(value)], axis=0).astype(
        jnp.bfloat16
    )


def add_parts(value):
    rows = value.shape[0] // 3
    return (value[2 * rows :] + value[rows : 2 * rows]) + value[:rows]


def fill_order(first, rank, order_ref, row, count):
    step = 64

    def fill(block, carry):
        start = pl.multiple_of(block * step, step)
        place = first + start + lax.broadcasted_iota(jnp.int32, (step, rank.shape[1]), 0)
        order_ref[pl.ds(pl.multiple_of(row + start, step), step), :] = jnp.where(
            place == rank, 1.0, 0.0
        ).astype(jnp.bfloat16)
        return carry

    lax.fori_loop(0, count // step, fill, 0)


def sort_kernel(
    first_ref, owner_ref, near_ref, far_ref, block_ref, other_ref,
    message_out, own_out, block_out, rank_out, order_ref, column_ref,
):
    columns, local = block_out.shape
    stacks = [near_ref[i] for i in range(near_ref.shape[0])] + [far_ref[i] for i in range(far_ref.shape[0])]
    places = jnp.concatenate(stacks, axis=1)
    n = places.shape[1]
    step = 64
    index = jnp.concatenate(
        [
            (first_ref[i] + lax.broadcasted_iota(jnp.int32, (1, local), 1)).astype(jnp.float32)
            for i in range(n // local)
        ],
        axis=1,
    )
    y_row = places[1:2, :]
    column_ref[...] = jnp.transpose(
        jnp.concatenate([y_row, index, jnp.zeros((6, n), jnp.float32)], axis=0)
    )

    def count(block, total):
        start = pl.multiple_of(block * step, step)
        y_column = jnp.broadcast_to(column_ref[pl.ds(start, step), 0:1], (step, n))
        index_column = jnp.broadcast_to(column_ref[pl.ds(start, step), 1:2], (step, n))
        before = (y_column < y_row) | ((y_column == y_row) & (index_column < index))
        return total + jnp.sum(jnp.where(before, 1.0, 0.0).reshape(step // 8, 8, n), axis=0)

    total = lax.fori_loop(0, n // step, count, jnp.zeros((8, n), jnp.float32))
    rank = jnp.sum(total, axis=0, keepdims=True).astype(jnp.int32)
    rank_out[...] = rank[:, :local]
    fill_order(first_ref[0], rank, order_ref, 0, local)
    blocks = [block_ref[i] for i in range(block_ref.shape[0])]
    blocks += [other_ref[i] for i in range(other_ref.shape[0])]
    everything = jnp.concatenate([jnp.concatenate(blocks, axis=1), places, jnp.zeros((4, n), jnp.float32)], axis=0)
    rows = everything.shape[0]
    parts = dot_nt(stacked_parts(everything), order_ref[...])
    whole = add_parts(parts)
    block_out[...] = whole[:columns]
    own_out[...] = whole[columns:]
    message_out[:columns, :] = whole[:columns].astype(jnp.bfloat16)
    lane = lax.broadcasted_iota(jnp.int32, (1, local), 1)
    flags = jnp.zeros((1, local), jnp.float32)
    for offset in range(owner_ref.shape[1]):
        flags = jnp.where((lane == offset) & (owner_ref[0, offset] >= 0), 1.0, flags)
    pieces = [parts[part * rows + columns : part * rows + columns + 3] for part in range(3)]
    pieces += [flags, jnp.zeros((EXTRA - 10, local), jnp.float32)]
    message_out[columns:, :] = jnp.concatenate(pieces, axis=0).astype(jnp.bfloat16)


def sort_region(first, tile_owner, near, far, block, other):
    local = near.shape[2]
    n = local * 2 * near.shape[0]
    columns = block.shape[1]
    smem = pl.BlockSpec(memory_space=pltpu.SMEM)
    return pl.pallas_call(
        sort_kernel,
        out_shape=(
            jax.ShapeDtypeStruct((columns + EXTRA, local), jnp.bfloat16),
            jax.ShapeDtypeStruct((8, local), jnp.float32),
            jax.ShapeDtypeStruct((columns, local), jnp.float32),
            jax.ShapeDtypeStruct((1, local), jnp.int32),
        ),
        in_specs=[smem, smem] + whole_vmem(4),
        out_specs=tuple(whole_vmem(4)),
        scratch_shapes=[pltpu.VMEM((local, n), jnp.bfloat16), pltpu.VMEM((n, 8), jnp.float32)],
        compiler_params=pltpu.CompilerParams(vmem_limit_bytes=VMEM),
        cost_estimate=pl.CostEstimate(
            flops=6 * n * local * (columns + 8), bytes_accessed=4 * n * local, transcendentals=0
        ),
        name="sort_region",
    )(first, tile_owner, near, far, block, other)


def unsort_kernel(first_ref, rank_ref, block_ref, block_out, order_ref):
    n, local = order_ref.shape
    for slot in range(n // local):
        fill_order(first_ref[slot], rank_ref[...], order_ref, slot * local, local)
    block_out[...] = add_parts(dot_nn(stacked_parts(block_ref[...]), order_ref[...]))


def unsort(first, rank, block):
    n = block.shape[1]
    local = rank.shape[1]
    return pl.pallas_call(
        unsort_kernel,
        out_shape=jax.ShapeDtypeStruct((block.shape[0], local), jnp.float32),
        in_specs=[pl.BlockSpec(memory_space=pltpu.SMEM)] + whole_vmem(2),
        out_specs=whole_vmem(1)[0],
        scratch_shapes=[pltpu.VMEM((n, local), jnp.bfloat16)],
        compiler_params=pltpu.CompilerParams(vmem_limit_bytes=VMEM),
        cost_estimate=pl.CostEstimate(
            flops=6 * n * local * block.shape[0], bytes_accessed=4 * n * local, transcendentals=0
        ),
        name="unsort",
    )(first, rank, block)


def plan_blocks(own_y, near, far, regions, here, flags, columns, capacity):
    reach = flags.shape[0]
    rows = own_y.shape[0] // ROWS
    stack = jnp.concatenate([near, far], axis=0)[:, :, columns:, :].astype(jnp.float32)
    chunks = stack.shape[3] // LANES
    y = (stack[:, :, 1] + stack[:, :, 4]) + stack[:, :, 7]
    y = y.reshape(-1, LANES)
    distance = regions - here
    ahead = jnp.arange(reach, dtype=jnp.int32)
    own_flag = jnp.sum(jnp.where(distance[..., None] == ahead, flags, 0.0), axis=-1)
    far_flag = jnp.sum(jnp.where(-distance[..., None] == ahead, stack[:, :, 9, :reach], 0.0), axis=-1)
    listed = jnp.broadcast_to(((own_flag + far_flag) > 0.5)[..., None], regions.shape + (chunks,))
    y_own = own_y.reshape(rows, ROWS)
    near_enough = (y[None, :, 0] <= y_own[:, -1:] + CUTOFF) & (y[None, :, -1] >= y_own[:, :1] - CUTOFF)
    active = near_enough & listed.reshape(1, -1)
    total = y.shape[0]
    index = jnp.arange(total, dtype=jnp.int32)
    counted = active.astype(jnp.int32)
    batches = (jnp.sum(counted, axis=1) + BATCH - 1) // BATCH
    row = jnp.arange(rows, dtype=jnp.int32)
    base = jnp.sum(jnp.where(row[:, None] < row[None, :], batches[:, None], 0), axis=0)
    place = base[:, None] * BATCH + jnp.sum(
        jnp.where(index[None, :, None] < index[None, None, :], counted[:, :, None], 0), axis=1
    )
    spot = jnp.arange(capacity * BATCH, dtype=jnp.int32)
    hit = active[:, :, None] & (place[:, :, None] == spot)
    ids = jnp.sum(jnp.where(hit, index[None, :, None] + 1, 0), axis=(0, 1)) - 1
    step = jnp.arange(capacity, dtype=jnp.int32)
    owner = jnp.sum((base + batches)[:, None] <= step[None, :], axis=0, dtype=jnp.int32)
    return ids, jnp.concatenate([jnp.minimum(owner, rows - 1), jnp.sum(batches, keepdims=True)])


def gaspari_cohn(squared):
    squared = jnp.maximum(squared, 1e-12)
    inverse = lax.rsqrt(squared)
    scaled = squared * inverse
    near = (((-0.25 * scaled + 0.5) * scaled + 0.625) * scaled - 5.0 / 3.0) * squared + 1.0
    left = jnp.maximum(2.0 - scaled, 0.0)
    left = left * left
    far = (left * left) * ((scaled + 2.0) * scaled - 0.5) * (inverse * (1.0 / 12.0))
    return jnp.where(scaled <= 1.0, near, far)


def tiles_kernel(build, wanted, ids_ref, plan_ref, own_ref, near_ref, far_ref, *refs):
    refs = list(refs)
    tiles_in = None if build else refs.pop(0)
    start_ref = None
    block_ref = scale_ref = out_ref = rounded_ref = gram_ref = None
    if wanted:
        start_ref, block_ref, scale_ref = refs[:3]
        refs = refs[3:]
    tiles_out = refs.pop(0) if build else None
    if wanted:
        out_ref, rounded_ref, gram_ref = refs[:3]
        refs = refs[3:]
        wide_ref, held_ref, all_ref, total_ref, sems, piece_sems = refs
    else:
        total_ref, wide_ref, held_ref, all_ref, sems, piece_sems = refs
    half, slots, height, local = near_ref.shape
    columns = total_ref.shape[1]
    capacity = held_ref.shape[0]
    chunks = local // LANES
    total = plan_ref[capacity]

    copies = [
        pltpu.make_async_copy(ref, all_ref.at[pl.ds(part * half, half)], piece_sems.at[part])
        for part, ref in enumerate((near_ref, far_ref))
    ]
    for copy in copies:
        copy.start()

    def copy_out(batch):
        return pltpu.make_async_copy(
            held_ref.at[batch], tiles_out.at[batch], sems.at[lax.rem(batch, RING)]
        )

    def copy_in(group):
        first = group * UNROLL
        return pltpu.make_async_copy(
            tiles_in.at[pl.ds(first, UNROLL)], held_ref.at[pl.ds(first, UNROLL)], sems.at[group]
        )

    groups = (total + UNROLL - 1) // UNROLL
    if not build:

        def start_copy(group, carry):
            copy_in(group).start()
            return carry

        lax.fori_loop(0, groups, start_copy, 0)
    if start_ref is None:
        total_ref[...] = jnp.zeros(total_ref.shape, jnp.float32)
    else:
        total_ref[...] = start_ref[...]
    if build:
        column = jnp.transpose(own_ref[...])
        for row in range(3):
            scale = 2.0 if row < 2 else 1.0
            wide_ref[row] = jnp.broadcast_to(scale * column[:, row : row + 1], (local, LANES))
    for copy in copies:
        copy.wait()

    def locate(batch, part):
        entry = ids_ref[batch * BATCH + part]
        chunk = jnp.maximum(entry, 0)
        place = chunk // chunks
        tile = place // slots
        lane = pl.multiple_of((chunk - place * chunks) * LANES, LANES)
        return entry, tile, place - tile * slots, lane

    def build_batch(batch):
        start = pl.multiple_of(plan_ref[batch] * ROWS, ROWS)
        for part in range(BATCH):
            entry, tile, place, lane = locate(batch, part)
            rows = all_ref[tile, place, columns:, pl.ds(lane, LANES)].astype(jnp.float32)
            far = (rows[0:3] + rows[3:6]) + rows[6:9]
            across_x = wide_ref[0, pl.ds(start, ROWS), :] - 2.0 * far[0:1, :]
            across_y = wide_ref[1, pl.ds(start, ROWS), :] - 2.0 * far[1:2, :]
            value = gaspari_cohn(across_x * across_x + across_y * across_y)
            spread = jnp.where(entry >= 0, far[2:3, :], 0.0)
            value = wide_ref[2, pl.ds(start, ROWS), :] * spread * value
            held_ref[batch, :, part * LANES : (part + 1) * LANES] = value.astype(jnp.bfloat16)

    def product(batch, valid=None):
        sides = []
        for part in range(BATCH):
            _, tile, place, lane = locate(batch, part)
            sides.append(all_ref[tile, place, :columns, pl.ds(lane, LANES)])
        side = jnp.concatenate(sides, axis=1)
        if valid is not None:
            side = jnp.where(valid, side, jnp.zeros_like(side))
        return dot_nt(held_ref[batch], side)

    def add_product(batch, value):
        start = pl.multiple_of(plan_ref[batch] * ROWS, ROWS)
        total_ref[pl.ds(start, ROWS), :] += value

    if build:

        @pl.when(total > 0)
        def _():
            build_batch(0)
            copy_out(0).start()

            def turn(batch, carry):
                @pl.when(batch >= RING)
                def _():
                    copy_out(batch - RING).wait()

                value = product(batch - 1)
                build_batch(batch)
                add_product(batch - 1, value)
                copy_out(batch).start()
                return carry

            lax.fori_loop(1, total, turn, 0)
            add_product(total - 1, product(total - 1))

            def finish(batch, carry):
                copy_out(batch).wait()
                return carry

            lax.fori_loop(jnp.maximum(total - RING, 0), total, finish, 0)

    else:

        def turn(group, carry):
            copy_in(group).wait()
            batches = [jnp.minimum(group * UNROLL + i, total - 1) for i in range(UNROLL)]
            values = [
                product(batch, group * UNROLL + i < total if i else None)
                for i, batch in enumerate(batches)
            ]
            for batch, value in zip(batches, values):
                add_product(batch, value)
            return carry

        lax.fori_loop(0, groups, turn, 0)

    if wanted:
        block = block_ref[...]
        result = jnp.transpose(total_ref[...]) + scale_ref[...] * block
        out_ref[...] = result
        rounded_ref[...] = result.astype(jnp.bfloat16)
        pairs = {"squares": (block, block), "mixed": (block, result), "images": (result, result)}
        for index, name in enumerate(wanted):
            gram_ref[index] = dot_nt(*pairs[name], HIGHEST)


def run_tiles(plan, own, near, far, tiles, capacity, columns, finish=None):
    build = tiles is None
    half, slots, height, local = near.shape
    smem = pl.BlockSpec(memory_space=pltpu.SMEM)
    anywhere = pl.BlockSpec(memory_space=pl.ANY)
    operands = [*plan, own, near, far]
    in_specs = [smem, smem] + whole_vmem(1) + [anywhere] * 2
    out_shape, out_specs = [], []
    if not build:
        operands.append(tiles)
        in_specs.append(anywhere)
    wanted = ()
    if finish is not None:
        total, block, scale, wanted = finish
        operands += [total, block, scale]
        in_specs += whole_vmem(3)
    if build:
        out_shape.append(jax.ShapeDtypeStruct((capacity, ROWS, BATCH * LANES), jnp.bfloat16))
        out_specs.append(anywhere)
    total_shape = (local, columns)
    scratch = []
    if wanted:
        out_shape += [
            jax.ShapeDtypeStruct((columns, local), jnp.float32),
            jax.ShapeDtypeStruct((columns, local), jnp.bfloat16),
            jax.ShapeDtypeStruct((len(wanted), columns, columns), jnp.float32),
        ]
        out_specs += whole_vmem(3)
    else:
        out_shape.append(jax.ShapeDtypeStruct(total_shape, jnp.float32))
        out_specs += whole_vmem(1)
    scratch += [
        pltpu.VMEM((3, local, LANES), jnp.float32),
        pltpu.VMEM((capacity, ROWS, BATCH * LANES), jnp.bfloat16),
        pltpu.VMEM((2 * half, slots, height, local), jnp.bfloat16),
    ]
    if wanted:
        scratch.append(pltpu.VMEM(total_shape, jnp.float32))
    scratch += [
        pltpu.SemaphoreType.DMA((RING if build else capacity // UNROLL,)),
        pltpu.SemaphoreType.DMA((2,)),
    ]
    work = 2 * local * local
    return pl.pallas_call(
        functools.partial(tiles_kernel, build, wanted),
        out_shape=tuple(out_shape),
        in_specs=in_specs,
        out_specs=tuple(out_specs),
        scratch_shapes=scratch,
        compiler_params=pltpu.CompilerParams(vmem_limit_bytes=VMEM),
        cost_estimate=pl.CostEstimate(
            flops=work * (120 if build else 60), bytes_accessed=8 * work, transcendentals=0
        ),
        name=("build" if build else "apply") + ("_last" if wanted else "_first"),
    )(*operands)


def reciprocal(value):
    inverse = lax.rsqrt(value)
    inverse = inverse * inverse
    return inverse * (2.0 - value * inverse)


def small_product(left, right):
    return [[sum(l * r[j] for l, r in zip(row, right)) for j in range(len(right[0]))] for row in left]


def small_difference(left, right):
    return [[l - r for l, r in zip(*rows)] for rows in zip(left, right)]


def small_inverse(matrix):
    (a, b), (c, d) = matrix
    scale = reciprocal(a * d - b * c)
    return [[d * scale, -b * scale], [-c * scale, a * scale]]


def solve_positive(matrix, target):
    n = matrix.shape[0]
    table = jnp.concatenate([0.5 * (matrix + jnp.transpose(matrix)), target], axis=1)
    bands = [table[k : k + 8, :] for k in range(0, n, 8)]
    row_index = lax.broadcasted_iota(jnp.int32, bands[0].shape, 0)
    for k in range(0, n, 4):
        own, row = k // 8, k % 8
        columns = [
            [jnp.broadcast_to(band[:, k + j : k + j + 1], band.shape) for band in bands] for j in range(4)
        ]
        pivot = [[columns[j][own][row + i : row + i + 1] for j in range(4)] for i in range(4)]
        upper, lower = pivot[:2], pivot[2:]
        top = small_inverse([r[:2] for r in upper])
        factor = small_product([r[:2] for r in lower], top)
        right = [r[2:] for r in upper]
        rest = small_inverse(small_difference([r[2:] for r in lower], small_product(factor, right)))
        rows = [[bands[own][row + i : row + i + 1]] for i in range(4)]
        last = small_product(rest, small_difference(rows[2:], small_product(factor, rows[:2])))
        first = small_product(top, small_difference(rows[:2], small_product(right, last)))
        new = [r[0] for r in first + last]
        bands = [
            band - ((columns[0][i] * new[0] + columns[1][i] * new[1]) + (columns[2][i] * new[2] + columns[3][i] * new[3]))
            for i, band in enumerate(bands)
        ]
        for i in range(4):
            bands[own] = jnp.where(row_index == row + i, new[i], bands[own])
    return jnp.concatenate([band[:, n:] for band in bands], axis=0)


def last_kernel(grams_ref, start_ref, images_ref, weights_ref, residual_ref):
    squares, mixed, images, cross = grams_ref[0], grams_ref[1], grams_ref[2], grams_ref[3]
    n = squares.shape[0]
    solved = solve_positive(mixed, jnp.concatenate([squares, images], axis=1))
    step, carried = solved[:, :n], solved[:, n:]
    product = dot_nn(images, solved, HIGHEST)
    second = solve_positive(cross - product[:, n:], jnp.transpose(mixed) - product[:, :n])
    first = jnp.transpose(step - dot_nn(carried, second, HIGHEST))
    second = jnp.transpose(second)
    start, image = start_ref[...], images_ref[:n, :]
    weights_ref[...] = dot_nn(first, start, HIGHEST) + dot_nn(second, image, HIGHEST)
    residual_ref[...] = start - dot_nn(first, image, HIGHEST) - dot_nn(second, images_ref[n:, :], HIGHEST)


def last_step(grams, start, images):
    return pl.pallas_call(
        last_kernel,
        out_shape=(jax.ShapeDtypeStruct(start.shape, jnp.float32),) * 2,
        in_specs=whole_vmem(3),
        out_specs=tuple(whole_vmem(2)),
        compiler_params=pltpu.CompilerParams(vmem_limit_bytes=VMEM),
        name="last_step",
    )(grams, start, images)


def shards(innovations, obs_geometry, obs_error, tile_owner):
    tiles_axis, regions = lax.axis_size("tile"), lax.axis_size("region")
    reach = tile_owner.shape[1]
    here, tile = lax.axis_index("region"), lax.axis_index("tile")
    columns, local = innovations.shape
    slot_tile = tile ^ jnp.arange(tiles_axis, dtype=jnp.int32)
    first = slot_tile * local
    slot_region = here ^ slot_offsets(regions)[slot_tile % 2]

    places = jnp.concatenate([obs_geometry, obs_error[None, :]], axis=0)
    message, own, start, rank = sort_region(
        first, tile_owner, *halves(places, "tile"), *halves(innovations, "tile")
    )
    scale = own[3:4]
    flags = jnp.where(tile_owner[0] >= 0, 1.0, 0.0).astype(jnp.float32)

    half_regions = regions // 2
    most = min(half_regions, 2 * reach - 1) * tiles_axis * (local // LANES)
    capacity = (local // ROWS) * -(-most // BATCH)
    capacity = -(-capacity // UNROLL) * UNROLL
    run = functools.partial(run_tiles, own=own, capacity=capacity, columns=columns)

    plans, tiles = [], []
    total = None
    for part, block in enumerate(exchange(message)):
        near, far = halves(block, "tile")
        inside = slot_region[:, part * half_regions : (part + 1) * half_regions]
        plans.append(plan_blocks(own[1], near, far, inside, here, flags, columns, capacity))
        finish = None if part == 0 else (total, start, scale, ("squares", "mixed", "images"))
        built, total, *others = run(plans[part], near=near, far=far, tiles=None, finish=finish)
        tiles.append(built)
    image = total
    image_rounded, grams = others

    for part, block in enumerate(exchange(image_rounded)):
        near, far = halves(block, "tile")
        finish = None if part == 0 else (total, image, scale, ("mixed",))
        total, *others = run(plans[part], near=near, far=far, tiles=tiles[part], finish=finish)
    second, cross = total, others[1]

    grams = jnp.concatenate([grams, cross], axis=0)
    grams = sum_over(sum_over(grams, "tile"), "region")
    near, far = halves(jnp.concatenate([image, second], axis=0), "tile")
    images = unsort(first, rank, jnp.concatenate([*near, *far], axis=1))
    return last_step(grams, innovations, images)


def solution(mesh):
    return jax.shard_map(
        shards,
        mesh=mesh,
        in_specs=(
            P(None, ("region", "tile")),
            P(None, ("region", "tile")),
            P(("region", "tile")),
            P("region", None),
        ),
        out_specs=(P(None, ("region", "tile")), P(None, ("region", "tile"))),
        check_vma=False,
    )
```

```python
import functools

import jax
import jax.numpy as jnp
from jax import lax
from jax.experimental import pallas as pl
from jax.experimental.pallas import tpu as pltpu
from jax.sharding import PartitionSpec as P

CUTOFF = 1.001
LANES = 128
ROWS = 64
BATCH = 4
UNROLL = 4
RING = 8
VMEM = 48 * 1024 * 1024
EXTRA = 16
HIGHEST = lax.Precision.HIGHEST


def whole_vmem(count):
    return [pl.BlockSpec(memory_space=pltpu.VMEM)] * count


def dot_nt(left, right, precision=None):
    return lax.dot_general(
        left, right, (((1,), (1,)), ((), ())), precision=precision, preferred_element_type=jnp.float32
    )


def dot_nn(left, right, precision=None):
    return lax.dot_general(
        left, right, (((1,), (0,)), ((), ())), precision=precision, preferred_element_type=jnp.float32
    )


def three_parts(value):
    high = value.astype(jnp.bfloat16)
    rest = value - high.astype(jnp.float32)
    middle = rest.astype(jnp.bfloat16)
    low = (rest - middle.astype(jnp.float32)).astype(jnp.bfloat16)
    return high, middle, low


def halves(block, axis):
    count = lax.axis_size(axis)
    block = block[None]
    bit = 1
    while 2 * bit < count:
        block = jnp.concatenate([block, swapped(block, axis, bit)], axis=0)
        bit *= 2
    return block, swapped(block, axis, bit)


def swapped(block, axis, bit):
    return lax.ppermute(block, axis, [(i, i ^ bit) for i in range(lax.axis_size(axis))])


def sum_tiles(block):
    bit = 1
    while bit < lax.axis_size("tile"):
        block = block + swapped(block, "tile", bit)
        bit *= 2
    return block


def swap_regions(block, even, odd):
    tiles = lax.axis_size("tile")
    route = [
        (region * tiles + tile, (region ^ (odd if tile % 2 else even)) * tiles + tile)
        for region in range(lax.axis_size("region"))
        for tile in range(tiles)
    ]
    return lax.ppermute(block, ("region", "tile"), route)


def sum_regions(block):
    bits, _ = region_orders(lax.axis_size("region"))
    middle = len(bits) // 2
    for even, odd in zip(bits, bits[middle:] + bits[:middle]):
        block = block + swap_regions(block, even, odd)
    return block


def region_orders(count):
    bits = []
    bit = count // 2
    while bit:
        bits.append(bit)
        bit //= 2
    return bits, bits[:1] + bits[-1:] + bits[1:-1] if len(bits) > 2 else bits[::-1]


def slot_offsets(count):
    table = []
    for bits in region_orders(count):
        offsets = [0]
        for bit in bits:
            offsets = offsets + [offset ^ bit for offset in offsets]
        table.append(offsets)
    return jnp.array(table, jnp.int32)


def exchange(block):
    regions = lax.axis_size("region")
    block = block[None]
    for even, odd in zip(*region_orders(regions)):
        other = swap_regions(block, even, odd)
        if 2 * block.shape[0] == regions:
            return block, other
        block = jnp.concatenate([block, other], axis=0)


def stacked_parts(value):
    return jnp.concatenate([part.astype(jnp.float32) for part in three_parts(value)], axis=0).astype(
        jnp.bfloat16
    )


def add_parts(value):
    rows = value.shape[0] // 3
    return (value[2 * rows :] + value[rows : 2 * rows]) + value[:rows]


def fill_order(first, rank, order_ref, row, count):
    step = 64

    def fill(block, carry):
        start = pl.multiple_of(block * step, step)
        place = first + start + lax.broadcasted_iota(jnp.int32, (step, rank.shape[1]), 0)
        order_ref[pl.ds(pl.multiple_of(row + start, step), step), :] = jnp.where(
            place == rank, 1.0, 0.0
        ).astype(jnp.bfloat16)
        return carry

    lax.fori_loop(0, count // step, fill, 0)


def sort_kernel(
    first_ref, owner_ref, near_ref, far_ref, block_ref, other_ref,
    message_out, own_out, block_out, rank_out, order_ref, column_ref,
):
    columns, local = block_out.shape
    stacks = [near_ref[i] for i in range(near_ref.shape[0])] + [far_ref[i] for i in range(far_ref.shape[0])]
    places = jnp.concatenate(stacks, axis=1)
    n = places.shape[1]
    step = 64
    index = jnp.concatenate(
        [
            (first_ref[i] + lax.broadcasted_iota(jnp.int32, (1, local), 1)).astype(jnp.float32)
            for i in range(n // local)
        ],
        axis=1,
    )
    y_row = places[1:2, :]
    column_ref[...] = jnp.transpose(
        jnp.concatenate([y_row, index, jnp.zeros((6, n), jnp.float32)], axis=0)
    )

    def count(block, total):
        start = pl.multiple_of(block * step, step)
        y_column = jnp.broadcast_to(column_ref[pl.ds(start, step), 0:1], (step, n))
        index_column = jnp.broadcast_to(column_ref[pl.ds(start, step), 1:2], (step, n))
        before = (y_column < y_row) | ((y_column == y_row) & (index_column < index))
        return total + jnp.sum(jnp.where(before, 1.0, 0.0).reshape(step // 8, 8, n), axis=0)

    total = lax.fori_loop(0, n // step, count, jnp.zeros((8, n), jnp.float32))
    rank = jnp.sum(total, axis=0, keepdims=True).astype(jnp.int32)
    rank_out[...] = rank[:, :local]
    fill_order(first_ref[0], rank, order_ref, 0, local)
    blocks = [block_ref[i] for i in range(block_ref.shape[0])]
    blocks += [other_ref[i] for i in range(other_ref.shape[0])]
    everything = jnp.concatenate([jnp.concatenate(blocks, axis=1), places, jnp.zeros((4, n), jnp.float32)], axis=0)
    rows = everything.shape[0]
    parts = dot_nt(stacked_parts(everything), order_ref[...])
    whole = add_parts(parts)
    block_out[...] = whole[:columns]
    own_out[...] = whole[columns:]
    message_out[:columns, :] = whole[:columns].astype(jnp.bfloat16)
    lane = lax.broadcasted_iota(jnp.int32, (1, local), 1)
    flags = jnp.zeros((1, local), jnp.float32)
    for offset in range(owner_ref.shape[1]):
        flags = jnp.where((lane == offset) & (owner_ref[0, offset] >= 0), 1.0, flags)
    pieces = [parts[part * rows + columns : part * rows + columns + 3] for part in range(3)]
    pieces += [flags, jnp.zeros((EXTRA - 10, local), jnp.float32)]
    message_out[columns:, :] = jnp.concatenate(pieces, axis=0).astype(jnp.bfloat16)


def sort_region(first, tile_owner, near, far, block, other):
    local = near.shape[2]
    n = local * 2 * near.shape[0]
    columns = block.shape[1]
    smem = pl.BlockSpec(memory_space=pltpu.SMEM)
    return pl.pallas_call(
        sort_kernel,
        out_shape=(
            jax.ShapeDtypeStruct((columns + EXTRA, local), jnp.bfloat16),
            jax.ShapeDtypeStruct((8, local), jnp.float32),
            jax.ShapeDtypeStruct((columns, local), jnp.float32),
            jax.ShapeDtypeStruct((1, local), jnp.int32),
        ),
        in_specs=[smem, smem] + whole_vmem(4),
        out_specs=tuple(whole_vmem(4)),
        scratch_shapes=[pltpu.VMEM((local, n), jnp.bfloat16), pltpu.VMEM((n, 8), jnp.float32)],
        compiler_params=pltpu.CompilerParams(vmem_limit_bytes=VMEM),
        cost_estimate=pl.CostEstimate(
            flops=6 * n * local * (columns + 8), bytes_accessed=4 * n * local, transcendentals=0
        ),
        name="sort_region",
    )(first, tile_owner, near, far, block, other)


def unsort_kernel(first_ref, rank_ref, block_ref, block_out, order_ref):
    n, local = order_ref.shape
    for slot in range(n // local):
        fill_order(first_ref[slot], rank_ref[...], order_ref, slot * local, local)
    block_out[...] = add_parts(dot_nn(stacked_parts(block_ref[...]), order_ref[...]))


def unsort(first, rank, block):
    n = block.shape[1]
    local = rank.shape[1]
    return pl.pallas_call(
        unsort_kernel,
        out_shape=jax.ShapeDtypeStruct((block.shape[0], local), jnp.float32),
        in_specs=[pl.BlockSpec(memory_space=pltpu.SMEM)] + whole_vmem(2),
        out_specs=whole_vmem(1)[0],
        scratch_shapes=[pltpu.VMEM((n, local), jnp.bfloat16)],
        compiler_params=pltpu.CompilerParams(vmem_limit_bytes=VMEM),
        cost_estimate=pl.CostEstimate(
            flops=6 * n * local * block.shape[0], bytes_accessed=4 * n * local, transcendentals=0
        ),
        name="unsort",
    )(first, rank, block)


def plan_blocks(own_y, near, far, regions, here, flags, columns, capacity):
    reach = flags.shape[0]
    rows = own_y.shape[0] // ROWS
    stack = jnp.concatenate([near, far], axis=0)[:, :, columns:, :].astype(jnp.float32)
    chunks = stack.shape[3] // LANES
    y = (stack[:, :, 1] + stack[:, :, 4]) + stack[:, :, 7]
    y = y.reshape(-1, LANES)
    distance = regions - here
    ahead = jnp.arange(reach, dtype=jnp.int32)
    own_flag = jnp.sum(jnp.where(distance[..., None] == ahead, flags, 0.0), axis=-1)
    far_flag = jnp.sum(jnp.where(-distance[..., None] == ahead, stack[:, :, 9, :reach], 0.0), axis=-1)
    listed = jnp.broadcast_to(((own_flag + far_flag) > 0.5)[..., None], regions.shape + (chunks,))
    y_own = own_y.reshape(rows, ROWS)
    near_enough = (y[None, :, 0] <= y_own[:, -1:] + CUTOFF) & (y[None, :, -1] >= y_own[:, :1] - CUTOFF)
    active = near_enough & listed.reshape(1, -1)
    total = y.shape[0]
    index = jnp.arange(total, dtype=jnp.int32)
    counted = active.astype(jnp.int32)
    batches = (jnp.sum(counted, axis=1) + BATCH - 1) // BATCH
    row = jnp.arange(rows, dtype=jnp.int32)
    base = jnp.sum(jnp.where(row[:, None] < row[None, :], batches[:, None], 0), axis=0)
    place = base[:, None] * BATCH + jnp.sum(
        jnp.where(index[None, :, None] < index[None, None, :], counted[:, :, None], 0), axis=1
    )
    spot = jnp.arange(capacity * BATCH, dtype=jnp.int32)
    hit = active[:, :, None] & (place[:, :, None] == spot)
    ids = jnp.sum(jnp.where(hit, index[None, :, None] + 1, 0), axis=(0, 1)) - 1
    step = jnp.arange(capacity, dtype=jnp.int32)
    owner = jnp.sum((base + batches)[:, None] <= step[None, :], axis=0, dtype=jnp.int32)
    return ids, jnp.concatenate([jnp.minimum(owner, rows - 1), jnp.sum(batches, keepdims=True)])


def gaspari_cohn(squared):
    squared = jnp.maximum(squared, 1e-12)
    inverse = lax.rsqrt(squared)
    scaled = squared * inverse
    near = (((-0.25 * scaled + 0.5) * scaled + 0.625) * scaled - 5.0 / 3.0) * squared + 1.0
    left = jnp.maximum(2.0 - scaled, 0.0)
    left = left * left
    far = (left * left) * ((scaled + 2.0) * scaled - 0.5) * (inverse * (1.0 / 12.0))
    return jnp.where(scaled <= 1.0, near, far)


def tiles_kernel(build, wanted, ids_ref, plan_ref, own_ref, near_ref, far_ref, *refs):
    refs = list(refs)
    tiles_in = None if build else refs.pop(0)
    start_ref = None
    block_ref = scale_ref = out_ref = rounded_ref = gram_ref = None
    if wanted:
        start_ref, block_ref, scale_ref = refs[:3]
        refs = refs[3:]
    tiles_out = refs.pop(0) if build else None
    if wanted:
        out_ref, rounded_ref, gram_ref = refs[:3]
        refs = refs[3:]
        wide_ref, held_ref, all_ref, total_ref, sems, piece_sems = refs
    else:
        total_ref, wide_ref, held_ref, all_ref, sems, piece_sems = refs
    half, slots, height, local = near_ref.shape
    columns = total_ref.shape[1]
    capacity = held_ref.shape[0]
    chunks = local // LANES
    total = plan_ref[capacity]

    copies = [
        pltpu.make_async_copy(ref, all_ref.at[pl.ds(part * half, half)], piece_sems.at[part])
        for part, ref in enumerate((near_ref, far_ref))
    ]
    for copy in copies:
        copy.start()

    def copy_out(batch):
        return pltpu.make_async_copy(
            held_ref.at[batch], tiles_out.at[batch], sems.at[lax.rem(batch, RING)]
        )

    def copy_in(group):
        first = group * UNROLL
        return pltpu.make_async_copy(
            tiles_in.at[pl.ds(first, UNROLL)], held_ref.at[pl.ds(first, UNROLL)], sems.at[group]
        )

    groups = (total + UNROLL - 1) // UNROLL
    if not build:

        def start_copy(group, carry):
            copy_in(group).start()
            return carry

        lax.fori_loop(0, groups, start_copy, 0)
    if start_ref is None:
        total_ref[...] = jnp.zeros(total_ref.shape, jnp.float32)
    else:
        total_ref[...] = start_ref[...]
    if build:
        column = jnp.transpose(own_ref[...])
        for row in range(3):
            scale = 2.0 if row < 2 else 1.0
            wide_ref[row] = jnp.broadcast_to(scale * column[:, row : row + 1], (local, LANES))
    for copy in copies:
        copy.wait()

    def locate(batch, part):
        entry = ids_ref[batch * BATCH + part]
        chunk = jnp.maximum(entry, 0)
        place = chunk // chunks
        tile = place // slots
        lane = pl.multiple_of((chunk - place * chunks) * LANES, LANES)
        return entry, tile, place - tile * slots, lane

    def build_batch(batch):
        start = pl.multiple_of(plan_ref[batch] * ROWS, ROWS)
        for part in range(BATCH):
            entry, tile, place, lane = locate(batch, part)
            rows = all_ref[tile, place, columns:, pl.ds(lane, LANES)].astype(jnp.float32)
            far = (rows[0:3] + rows[3:6]) + rows[6:9]
            across_x = wide_ref[0, pl.ds(start, ROWS), :] - 2.0 * far[0:1, :]
            across_y = wide_ref[1, pl.ds(start, ROWS), :] - 2.0 * far[1:2, :]
            value = gaspari_cohn(across_x * across_x + across_y * across_y)
            spread = jnp.where(entry >= 0, far[2:3, :], 0.0)
            value = wide_ref[2, pl.ds(start, ROWS), :] * spread * value
            held_ref[batch, :, part * LANES : (part + 1) * LANES] = value.astype(jnp.bfloat16)

    def product(batch, valid=None):
        sides = []
        for part in range(BATCH):
            _, tile, place, lane = locate(batch, part)
            sides.append(all_ref[tile, place, :columns, pl.ds(lane, LANES)])
        side = jnp.concatenate(sides, axis=1)
        if valid is not None:
            side = jnp.where(valid, side, jnp.zeros_like(side))
        return dot_nt(held_ref[batch], side)

    def add_product(batch, value):
        start = pl.multiple_of(plan_ref[batch] * ROWS, ROWS)
        total_ref[pl.ds(start, ROWS), :] += value

    if build:

        @pl.when(total > 0)
        def _():
            build_batch(0)
            copy_out(0).start()

            def turn(batch, carry):
                @pl.when(batch >= RING)
                def _():
                    copy_out(batch - RING).wait()

                value = product(batch - 1)
                build_batch(batch)
                add_product(batch - 1, value)
                copy_out(batch).start()
                return carry

            lax.fori_loop(1, total, turn, 0)
            add_product(total - 1, product(total - 1))

            def finish(batch, carry):
                copy_out(batch).wait()
                return carry

            lax.fori_loop(jnp.maximum(total - RING, 0), total, finish, 0)

    else:

        def turn(group, carry):
            copy_in(group).wait()
            batches = [jnp.minimum(group * UNROLL + i, total - 1) for i in range(UNROLL)]
            values = [
                product(batch, group * UNROLL + i < total if i else None)
                for i, batch in enumerate(batches)
            ]
            for batch, value in zip(batches, values):
                add_product(batch, value)
            return carry

        lax.fori_loop(0, groups, turn, 0)

    if wanted:
        block = block_ref[...]
        result = jnp.transpose(total_ref[...]) + scale_ref[...] * block
        out_ref[...] = result
        rounded_ref[...] = result.astype(jnp.bfloat16)
        pairs = {"squares": (block, block), "mixed": (block, result), "images": (result, result)}
        for index, name in enumerate(wanted):
            gram_ref[index] = dot_nt(*pairs[name], HIGHEST)


def run_tiles(plan, own, near, far, tiles, capacity, columns, finish=None):
    build = tiles is None
    half, slots, height, local = near.shape
    smem = pl.BlockSpec(memory_space=pltpu.SMEM)
    anywhere = pl.BlockSpec(memory_space=pl.ANY)
    operands = [*plan, own, near, far]
    in_specs = [smem, smem] + whole_vmem(1) + [anywhere] * 2
    out_shape, out_specs = [], []
    if not build:
        operands.append(tiles)
        in_specs.append(anywhere)
    wanted = ()
    if finish is not None:
        total, block, scale, wanted = finish
        operands += [total, block, scale]
        in_specs += whole_vmem(3)
    if build:
        out_shape.append(jax.ShapeDtypeStruct((capacity, ROWS, BATCH * LANES), jnp.bfloat16))
        out_specs.append(anywhere)
    total_shape = (local, columns)
    scratch = []
    if wanted:
        out_shape += [
            jax.ShapeDtypeStruct((columns, local), jnp.float32),
            jax.ShapeDtypeStruct((columns, local), jnp.bfloat16),
            jax.ShapeDtypeStruct((len(wanted), columns, columns), jnp.float32),
        ]
        out_specs += whole_vmem(3)
    else:
        out_shape.append(jax.ShapeDtypeStruct(total_shape, jnp.float32))
        out_specs += whole_vmem(1)
    scratch += [
        pltpu.VMEM((3, local, LANES), jnp.float32),
        pltpu.VMEM((capacity, ROWS, BATCH * LANES), jnp.bfloat16),
        pltpu.VMEM((2 * half, slots, height, local), jnp.bfloat16),
    ]
    if wanted:
        scratch.append(pltpu.VMEM(total_shape, jnp.float32))
    scratch += [
        pltpu.SemaphoreType.DMA((RING if build else capacity // UNROLL,)),
        pltpu.SemaphoreType.DMA((2,)),
    ]
    work = 2 * local * local
    return pl.pallas_call(
        functools.partial(tiles_kernel, build, wanted),
        out_shape=tuple(out_shape),
        in_specs=in_specs,
        out_specs=tuple(out_specs),
        scratch_shapes=scratch,
        compiler_params=pltpu.CompilerParams(vmem_limit_bytes=VMEM),
        cost_estimate=pl.CostEstimate(
            flops=work * (18000 if build else 9000), bytes_accessed=8 * work, transcendentals=0
        ),
        name=("build" if build else "apply") + ("_last" if wanted else "_first"),
    )(*operands)


def reciprocal(value):
    inverse = lax.rsqrt(value)
    inverse = inverse * inverse
    return inverse * (2.0 - value * inverse)


def small_product(left, right):
    return [[sum(l * r[j] for l, r in zip(row, right)) for j in range(len(right[0]))] for row in left]


def small_difference(left, right):
    return [[l - r for l, r in zip(*rows)] for rows in zip(left, right)]


def small_inverse(matrix):
    (a, b), (c, d) = matrix
    scale = reciprocal(a * d - b * c)
    return [[d * scale, -b * scale], [-c * scale, a * scale]]


def solve_positive(matrix, target):
    n = matrix.shape[0]
    table = jnp.concatenate([0.5 * (matrix + jnp.transpose(matrix)), target], axis=1)
    bands = [table[k : k + 8, :] for k in range(0, n, 8)]
    row_index = lax.broadcasted_iota(jnp.int32, bands[0].shape, 0)
    for k in range(0, n, 4):
        own, row = k // 8, k % 8
        columns = [
            [jnp.broadcast_to(band[:, k + j : k + j + 1], band.shape) for band in bands] for j in range(4)
        ]
        pivot = [[columns[j][own][row + i : row + i + 1] for j in range(4)] for i in range(4)]
        upper, lower = pivot[:2], pivot[2:]
        top = small_inverse([r[:2] for r in upper])
        factor = small_product([r[:2] for r in lower], top)
        right = [r[2:] for r in upper]
        rest = small_inverse(small_difference([r[2:] for r in lower], small_product(factor, right)))
        rows = [[bands[own][row + i : row + i + 1]] for i in range(4)]
        last = small_product(rest, small_difference(rows[2:], small_product(factor, rows[:2])))
        first = small_product(top, small_difference(rows[:2], small_product(right, last)))
        new = [r[0] for r in first + last]
        bands = [
            band - ((columns[0][i] * new[0] + columns[1][i] * new[1]) + (columns[2][i] * new[2] + columns[3][i] * new[3]))
            for i, band in enumerate(bands)
        ]
        for i in range(4):
            bands[own] = jnp.where(row_index == row + i, new[i], bands[own])
    return jnp.concatenate([band[:, n:] for band in bands], axis=0)


def last_kernel(grams_ref, start_ref, images_ref, weights_ref, residual_ref):
    squares, mixed, images, cross = grams_ref[0], grams_ref[1], grams_ref[2], grams_ref[3]
    n = squares.shape[0]
    solved = solve_positive(mixed, jnp.concatenate([squares, images], axis=1))
    step, carried = solved[:, :n], solved[:, n:]
    product = dot_nn(images, solved, HIGHEST)
    second = solve_positive(cross - product[:, n:], jnp.transpose(mixed) - product[:, :n])
    first = jnp.transpose(step - dot_nn(carried, second, HIGHEST))
    second = jnp.transpose(second)
    start, image = start_ref[...], images_ref[:n, :]
    weights_ref[...] = dot_nn(first, start, HIGHEST) + dot_nn(second, image, HIGHEST)
    residual_ref[...] = start - dot_nn(first, image, HIGHEST) - dot_nn(second, images_ref[n:, :], HIGHEST)


def last_step(grams, start, images):
    return pl.pallas_call(
        last_kernel,
        out_shape=(jax.ShapeDtypeStruct(start.shape, jnp.float32),) * 2,
        in_specs=whole_vmem(3),
        out_specs=tuple(whole_vmem(2)),
        compiler_params=pltpu.CompilerParams(vmem_limit_bytes=VMEM),
        name="last_step",
    )(grams, start, images)


def shards(innovations, obs_geometry, obs_error, tile_owner):
    tiles_axis, regions = lax.axis_size("tile"), lax.axis_size("region")
    reach = tile_owner.shape[1]
    here, tile = lax.axis_index("region"), lax.axis_index("tile")
    columns, local = innovations.shape
    slot_tile = tile ^ jnp.arange(tiles_axis, dtype=jnp.int32)
    first = slot_tile * local
    slot_region = here ^ slot_offsets(regions)[slot_tile % 2]

    places = jnp.concatenate([obs_geometry, obs_error[None, :]], axis=0)
    message, own, start, rank = sort_region(
        first, tile_owner, *halves(places, "tile"), *halves(innovations, "tile")
    )
    scale = own[3:4]
    flags = jnp.where(tile_owner[0] >= 0, 1.0, 0.0).astype(jnp.float32)

    half_regions = regions // 2
    most = min(half_regions, 2 * reach - 1) * tiles_axis * (local // LANES)
    capacity = (local // ROWS) * -(-most // BATCH)
    capacity = -(-capacity // UNROLL) * UNROLL
    run = functools.partial(run_tiles, own=own, capacity=capacity, columns=columns)

    plans, tiles = [], []
    total = None
    for part, block in enumerate(exchange(message)):
        if part:
            block, total = lax.optimization_barrier((block, total))
        near, far = halves(block, "tile")
        inside = slot_region[:, part * half_regions : (part + 1) * half_regions]
        plans.append(plan_blocks(own[1], near, far, inside, here, flags, columns, capacity))
        finish = None if part == 0 else (total, start, scale, ("squares", "mixed", "images"))
        built, total, *others = run(plans[part], near=near, far=far, tiles=None, finish=finish)
        tiles.append(built)
    image = total
    image_rounded, grams = others

    for part, block in enumerate(exchange(image_rounded)):
        if part:
            block, total = lax.optimization_barrier((block, total))
        near, far = halves(block, "tile")
        finish = None if part == 0 else (total, image, scale, ("mixed",))
        total, *others = run(plans[part], near=near, far=far, tiles=tiles[part], finish=finish)
    second, cross = total, others[1]

    grams = jnp.concatenate([grams, cross], axis=0)
    grams = sum_regions(sum_tiles(grams))
    near, far = halves(jnp.concatenate([image, second], axis=0), "tile")
    images = unsort(first, rank, jnp.concatenate([*near, *far], axis=1))
    return last_step(grams, innovations, images)


def solution(mesh):
    return jax.shard_map(
        shards,
        mesh=mesh,
        in_specs=(
            P(None, ("region", "tile")),
            P(None, ("region", "tile")),
            P(("region", "tile")),
            P("region", None),
        ),
        out_specs=(P(None, ("region", "tile")), P(None, ("region", "tile"))),
        check_vma=False,
    )
```

```python
import functools

import jax
import jax.numpy as jnp
from jax import lax
from jax.experimental import pallas as pl
from jax.experimental.pallas import tpu as pltpu
from jax.sharding import PartitionSpec as P

CUTOFF = 1.001
LANES = 128
ROWS = 64
BATCH = 4
UNROLL = 4
RING = 8
VMEM = 48 * 1024 * 1024
EXTRA = 16
HIGHEST = lax.Precision.HIGHEST


def whole_vmem(count):
    return [pl.BlockSpec(memory_space=pltpu.VMEM)] * count


def dot_nt(left, right, precision=None):
    return lax.dot_general(
        left, right, (((1,), (1,)), ((), ())), precision=precision, preferred_element_type=jnp.float32
    )


def dot_nn(left, right, precision=None):
    return lax.dot_general(
        left, right, (((1,), (0,)), ((), ())), precision=precision, preferred_element_type=jnp.float32
    )


def three_parts(value):
    high = value.astype(jnp.bfloat16)
    rest = value - high.astype(jnp.float32)
    middle = rest.astype(jnp.bfloat16)
    low = (rest - middle.astype(jnp.float32)).astype(jnp.bfloat16)
    return high, middle, low


def halves(block, axis):
    count = lax.axis_size(axis)
    block = block[None]
    bit = 1
    while 2 * bit < count:
        block = jnp.concatenate([block, swapped(block, axis, bit)], axis=0)
        bit *= 2
    return block, swapped(block, axis, bit)


def swapped(block, axis, bit):
    return lax.ppermute(block, axis, [(i, i ^ bit) for i in range(lax.axis_size(axis))])


def sum_tiles(block):
    bit = 1
    while bit < lax.axis_size("tile"):
        block = block + swapped(block, "tile", bit)
        bit *= 2
    return block


def swap_regions(block, even, odd):
    tiles = lax.axis_size("tile")
    route = [
        (region * tiles + tile, (region ^ (odd if tile % 2 else even)) * tiles + tile)
        for region in range(lax.axis_size("region"))
        for tile in range(tiles)
    ]
    return lax.ppermute(block, ("region", "tile"), route)


def sum_regions(block):
    bits, _ = region_orders(lax.axis_size("region"))
    middle = len(bits) // 2
    for even, odd in zip(bits, bits[middle:] + bits[:middle]):
        block = block + swap_regions(block, even, odd)
    return block


def region_orders(count):
    bits = []
    bit = count // 2
    while bit:
        bits.append(bit)
        bit //= 2
    return bits, bits[:1] + bits[-1:] + bits[1:-1] if len(bits) > 2 else bits[::-1]


def slot_offsets(count):
    table = []
    for bits in region_orders(count):
        offsets = [0]
        for bit in bits:
            offsets = offsets + [offset ^ bit for offset in offsets]
        table.append(offsets)
    return [jnp.array(offsets, jnp.int32) for offsets in table]


def exchange(block):
    regions = lax.axis_size("region")
    block = block[None]
    for even, odd in zip(*region_orders(regions)):
        other = swap_regions(block, even, odd)
        if 2 * block.shape[0] == regions:
            return block, other
        block = jnp.concatenate([block, other], axis=0)


def stacked_parts(value):
    return jnp.concatenate([part.astype(jnp.float32) for part in three_parts(value)], axis=0).astype(
        jnp.bfloat16
    )


def add_parts(value):
    rows = value.shape[0] // 3
    return (value[2 * rows :] + value[rows : 2 * rows]) + value[:rows]


def fill_order(first, rank, order_ref, row, count):
    step = 64

    def fill(block, carry):
        start = pl.multiple_of(block * step, step)
        place = first + start + lax.broadcasted_iota(jnp.int32, (step, rank.shape[1]), 0)
        order_ref[pl.ds(pl.multiple_of(row + start, step), step), :] = jnp.where(
            place == rank, 1.0, 0.0
        ).astype(jnp.bfloat16)
        return carry

    lax.fori_loop(0, count // step, fill, 0)


def sort_kernel(
    first_ref, owner_ref, near_ref, far_ref, block_ref, other_ref,
    message_out, own_out, block_out, rank_out, order_ref, column_ref,
):
    columns, local = block_out.shape
    stacks = [near_ref[i] for i in range(near_ref.shape[0])] + [far_ref[i] for i in range(far_ref.shape[0])]
    places = jnp.concatenate(stacks, axis=1)
    n = places.shape[1]
    step = 64
    index = jnp.concatenate(
        [
            (first_ref[i] + lax.broadcasted_iota(jnp.int32, (1, local), 1)).astype(jnp.float32)
            for i in range(n // local)
        ],
        axis=1,
    )
    y_row = places[1:2, :]
    column_ref[...] = jnp.transpose(
        jnp.concatenate([y_row, index, jnp.zeros((6, n), jnp.float32)], axis=0)
    )

    def count(block, total):
        start = pl.multiple_of(block * step, step)
        y_column = jnp.broadcast_to(column_ref[pl.ds(start, step), 0:1], (step, n))
        index_column = jnp.broadcast_to(column_ref[pl.ds(start, step), 1:2], (step, n))
        before = (y_column < y_row) | ((y_column == y_row) & (index_column < index))
        return total + jnp.sum(jnp.where(before, 1.0, 0.0).reshape(step // 8, 8, n), axis=0)

    total = lax.fori_loop(0, n // step, count, jnp.zeros((8, n), jnp.float32))
    rank = jnp.sum(total, axis=0, keepdims=True).astype(jnp.int32)
    rank_out[...] = rank[:, :local]
    fill_order(first_ref[0], rank, order_ref, 0, local)
    blocks = [block_ref[i] for i in range(block_ref.shape[0])]
    blocks += [other_ref[i] for i in range(other_ref.shape[0])]
    everything = jnp.concatenate([jnp.concatenate(blocks, axis=1), places, jnp.zeros((4, n), jnp.float32)], axis=0)
    rows = everything.shape[0]
    parts = dot_nt(stacked_parts(everything), order_ref[...])
    whole = add_parts(parts)
    block_out[...] = whole[:columns]
    own_out[...] = whole[columns:]
    message_out[:columns, :] = whole[:columns].astype(jnp.bfloat16)
    lane = lax.broadcasted_iota(jnp.int32, (1, local), 1)
    flags = jnp.zeros((1, local), jnp.float32)
    for offset in range(owner_ref.shape[1]):
        flags = jnp.where((lane == offset) & (owner_ref[0, offset] >= 0), 1.0, flags)
    pieces = [parts[part * rows + columns : part * rows + columns + 3] for part in range(3)]
    pieces += [flags, jnp.zeros((EXTRA - 10, local), jnp.float32)]
    message_out[columns:, :] = jnp.concatenate(pieces, axis=0).astype(jnp.bfloat16)


def sort_region(first, tile_owner, near, far, block, other):
    local = near.shape[2]
    n = local * 2 * near.shape[0]
    columns = block.shape[1]
    smem = pl.BlockSpec(memory_space=pltpu.SMEM)
    return pl.pallas_call(
        sort_kernel,
        out_shape=(
            jax.ShapeDtypeStruct((columns + EXTRA, local), jnp.bfloat16),
            jax.ShapeDtypeStruct((8, local), jnp.float32),
            jax.ShapeDtypeStruct((columns, local), jnp.float32),
            jax.ShapeDtypeStruct((1, local), jnp.int32),
        ),
        in_specs=[smem, smem] + whole_vmem(4),
        out_specs=tuple(whole_vmem(4)),
        scratch_shapes=[pltpu.VMEM((local, n), jnp.bfloat16), pltpu.VMEM((n, 8), jnp.float32)],
        compiler_params=pltpu.CompilerParams(vmem_limit_bytes=VMEM),
        cost_estimate=pl.CostEstimate(
            flops=6 * n * local * (columns + 8), bytes_accessed=4 * n * local, transcendentals=0
        ),
        name="sort_region",
    )(first, tile_owner, near, far, block, other)


def unsort_kernel(first_ref, rank_ref, block_ref, block_out, order_ref):
    n, local = order_ref.shape
    for slot in range(n // local):
        fill_order(first_ref[slot], rank_ref[...], order_ref, slot * local, local)
    block_out[...] = add_parts(dot_nn(stacked_parts(block_ref[...]), order_ref[...]))


def unsort(first, rank, block):
    n = block.shape[1]
    local = rank.shape[1]
    return pl.pallas_call(
        unsort_kernel,
        out_shape=jax.ShapeDtypeStruct((block.shape[0], local), jnp.float32),
        in_specs=[pl.BlockSpec(memory_space=pltpu.SMEM)] + whole_vmem(2),
        out_specs=whole_vmem(1)[0],
        scratch_shapes=[pltpu.VMEM((n, local), jnp.bfloat16)],
        compiler_params=pltpu.CompilerParams(vmem_limit_bytes=VMEM),
        cost_estimate=pl.CostEstimate(
            flops=6 * n * local * block.shape[0], bytes_accessed=4 * n * local, transcendentals=0
        ),
        name="unsort",
    )(first, rank, block)


def plan_blocks(own_y, near, far, regions, here, flags, columns, capacity):
    reach = flags.shape[0]
    rows = own_y.shape[0] // ROWS
    stack = jnp.concatenate([near, far], axis=0)[:, :, columns:, :].astype(jnp.float32)
    chunks = stack.shape[3] // LANES
    y = (stack[:, :, 1] + stack[:, :, 4]) + stack[:, :, 7]
    y = y.reshape(-1, LANES)
    distance = regions - here
    ahead = jnp.arange(reach, dtype=jnp.int32)
    own_flag = jnp.sum(jnp.where(distance[..., None] == ahead, flags, 0.0), axis=-1)
    far_flag = jnp.sum(jnp.where(-distance[..., None] == ahead, stack[:, :, 9, :reach], 0.0), axis=-1)
    listed = jnp.broadcast_to(((own_flag + far_flag) > 0.5)[..., None], regions.shape + (chunks,))
    y_own = own_y.reshape(rows, ROWS)
    near_enough = (y[None, :, 0] <= y_own[:, -1:] + CUTOFF) & (y[None, :, -1] >= y_own[:, :1] - CUTOFF)
    active = near_enough & listed.reshape(1, -1)
    total = y.shape[0]
    index = jnp.arange(total, dtype=jnp.int32)
    counted = active.astype(jnp.int32)
    batches = (jnp.sum(counted, axis=1) + BATCH - 1) // BATCH
    row = jnp.arange(rows, dtype=jnp.int32)
    base = jnp.sum(jnp.where(row[:, None] < row[None, :], batches[:, None], 0), axis=0)
    place = base[:, None] * BATCH + jnp.sum(
        jnp.where(index[None, :, None] < index[None, None, :], counted[:, :, None], 0), axis=1
    )
    spot = jnp.arange(capacity * BATCH, dtype=jnp.int32)
    hit = active[:, :, None] & (place[:, :, None] == spot)
    ids = jnp.sum(jnp.where(hit, index[None, :, None] + 1, 0), axis=(0, 1)) - 1
    step = jnp.arange(capacity, dtype=jnp.int32)
    owner = jnp.sum((base + batches)[:, None] <= step[None, :], axis=0, dtype=jnp.int32)
    return ids, jnp.concatenate([jnp.minimum(owner, rows - 1), jnp.sum(batches, keepdims=True)])


def gaspari_cohn(squared):
    squared = jnp.maximum(squared, 1e-12)
    inverse = lax.rsqrt(squared)
    scaled = squared * inverse
    near = (((-0.25 * scaled + 0.5) * scaled + 0.625) * scaled - 5.0 / 3.0) * squared + 1.0
    left = jnp.maximum(2.0 - scaled, 0.0)
    left = left * left
    far = (left * left) * ((scaled + 2.0) * scaled - 0.5) * (inverse * (1.0 / 12.0))
    return jnp.where(scaled <= 1.0, near, far)


def tiles_kernel(build, wanted, ids_ref, plan_ref, own_ref, near_ref, other_ref, *refs):
    refs = list(refs)
    tiles_in = None if build else refs.pop(0)
    start_ref = None
    block_ref = scale_ref = out_ref = rounded_ref = gram_ref = None
    if wanted:
        start_ref, block_ref, scale_ref = refs[:3]
        refs = refs[3:]
    tiles_out = refs.pop(0) if build else None
    if wanted:
        out_ref, rounded_ref, gram_ref = refs[:3]
        refs = refs[3:]
        wide_ref, far_ref, held_ref, all_ref, total_ref, sems, piece_sems = refs
    else:
        total_ref, wide_ref, far_ref, held_ref, all_ref, sems, piece_sems = refs
    half, height, local = near_ref.shape
    columns = total_ref.shape[1]
    capacity = held_ref.shape[0]
    chunk_bits = (local // LANES).bit_length() - 1
    total = plan_ref[capacity]

    copies = [
        pltpu.make_async_copy(ref, all_ref.at[pl.ds(part * half, half)], piece_sems.at[part])
        for part, ref in enumerate((near_ref, other_ref))
    ]
    for copy in copies:
        copy.start()

    def copy_out(batch):
        return pltpu.make_async_copy(
            held_ref.at[batch], tiles_out.at[batch], sems.at[lax.rem(batch, RING)]
        )

    def copy_in(group):
        first = group * UNROLL
        return pltpu.make_async_copy(
            tiles_in.at[pl.ds(first, UNROLL)], held_ref.at[pl.ds(first, UNROLL)], sems.at[group]
        )

    groups = (total + UNROLL - 1) // UNROLL
    if not build:

        def start_copy(group, carry):
            copy_in(group).start()
            return carry

        lax.fori_loop(0, groups, start_copy, 0)
    if start_ref is None:
        total_ref[...] = jnp.zeros(total_ref.shape, jnp.float32)
    else:
        total_ref[...] = start_ref[...]
    if build:
        column = jnp.transpose(own_ref[...])
        for row in range(3):
            scale = 2.0 if row < 2 else 1.0
            wide_ref[row] = jnp.broadcast_to(scale * column[:, row : row + 1], (local, LANES))
    for copy in copies:
        copy.wait()
    if build:
        for place in range(2 * half):
            rows = all_ref[place, columns:, :].astype(jnp.float32)
            rows = (rows[0:3] + rows[3:6]) + rows[6:9]
            far_ref[place, 0:3, :] = jnp.concatenate([2.0 * rows[0:2], rows[2:3]], axis=0)

    def locate(batch, part):
        entry = ids_ref[batch * BATCH + part]
        chunk = jnp.maximum(entry, 0)
        lane = pl.multiple_of((chunk & ((1 << chunk_bits) - 1)) * LANES, LANES)
        return entry, lax.shift_right_logical(chunk, chunk_bits), lane

    def build_batch(batch):
        start = pl.multiple_of(plan_ref[batch] * ROWS, ROWS)
        for part in range(BATCH):
            entry, place, lane = locate(batch, part)
            far = far_ref[place, :, pl.ds(lane, LANES)]
            across_x = wide_ref[0, pl.ds(start, ROWS), :] - far[0:1, :]
            across_y = wide_ref[1, pl.ds(start, ROWS), :] - far[1:2, :]
            value = gaspari_cohn(across_x * across_x + across_y * across_y)
            spread = jnp.where(entry >= 0, far[2:3, :], 0.0)
            value = wide_ref[2, pl.ds(start, ROWS), :] * spread * value
            held_ref[batch, :, part * LANES : (part + 1) * LANES] = value.astype(jnp.bfloat16)

    def product(batch, valid=None):
        sides = []
        for part in range(BATCH):
            _, place, lane = locate(batch, part)
            sides.append(all_ref[place, :columns, pl.ds(lane, LANES)])
        side = jnp.concatenate(sides, axis=1)
        if valid is not None:
            side = jnp.where(valid, side, jnp.zeros_like(side))
        return dot_nt(held_ref[batch], side)

    def add_product(batch, value):
        start = pl.multiple_of(plan_ref[batch] * ROWS, ROWS)
        total_ref[pl.ds(start, ROWS), :] += value

    if build:

        @pl.when(total > 0)
        def _():
            build_batch(0)
            copy_out(0).start()

            def turn(batch, carry):
                @pl.when(batch >= RING)
                def _():
                    copy_out(batch - RING).wait()

                value = product(batch - 1)
                build_batch(batch)
                add_product(batch - 1, value)
                copy_out(batch).start()
                return carry

            lax.fori_loop(1, total, turn, 0)
            add_product(total - 1, product(total - 1))

            def finish(batch, carry):
                copy_out(batch).wait()
                return carry

            lax.fori_loop(jnp.maximum(total - RING, 0), total, finish, 0)

    else:

        def turn(group, carry):
            copy_in(group).wait()
            batches = [jnp.minimum(group * UNROLL + i, total - 1) for i in range(UNROLL)]
            values = [
                product(batch, group * UNROLL + i < total if i else None)
                for i, batch in enumerate(batches)
            ]
            for batch, value in zip(batches, values):
                add_product(batch, value)
            return carry

        lax.fori_loop(0, groups, turn, 0)

    if wanted:
        block = block_ref[...]
        result = jnp.transpose(total_ref[...]) + scale_ref[...] * block
        out_ref[...] = result
        rounded_ref[...] = result.astype(jnp.bfloat16)
        gram_ref[...] = dot_nt(block, jnp.concatenate([block, result], axis=0), HIGHEST)


def run_tiles(plan, own, near, far, tiles, capacity, columns, finish=None):
    build = tiles is None
    near, far = [piece.reshape((-1,) + piece.shape[2:]) for piece in (near, far)]
    half, height, local = near.shape
    smem = pl.BlockSpec(memory_space=pltpu.SMEM)
    anywhere = pl.BlockSpec(memory_space=pl.ANY)
    operands = [*plan, own, near, far]
    in_specs = [smem, smem] + whole_vmem(1) + [anywhere] * 2
    out_shape, out_specs = [], []
    if not build:
        operands.append(tiles)
        in_specs.append(anywhere)
    wanted = False
    if finish is not None:
        wanted = True
        total, block, scale = finish
        operands += [total, block, scale]
        in_specs += whole_vmem(3)
    if build:
        out_shape.append(jax.ShapeDtypeStruct((capacity, ROWS, BATCH * LANES), jnp.bfloat16))
        out_specs.append(anywhere)
    total_shape = (local, columns)
    scratch = []
    if wanted:
        out_shape += [
            jax.ShapeDtypeStruct((columns, local), jnp.float32),
            jax.ShapeDtypeStruct((columns, local), jnp.bfloat16),
            jax.ShapeDtypeStruct((columns, 2 * columns), jnp.float32),
        ]
        out_specs += whole_vmem(3)
    else:
        out_shape.append(jax.ShapeDtypeStruct(total_shape, jnp.float32))
        out_specs += whole_vmem(1)
    scratch += [
        pltpu.VMEM((3, local, LANES), jnp.float32),
        pltpu.VMEM((2 * half, 8, local), jnp.float32),
        pltpu.VMEM((capacity, ROWS, BATCH * LANES), jnp.bfloat16),
        pltpu.VMEM((2 * half, height, local), jnp.bfloat16),
    ]
    if wanted:
        scratch.append(pltpu.VMEM(total_shape, jnp.float32))
    scratch += [
        pltpu.SemaphoreType.DMA((RING if build else capacity // UNROLL,)),
        pltpu.SemaphoreType.DMA((2,)),
    ]
    work = 2 * local * local
    return pl.pallas_call(
        functools.partial(tiles_kernel, build, wanted),
        out_shape=tuple(out_shape),
        in_specs=in_specs,
        out_specs=tuple(out_specs),
        scratch_shapes=scratch,
        compiler_params=pltpu.CompilerParams(vmem_limit_bytes=VMEM),
        cost_estimate=pl.CostEstimate(
            flops=work * (18000 if build else 9000), bytes_accessed=8 * work, transcendentals=0
        ),
        name=("build" if build else "apply") + ("_last" if wanted else "_first"),
    )(*operands)


def reciprocal(value):
    inverse = lax.rsqrt(value)
    inverse = inverse * inverse
    return inverse * (2.0 - value * inverse)


def small_product(left, right):
    return [[sum(l * r[j] for l, r in zip(row, right)) for j in range(len(right[0]))] for row in left]


def small_difference(left, right):
    return [[l - r for l, r in zip(*rows)] for rows in zip(left, right)]


def small_inverse(matrix):
    (a, b), (c, d) = matrix
    scale = reciprocal(a * d - b * c)
    return [[d * scale, -b * scale], [-c * scale, a * scale]]


def solve_positive(matrix, target):
    n = matrix.shape[0]
    table = jnp.concatenate([0.5 * (matrix + jnp.transpose(matrix)), target], axis=1)
    bands = [table[k : k + 8, :] for k in range(0, n, 8)]
    row_index = lax.broadcasted_iota(jnp.int32, bands[0].shape, 0)
    for k in range(0, n, 4):
        own, row = k // 8, k % 8
        columns = [
            [jnp.broadcast_to(band[:, k + j : k + j + 1], band.shape) for band in bands] for j in range(4)
        ]
        pivot = [[columns[j][own][row + i : row + i + 1] for j in range(4)] for i in range(4)]
        upper, lower = pivot[:2], pivot[2:]
        top = small_inverse([r[:2] for r in upper])
        factor = small_product([r[:2] for r in lower], top)
        right = [r[2:] for r in upper]
        rest = small_inverse(small_difference([r[2:] for r in lower], small_product(factor, right)))
        rows = [[bands[own][row + i : row + i + 1]] for i in range(4)]
        last = small_product(rest, small_difference(rows[2:], small_product(factor, rows[:2])))
        first = small_product(top, small_difference(rows[:2], small_product(right, last)))
        new = [r[0] for r in first + last]
        bands = [
            band - ((columns[0][i] * new[0] + columns[1][i] * new[1]) + (columns[2][i] * new[2] + columns[3][i] * new[3]))
            for i, band in enumerate(bands)
        ]
        for i in range(4):
            bands[own] = jnp.where(row_index == row + i, new[i], bands[own])
    return jnp.concatenate([band[:, n:] for band in bands], axis=0)


def last_kernel(grams_ref, start_ref, images_ref, weights_ref, residual_ref):
    n = grams_ref.shape[1]
    squares, mixed = grams_ref[0, :, :n], grams_ref[0, :, n:]
    images, cross = grams_ref[1, :, :n], grams_ref[1, :, n:]
    solved = solve_positive(mixed, jnp.concatenate([squares, images], axis=1))
    step, carried = solved[:, :n], solved[:, n:]
    product = dot_nn(images, solved, HIGHEST)
    second = solve_positive(cross - product[:, n:], jnp.transpose(mixed) - product[:, :n])
    first = jnp.transpose(step - dot_nn(carried, second, HIGHEST))
    second = jnp.transpose(second)
    start, image = start_ref[...], images_ref[:n, :]
    weights_ref[...] = dot_nn(first, start, HIGHEST) + dot_nn(second, image, HIGHEST)
    residual_ref[...] = start - dot_nn(first, image, HIGHEST) - dot_nn(second, images_ref[n:, :], HIGHEST)


def last_step(grams, start, images):
    return pl.pallas_call(
        last_kernel,
        out_shape=(jax.ShapeDtypeStruct(start.shape, jnp.float32),) * 2,
        in_specs=whole_vmem(3),
        out_specs=tuple(whole_vmem(2)),
        compiler_params=pltpu.CompilerParams(vmem_limit_bytes=VMEM),
        name="last_step",
    )(grams, start, images)


def shards(innovations, obs_geometry, obs_error, tile_owner):
    tiles_axis, regions = lax.axis_size("tile"), lax.axis_size("region")
    reach = tile_owner.shape[1]
    here, tile = lax.axis_index("region"), lax.axis_index("tile")
    columns, local = innovations.shape
    slot_tile = tile ^ jnp.arange(tiles_axis, dtype=jnp.int32)
    first = slot_tile * local
    even, odd = slot_offsets(regions)
    slot_region = here ^ jnp.where((slot_tile % 2 == 0)[:, None], even, odd)

    places = jnp.concatenate([obs_geometry, obs_error[None, :]], axis=0)
    message, own, start, rank = sort_region(
        first, tile_owner, *halves(places, "tile"), *halves(innovations, "tile")
    )
    scale = own[3:4]
    flags = jnp.where(tile_owner[0] >= 0, 1.0, 0.0).astype(jnp.float32)

    half_regions = regions // 2
    most = min(half_regions, 2 * reach - 1) * tiles_axis * (local // LANES)
    capacity = (local // ROWS) * -(-most // BATCH)
    capacity = -(-capacity // UNROLL) * UNROLL
    run = functools.partial(run_tiles, own=own, capacity=capacity, columns=columns)

    plans, tiles = [], []
    total = None
    for part, block in enumerate(exchange(message)):
        if part:
            block, total = lax.optimization_barrier((block, total))
        near, far = halves(block, "tile")
        inside = slot_region[:, part * half_regions : (part + 1) * half_regions]
        plans.append(plan_blocks(own[1], near, far, inside, here, flags, columns, capacity))
        finish = None if part == 0 else (total, start, scale)
        built, total, *others = run(plans[part], near=near, far=far, tiles=None, finish=finish)
        tiles.append(built)
    image = total
    image_rounded, grams = others

    for part, block in enumerate(exchange(image_rounded)):
        if part:
            block, total = lax.optimization_barrier((block, total))
        near, far = halves(block, "tile")
        finish = None if part == 0 else (total, image, scale)
        total, *others = run(plans[part], near=near, far=far, tiles=tiles[part], finish=finish)
    second, cross = total, others[1]

    grams = jnp.stack([grams, cross])
    grams = sum_regions(sum_tiles(grams))
    near, far = halves(jnp.concatenate([image, second], axis=0), "tile")
    images = unsort(first, rank, jnp.concatenate([*near, *far], axis=1))
    return last_step(grams, innovations, images)


def solution(mesh):
    return jax.shard_map(
        shards,
        mesh=mesh,
        in_specs=(
            P(None, ("region", "tile")),
            P(None, ("region", "tile")),
            P(("region", "tile")),
            P("region", None),
        ),
        out_specs=(P(None, ("region", "tile")), P(None, ("region", "tile"))),
        check_vma=False,
    )
```

```python
import functools

import jax
import jax.numpy as jnp
from jax import lax
from jax.experimental import pallas as pl
from jax.experimental.pallas import tpu as pltpu
from jax.sharding import PartitionSpec as P

CUTOFF = 1.001
LANES = 128
ROWS = 64
PAIR = 2
BATCH = 2 * PAIR
RING = 8
UNROLL = 4
VMEM = 16 * 1024 * 1024
EXTRA = 16
HIGHEST = lax.Precision.HIGHEST


def whole_vmem(count):
    return [pl.BlockSpec(memory_space=pltpu.VMEM)] * count


def in_hbm(value):
    return pltpu.with_memory_space_constraint(value, pltpu.HBM)


def dot_nt(left, right, precision=None):
    return lax.dot_general(
        left, right, (((1,), (1,)), ((), ())), precision=precision, preferred_element_type=jnp.float32
    )


def dot_nn(left, right, precision=None):
    return lax.dot_general(
        left, right, (((1,), (0,)), ((), ())), precision=precision, preferred_element_type=jnp.float32
    )


def three_parts(value):
    high = value.astype(jnp.bfloat16)
    rest = value - high.astype(jnp.float32)
    middle = rest.astype(jnp.bfloat16)
    low = (rest - middle.astype(jnp.float32)).astype(jnp.bfloat16)
    return high, middle, low


def halves(block, axis):
    count = lax.axis_size(axis)
    block = block[None]
    bit = 1
    while 2 * bit < count:
        block = jnp.concatenate([block, swapped(block, axis, bit)], axis=0)
        bit *= 2
    return block, swapped(block, axis, bit)


def swapped(block, axis, bit):
    return lax.ppermute(block, axis, [(i, i ^ bit) for i in range(lax.axis_size(axis))])


def sum_tiles(block):
    bit = 1
    while bit < lax.axis_size("tile"):
        block = block + swapped(block, "tile", bit)
        bit *= 2
    return block


def swap_regions(block, even, odd):
    tiles = lax.axis_size("tile")
    route = [
        (region * tiles + tile, (region ^ (odd if tile % 2 else even)) * tiles + tile)
        for region in range(lax.axis_size("region"))
        for tile in range(tiles)
    ]
    return lax.ppermute(block, ("region", "tile"), route)


def sum_regions(block):
    bits, _ = region_orders(lax.axis_size("region"))
    middle = len(bits) // 2
    for even, odd in zip(bits, bits[middle:] + bits[:middle]):
        block = block + swap_regions(block, even, odd)
    return block


def region_orders(count):
    bits = []
    bit = count // 2
    while bit:
        bits.append(bit)
        bit //= 2
    return bits, bits[:1] + bits[-1:] + bits[1:-1] if len(bits) > 2 else bits[::-1]


def slot_offsets(count):
    table = []
    for bits in region_orders(count):
        offsets = [0]
        for bit in bits:
            offsets = offsets + [offset ^ bit for offset in offsets]
        table.append(offsets)
    return [jnp.array(offsets, jnp.int32) for offsets in table]


def exchange(block):
    regions = lax.axis_size("region")
    block = block[None]
    for even, odd in zip(*region_orders(regions)):
        other = swap_regions(block, even, odd)
        if 2 * block.shape[0] == regions:
            return block, other
        block = jnp.concatenate([block, other], axis=0)


def stacked_parts(value):
    return jnp.concatenate([part.astype(jnp.float32) for part in three_parts(value)], axis=0).astype(
        jnp.bfloat16
    )


def add_parts(value):
    rows = value.shape[0] // 3
    return (value[2 * rows :] + value[rows : 2 * rows]) + value[:rows]


def fill_order(first, rank, order_ref, row, count):
    step = 64

    def fill(block, carry):
        start = pl.multiple_of(block * step, step)
        place = first + start + lax.broadcasted_iota(jnp.int32, (step, rank.shape[1]), 0)
        order_ref[pl.ds(pl.multiple_of(row + start, step), step), :] = jnp.where(
            place == rank, 1.0, 0.0
        ).astype(jnp.bfloat16)
        return carry

    lax.fori_loop(0, count // step, fill, 0)


def sort_kernel(
    first_ref, owner_ref, near_ref, far_ref, near_error_ref, far_error_ref, block_ref, other_ref,
    message_out, own_out, block_out, rank_out,
    order_ref, column_ref, owned_ref, places_ref, errors_ref, blocks_ref, sems,
):
    columns, local = block_out.shape
    half = block_ref.shape[0]
    pairs = [(owner_ref, owned_ref)]
    for sources, target in (
        ((near_ref, far_ref), places_ref),
        ((near_error_ref, far_error_ref), errors_ref),
        ((block_ref, other_ref), blocks_ref),
    ):
        pairs += [(ref, target.at[pl.ds(part * half, half)]) for part, ref in enumerate(sources)]
    copies = [
        pltpu.make_async_copy(source, target, sems.at[index])
        for index, (source, target) in enumerate(pairs)
    ]
    for copy in copies:
        copy.start()
    for copy in copies[:5]:
        copy.wait()
    places = jnp.concatenate(
        [jnp.concatenate([places_ref[i], errors_ref[i]], axis=0) for i in range(2 * half)], axis=1
    )
    n = places.shape[1]
    step = 64
    index = jnp.concatenate(
        [
            (first_ref[i] + lax.broadcasted_iota(jnp.int32, (1, local), 1)).astype(jnp.float32)
            for i in range(n // local)
        ],
        axis=1,
    )
    y_row = places[1:2, :]
    column_ref[...] = jnp.transpose(
        jnp.concatenate([y_row, index, jnp.zeros((6, n), jnp.float32)], axis=0)
    )

    def count(block, total):
        start = pl.multiple_of(block * step, step)
        y_column = jnp.broadcast_to(column_ref[pl.ds(start, step), 0:1], (step, n))
        index_column = jnp.broadcast_to(column_ref[pl.ds(start, step), 1:2], (step, n))
        before = (y_column < y_row) | ((y_column == y_row) & (index_column < index))
        return total + jnp.sum(jnp.where(before, 1.0, 0.0).reshape(step // 8, 8, n), axis=0)

    total = lax.fori_loop(0, n // step, count, jnp.zeros((8, n), jnp.float32))
    rank = jnp.sum(total, axis=0, keepdims=True).astype(jnp.int32)
    rank_out[...] = rank[:, :local]
    fill_order(first_ref[0], rank, order_ref, 0, local)
    for copy in copies[5:]:
        copy.wait()
    blocks = [blocks_ref[i] for i in range(2 * half)]
    everything = jnp.concatenate([jnp.concatenate(blocks, axis=1), places, jnp.zeros((4, n), jnp.float32)], axis=0)
    rows = everything.shape[0]
    parts = dot_nt(stacked_parts(everything), order_ref[...])
    whole = add_parts(parts)
    block_out[...] = whole[:columns]
    own_out[...] = whole[columns:]
    message_out[:columns, :] = whole[:columns].astype(jnp.bfloat16)
    lane = lax.broadcasted_iota(jnp.int32, (1, local), 1)
    flags = jnp.zeros((1, local), jnp.float32)
    for offset in range(owner_ref.shape[1]):
        flags = jnp.where((lane == offset) & (owned_ref[0, offset] >= 0), 1.0, flags)
    pieces = [parts[part * rows + columns : part * rows + columns + 3] for part in range(3)]
    pieces += [flags, jnp.zeros((EXTRA - 10, local), jnp.float32)]
    message_out[columns:, :] = jnp.concatenate(pieces, axis=0).astype(jnp.bfloat16)


def sort_region(first, tile_owner, near, far, near_error, far_error, block, other):
    local = near.shape[2]
    n = local * 2 * near.shape[0]
    columns = block.shape[1]
    smem = pl.BlockSpec(memory_space=pltpu.SMEM)
    return pl.pallas_call(
        sort_kernel,
        out_shape=(
            jax.ShapeDtypeStruct((columns + EXTRA, local), jnp.bfloat16),
            jax.ShapeDtypeStruct((8, local), jnp.float32),
            jax.ShapeDtypeStruct((columns, local), jnp.float32),
            jax.ShapeDtypeStruct((1, local), jnp.int32),
        ),
        in_specs=[smem] + [pl.BlockSpec(memory_space=pl.ANY)] * 7,
        out_specs=tuple(whole_vmem(4)),
        scratch_shapes=[
            pltpu.VMEM((local, n), jnp.bfloat16),
            pltpu.VMEM((n, 8), jnp.float32),
            pltpu.SMEM(tile_owner.shape, jnp.int32),
            pltpu.VMEM((n // local, 3, local), jnp.float32),
            pltpu.VMEM((n // local, 1, local), jnp.float32),
            pltpu.VMEM((n // local, columns, local), jnp.float32),
            pltpu.SemaphoreType.DMA((7,)),
        ],
        compiler_params=pltpu.CompilerParams(vmem_limit_bytes=VMEM),
        cost_estimate=pl.CostEstimate(
            flops=6 * n * local * (columns + 8), bytes_accessed=4 * n * local, transcendentals=0
        ),
        name="sort_region",
    )(first, in_hbm(tile_owner), in_hbm(near), far, in_hbm(near_error), far_error, in_hbm(block), other)


def unsort_kernel(first_ref, rank_ref, block_ref, block_out, order_ref):
    n, local = order_ref.shape
    for slot in range(n // local):
        fill_order(first_ref[slot], rank_ref[...], order_ref, slot * local, local)
    block_out[...] = add_parts(dot_nn(stacked_parts(block_ref[...]), order_ref[...]))


def unsort(first, rank, block):
    n = block.shape[1]
    local = rank.shape[1]
    return pl.pallas_call(
        unsort_kernel,
        out_shape=jax.ShapeDtypeStruct((block.shape[0], local), jnp.float32),
        in_specs=[pl.BlockSpec(memory_space=pltpu.SMEM)] + whole_vmem(2),
        out_specs=whole_vmem(1)[0],
        scratch_shapes=[pltpu.VMEM((n, local), jnp.bfloat16)],
        compiler_params=pltpu.CompilerParams(vmem_limit_bytes=VMEM),
        cost_estimate=pl.CostEstimate(
            flops=6 * n * local * block.shape[0], bytes_accessed=4 * n * local, transcendentals=0
        ),
        name="unsort",
    )(first, rank, block)


def plan_blocks(own_y, near, far, regions, here, flags, columns, capacity):
    reach = flags.shape[0]
    rows = own_y.shape[0] // ROWS
    y_own = own_y.reshape(rows, ROWS)
    distance = regions - here
    ahead = jnp.arange(reach, dtype=jnp.int32)
    own_flag = jnp.sum(jnp.where(distance[..., None] == ahead, flags, 0.0), axis=-1)
    half = near.shape[0]
    counted = []
    for part, piece in enumerate((near, far)):
        extra = piece[:, :, columns:, :]
        y = [extra[:, :, k].astype(jnp.float32).reshape(half, -1, extra.shape[3] // LANES, LANES) for k in (1, 4, 7)]
        lowest = (y[0][..., 0] + y[1][..., 0]) + y[2][..., 0]
        highest = (y[0][..., -1] + y[1][..., -1]) + y[2][..., -1]
        side = slice(part * half, (part + 1) * half)
        far_flag = jnp.sum(
            jnp.where(-distance[side, :, None] == ahead, extra[:, :, 9, :reach].astype(jnp.float32), 0.0), axis=-1
        )
        listed = ((own_flag[side] + far_flag) > 0.5)[..., None]
        active = listed & (lowest <= y_own[:, -1, None, None, None] + CUTOFF)
        active = active & (highest >= y_own[:, 0, None, None, None] - CUTOFF)
        counted.append(active.astype(jnp.int32).reshape(rows, -1))
    size = counted[0].shape[1]
    totals = [jnp.sum(count, axis=1) for count in counted]
    pairs = lax.shift_right_logical(totals[0] + totals[1] + PAIR - 1, PAIR.bit_length() - 1)
    row = jnp.arange(rows, dtype=jnp.int32)
    base = jnp.sum(jnp.where(row[:, None] < row[None, :], pairs[:, None], 0), axis=0)
    index = jnp.arange(size, dtype=jnp.int32)
    spot = jnp.arange(capacity * BATCH, dtype=jnp.int32)
    ids = jnp.full(spot.shape, -1, jnp.int32)
    for part, count in enumerate(counted):
        before = jnp.sum(jnp.where(index[None, :, None] < index[None, None, :], count[:, :, None], 0), axis=1)
        place = (base * PAIR + (totals[0] if part else 0))[:, None] + before
        hit = (count > 0)[:, :, None] & (place[:, :, None] == spot)
        ids = ids + jnp.sum(jnp.where(hit, index[None, :, None] + (part * size + 1), 0), axis=(0, 1))
    step = jnp.arange(capacity * BATCH // PAIR, dtype=jnp.int32)
    owner = jnp.sum((base + pairs)[:, None] <= step[None, :], axis=0, dtype=jnp.int32)
    return ids, jnp.minimum(owner, rows - 1), base + pairs


def gaspari_cohn(squared):
    squared = jnp.maximum(squared, 1e-12)
    inverse = lax.rsqrt(squared)
    scaled = squared * inverse
    near = (((-3.0 * scaled + 6.0) * scaled + 7.5) * scaled - 20.0) * squared + 12.0
    left = jnp.maximum(2.0 - scaled, 0.0)
    left = left * left
    far = (left * left) * (((scaled + 2.0) * scaled - 0.5) * inverse)
    return jnp.where(scaled <= 1.0, near, far)


def tiles_kernel(build, started, wanted, ids_ref, owner_ref, count_ref, own_ref, near_ref, other_ref, *refs):
    refs = list(refs)
    tiles_ref = None if build else refs.pop(0)
    start_ref = refs.pop(0) if started else None
    block_ref = scale_ref = out_ref = rounded_ref = gram_ref = None
    if wanted:
        block_ref, scale_ref = refs[:2]
        refs = refs[2:]
    tiles_ref = refs.pop(0) if build else tiles_ref
    if wanted:
        out_ref, rounded_ref, gram_ref = refs[:3]
        refs = refs[3:]
        wide_ref, far_ref, all_ref, total_ref, piece_sems = refs
        held_ref = tiles_ref
    else:
        total_ref, wide_ref, far_ref, all_ref, piece_sems, held_ref, sems = refs
    half, height, local = near_ref.shape
    columns = total_ref.shape[1]
    capacity = held_ref.shape[0]
    chunk_bits = (local // LANES).bit_length() - 1
    total = lax.div(count_ref[local // ROWS - 1] * PAIR + BATCH - 1, BATCH)

    copies = [
        pltpu.make_async_copy(ref, all_ref.at[pl.ds(part * half, half)], piece_sems.at[part])
        for part, ref in enumerate((near_ref, other_ref))
    ]
    for copy in copies:
        copy.start()

    def copy_out(batch):
        return pltpu.make_async_copy(
            held_ref.at[batch], tiles_ref.at[batch], sems.at[lax.rem(batch, RING)]
        )

    def copy_in(group):
        first = group * UNROLL
        return pltpu.make_async_copy(
            tiles_ref.at[pl.ds(first, UNROLL)], held_ref.at[pl.ds(first, UNROLL)], sems.at[group]
        )

    groups = lax.div(total + UNROLL - 1, UNROLL)
    if not build and not wanted:

        def start_copy(group, carry):
            copy_in(group).start()
            return carry

        lax.fori_loop(0, groups, start_copy, 0)
    if start_ref is None:
        total_ref[...] = jnp.zeros(total_ref.shape, jnp.float32)
    else:
        total_ref[...] = start_ref[...]
    if build:
        column = jnp.transpose(own_ref[...])
        for row in range(3):
            scale = 2.0 if row < 2 else 1.0
            wide_ref[row] = jnp.broadcast_to(scale * column[:, row : row + 1], (local, LANES))
    for copy in copies:
        copy.wait()
    if build:
        for place in range(2 * half):
            rows = all_ref[place, columns:, :].astype(jnp.float32)
            rows = (rows[0:3] + rows[3:6]) + rows[6:9]
            far_ref[place, 0:3, :] = jnp.concatenate([2.0 * rows[0:2], (1.0 / 12.0) * rows[2:3]], axis=0)

    def locate(batch, part):
        entry = ids_ref[batch * BATCH + part]
        chunk = jnp.maximum(entry, 0)
        lane = pl.multiple_of((chunk & ((1 << chunk_bits) - 1)) * LANES, LANES)
        return entry, lax.shift_right_logical(chunk, chunk_bits), lane

    def rows_of(batch, pair):
        return pl.ds(pl.multiple_of(owner_ref[batch * (BATCH // PAIR) + pair] * ROWS, ROWS), ROWS)

    def build_batch(batch):
        for part in range(BATCH):
            rows = rows_of(batch, part // PAIR)
            entry, place, lane = locate(batch, part)
            far = far_ref[place, :, pl.ds(lane, LANES)]
            across_x = wide_ref[0, rows, :] - far[0:1, :]
            across_y = wide_ref[1, rows, :] - far[1:2, :]
            value = gaspari_cohn(across_x * across_x + across_y * across_y)
            spread = jnp.where(entry >= 0, far[2:3, :], 0.0)
            value = wide_ref[2, rows, :] * spread * value
            held_ref[batch, :, part * LANES : (part + 1) * LANES] = value.astype(jnp.bfloat16)

    def product(batch, valid=None):
        values = []
        for pair in range(BATCH // PAIR):
            sides = []
            for part in range(pair * PAIR, (pair + 1) * PAIR):
                _, place, lane = locate(batch, part)
                sides.append(all_ref[place, :columns, pl.ds(lane, LANES)])
            side = jnp.concatenate(sides, axis=1)
            if valid is not None:
                side = jnp.where(valid, side, jnp.zeros_like(side))
            lanes = slice(pair * PAIR * LANES, (pair + 1) * PAIR * LANES)
            values.append(dot_nt(held_ref[batch, :, lanes], side))
        return values

    def add_product(batch, values):
        for pair, value in enumerate(values):
            total_ref[rows_of(batch, pair), :] += value

    if build:

        @pl.when(total > 0)
        def _():
            build_batch(0)
            if not wanted:
                copy_out(0).start()

            def turn(batch, carry):
                if not wanted:

                    @pl.when(batch >= RING)
                    def _():
                        copy_out(batch - RING).wait()

                value = product(batch - 1)
                build_batch(batch)
                add_product(batch - 1, value)
                if not wanted:
                    copy_out(batch).start()
                return carry

            lax.fori_loop(1, total, turn, 0)
            add_product(total - 1, product(total - 1))
            if not wanted:

                def finish(batch, carry):
                    copy_out(batch).wait()
                    return carry

                lax.fori_loop(jnp.maximum(total - RING, 0), total, finish, 0)

    else:

        def turn(group, carry):
            if not wanted:
                copy_in(group).wait()
            batches = [jnp.minimum(group * UNROLL + i, total - 1) for i in range(UNROLL)]
            values = [
                product(batch, group * UNROLL + i < total if i else None)
                for i, batch in enumerate(batches)
            ]
            for batch, value in zip(batches, values):
                add_product(batch, value)
            return carry

        lax.fori_loop(0, groups, turn, 0)

    if wanted:
        block = block_ref[...]
        result = jnp.transpose(total_ref[...]) + scale_ref[...] * block
        out_ref[...] = result
        rounded_ref[...] = result.astype(jnp.bfloat16)
        gram_ref[...] = dot_nt(block, jnp.concatenate([block, result], axis=0), HIGHEST)


def run_tiles(plan, own, near, far, tiles, capacity, columns, start, finish):
    build = tiles is None
    wanted = finish is not None
    kept = pl.BlockSpec(memory_space=pltpu.VMEM if wanted else pltpu.HBM)
    near, far = [piece.reshape((-1,) + piece.shape[2:]) for piece in (near, far)]
    half, height, local = near.shape
    smem = pl.BlockSpec(memory_space=pltpu.SMEM)
    anywhere = pl.BlockSpec(memory_space=pl.ANY)
    operands = [*plan, own, near, far]
    in_specs = [smem, smem, smem] + whole_vmem(1) + [anywhere] * 2
    out_shape, out_specs = [], []
    if not build:
        operands.append(tiles)
        in_specs.append(kept)
    if start is not None:
        operands.append(start)
        in_specs += whole_vmem(1)
    if wanted:
        operands += finish
        in_specs += whole_vmem(2)
    if build:
        space = pltpu.VMEM if wanted else pltpu.HBM
        out_shape.append(space((capacity, ROWS, BATCH * LANES), jnp.bfloat16))
        out_specs.append(kept)
    total_shape = (local, columns)
    scratch = []
    if wanted:
        out_shape += [
            jax.ShapeDtypeStruct((columns, local), jnp.float32),
            jax.ShapeDtypeStruct((columns, local), jnp.bfloat16),
            jax.ShapeDtypeStruct((columns, 2 * columns), jnp.float32),
        ]
        out_specs += whole_vmem(3)
    else:
        out_shape.append(jax.ShapeDtypeStruct(total_shape, jnp.float32))
        out_specs += whole_vmem(1)
    scratch += [
        pltpu.VMEM((3, local, LANES), jnp.float32),
        pltpu.VMEM((2 * half, 8, local), jnp.float32),
        pltpu.VMEM((2 * half, height, local), jnp.bfloat16),
    ]
    if wanted:
        scratch.append(pltpu.VMEM(total_shape, jnp.float32))
    scratch.append(pltpu.SemaphoreType.DMA((2,)))
    if not wanted:
        scratch.append(pltpu.VMEM((capacity, ROWS, BATCH * LANES), jnp.bfloat16))
        scratch.append(pltpu.SemaphoreType.DMA((RING if build else capacity // UNROLL,)))
    work = 2 * local * local
    return pl.pallas_call(
        functools.partial(tiles_kernel, build, start is not None, wanted),
        out_shape=tuple(out_shape),
        in_specs=in_specs,
        out_specs=tuple(out_specs),
        scratch_shapes=scratch,
        compiler_params=pltpu.CompilerParams(vmem_limit_bytes=VMEM),
        cost_estimate=pl.CostEstimate(
            flops=work * (18000 if build else 9000), bytes_accessed=8 * work, transcendentals=0
        ),
        name=("build" if build else "apply") + ("_last" if wanted else "_first"),
    )(*operands)


def reciprocal(value):
    root = lax.rsqrt(value)
    return root * root


def small_product(left, right):
    return [[sum(l * r[j] for l, r in zip(row, right)) for j in range(len(right[0]))] for row in left]


def small_difference(left, right):
    return [[l - r for l, r in zip(*rows)] for rows in zip(left, right)]


def small_inverse(matrix):
    (a, b), (c, d) = matrix
    scale = reciprocal(a * d - b * c)
    return [[d * scale, -b * scale], [-c * scale, a * scale]]


def solve_positive(matrix, target):
    n = matrix.shape[0]
    table = jnp.concatenate([0.5 * (matrix + jnp.transpose(matrix)), target], axis=1)
    bands = [table[k : k + 8, :] for k in range(0, n, 8)]
    row_index = lax.broadcasted_iota(jnp.int32, bands[0].shape, 0)
    for k in range(0, n, 4):
        own, row = k // 8, k % 8
        columns = [
            [jnp.broadcast_to(band[:, k + j : k + j + 1], band.shape) for band in bands] for j in range(4)
        ]
        pivot = [[columns[j][own][row + i : row + i + 1] for j in range(4)] for i in range(4)]
        upper, lower = pivot[:2], pivot[2:]
        top = small_inverse([r[:2] for r in upper])
        factor = small_product([r[:2] for r in lower], top)
        right = [r[2:] for r in upper]
        rest = small_inverse(small_difference([r[2:] for r in lower], small_product(factor, right)))
        rows = [[bands[own][row + i : row + i + 1]] for i in range(4)]
        last = small_product(rest, small_difference(rows[2:], small_product(factor, rows[:2])))
        first = small_product(top, small_difference(rows[:2], small_product(right, last)))
        new = [r[0] for r in first + last]
        bands = [
            band - ((columns[0][i] * new[0] + columns[1][i] * new[1]) + (columns[2][i] * new[2] + columns[3][i] * new[3]))
            for i, band in enumerate(bands)
        ]
        for i in range(4):
            bands[own] = jnp.where(row_index == row + i, new[i], bands[own])
    return jnp.concatenate([band[:, n:] for band in bands], axis=0)


def last_kernel(grams_ref, start_ref, images_ref, weights_ref, residual_ref):
    n = grams_ref.shape[1]
    squares, mixed = grams_ref[0, :, :n], grams_ref[0, :, n:]
    images, cross = grams_ref[1, :, :n], grams_ref[1, :, n:]
    solved = solve_positive(mixed, jnp.concatenate([squares, images], axis=1))
    step, carried = solved[:, :n], solved[:, n:]
    product = dot_nn(images, solved, HIGHEST)
    second = solve_positive(cross - product[:, n:], jnp.transpose(mixed) - product[:, :n])
    first = jnp.transpose(step - dot_nn(carried, second, HIGHEST))
    second = jnp.transpose(second)
    both = jnp.concatenate([first, second], axis=1)
    start, images = start_ref[...], images_ref[...]
    weights_ref[...] = dot_nn(both, jnp.concatenate([start, images[:n]], axis=0), HIGHEST)
    residual_ref[...] = start - dot_nn(both, images, HIGHEST)


def last_step(grams, start, images):
    return pl.pallas_call(
        last_kernel,
        out_shape=(jax.ShapeDtypeStruct(start.shape, jnp.float32),) * 2,
        in_specs=whole_vmem(3),
        out_specs=tuple(whole_vmem(2)),
        compiler_params=pltpu.CompilerParams(vmem_limit_bytes=VMEM),
        name="last_step",
    )(grams, start, images)


def shards(innovations, obs_geometry, obs_error, tile_owner):
    tiles_axis, regions = lax.axis_size("tile"), lax.axis_size("region")
    reach = tile_owner.shape[1]
    here, tile = lax.axis_index("region"), lax.axis_index("tile")
    columns, local = innovations.shape
    slot_tile = tile ^ jnp.arange(tiles_axis, dtype=jnp.int32)
    first = slot_tile * local
    even, odd = slot_offsets(regions)
    slot_region = here ^ jnp.where((slot_tile % 2 == 0)[:, None], even, odd)

    message, own, start, rank = sort_region(
        first,
        tile_owner,
        *halves(obs_geometry, "tile"),
        *halves(obs_error[None, :], "tile"),
        *halves(innovations, "tile"),
    )
    scale = own[3:4]
    flags = jnp.where(tile_owner[0] >= 0, 1.0, 0.0).astype(jnp.float32)

    def capacity_of(count):
        most = min(count, 2 * reach - 1) * tiles_axis * (local // LANES)
        batches = -(-(local // ROWS) * -(-most // PAIR) * PAIR // BATCH)
        return -(-batches // UNROLL) * UNROLL

    def sweep(sent, block, plans, stored):
        total, slot, results = None, 0, None
        groups = exchange(sent)
        for index, group in enumerate(groups):
            if index:
                group, total = lax.optimization_barrier((group, total))
            count = group.shape[0]
            capacity = capacity_of(count)
            near, far = halves(group, "tile")
            if stored is None:
                inside = slot_region[:, slot : slot + count]
                plan = plan_blocks(own[1], near, far, inside, here, flags, columns, capacity)
                plans.append(plan)
            slot += count
            last = index + 1 == len(groups)
            results = run_tiles(
                plans[index], own, near, far, None if stored is None else stored[index], capacity,
                columns, total, (block, scale) if last else None,
            )
            if stored is None:
                made.append(results[0])
                results = results[1:]
            total = results[0]
        return results

    plans, made = [], []
    image, image_rounded, grams = sweep(message, start, plans, None)
    second, _, cross = sweep(image_rounded, image, plans, made)
    grams = jnp.stack([grams, cross])
    grams = sum_regions(sum_tiles(grams))
    near, far = halves(jnp.concatenate([image, second], axis=0), "tile")
    images = unsort(first, rank, jnp.concatenate([*near, *far], axis=1))
    return last_step(grams, innovations, images)


def solution(mesh):
    return jax.shard_map(
        shards,
        mesh=mesh,
        in_specs=(
            P(None, ("region", "tile")),
            P(None, ("region", "tile")),
            P(("region", "tile")),
            P("region", None),
        ),
        out_specs=(P(None, ("region", "tile")), P(None, ("region", "tile"))),
        check_vma=False,
    )
```

```python
import functools

import jax
import jax.numpy as jnp
from jax import lax
from jax.experimental import pallas as pl
from jax.experimental.pallas import tpu as pltpu
from jax.sharding import PartitionSpec as P

CUTOFF = 1.001
ROW_SHIFT, SKIP = 20, 1 << 19
LANES = 128
ROWS = 64
PAIR = 2
BATCH = 2 * PAIR
RING = 8
UNROLL = 4
VMEM = 16 * 1024 * 1024
HIGHEST = lax.Precision.HIGHEST


def whole_vmem(count):
    return [pl.BlockSpec(memory_space=pltpu.VMEM)] * count


def in_hbm(value):
    return pltpu.with_memory_space_constraint(value, pltpu.HBM)


def dot_nt(left, right, precision=None):
    return lax.dot_general(
        left, right, (((1,), (1,)), ((), ())), precision=precision, preferred_element_type=jnp.float32
    )


def dot_nn(left, right, precision=None):
    return lax.dot_general(
        left, right, (((1,), (0,)), ((), ())), precision=precision, preferred_element_type=jnp.float32
    )


def three_parts(value):
    high = value.astype(jnp.bfloat16)
    rest = value - high.astype(jnp.float32)
    middle = rest.astype(jnp.bfloat16)
    low = (rest - middle.astype(jnp.float32)).astype(jnp.bfloat16)
    return high, middle, low


def halves(block, axis):
    count = lax.axis_size(axis)
    block = block[None]
    bit = 1
    while 2 * bit < count:
        block = jnp.concatenate([block, swapped(block, axis, bit)], axis=0)
        bit *= 2
    return block, swapped(block, axis, bit)


def swapped(block, axis, bit):
    return lax.ppermute(block, axis, [(i, i ^ bit) for i in range(lax.axis_size(axis))])


def sum_tiles(block):
    bit = 1
    while bit < lax.axis_size("tile"):
        block = block + swapped(block, "tile", bit)
        bit *= 2
    return block


def swap_regions(block, even, odd):
    tiles = lax.axis_size("tile")
    route = [
        (region * tiles + tile, (region ^ (odd if tile % 2 else even)) * tiles + tile)
        for region in range(lax.axis_size("region"))
        for tile in range(tiles)
    ]
    return lax.ppermute(block, ("region", "tile"), route)


def sum_regions(block):
    bits, _ = region_orders(lax.axis_size("region"))
    middle = len(bits) // 2
    for even, odd in zip(bits, bits[middle:] + bits[:middle]):
        block = block + swap_regions(block, even, odd)
    return block


def region_orders(count):
    bits = []
    bit = count // 2
    while bit:
        bits.append(bit)
        bit //= 2
    return bits, bits[:1] + bits[-1:] + bits[1:-1] if len(bits) > 2 else bits[::-1]


def slot_offsets(count):
    table = []
    for bits in region_orders(count):
        offsets = [0]
        for bit in bits:
            offsets = offsets + [offset ^ bit for offset in offsets]
        table.append(offsets)
    return [jnp.array(offsets, jnp.int32) for offsets in table]


def exchange(block):
    regions = lax.axis_size("region")
    block = block[None]
    for even, odd in zip(*region_orders(regions)):
        other = swap_regions(block, even, odd)
        if 2 * block.shape[0] == regions:
            return block, other
        block = jnp.concatenate([block, other], axis=0)


def stacked_parts(value):
    return jnp.concatenate([part.astype(jnp.float32) for part in three_parts(value)], axis=0).astype(
        jnp.bfloat16
    )


def add_parts(value):
    rows = value.shape[0] // 3
    return (value[2 * rows :] + value[rows : 2 * rows]) + value[:rows]


def fill_order(first, rank, order_ref, row, count):
    step = 64

    def fill(block, carry):
        start = pl.multiple_of(block * step, step)
        place = first + start + lax.broadcasted_iota(jnp.int32, (step, rank.shape[1]), 0)
        order_ref[pl.ds(pl.multiple_of(row + start, step), step), :] = jnp.where(
            place == rank, 1.0, 0.0
        ).astype(jnp.bfloat16)
        return carry

    lax.fori_loop(0, count // step, fill, 0)


def sort_kernel(
    first_ref, owner_ref, near_ref, far_ref, near_error_ref, far_error_ref, block_ref, other_ref,
    rounded_out, places_out, own_out, block_out, rank_out,
    order_ref, column_ref, owned_ref, places_ref, errors_ref, blocks_ref, sems,
):
    columns, local = block_out.shape
    half = block_ref.shape[0]
    pairs = [(owner_ref, owned_ref)]
    for sources, target in (
        ((near_ref, far_ref), places_ref),
        ((near_error_ref, far_error_ref), errors_ref),
        ((block_ref, other_ref), blocks_ref),
    ):
        pairs += [(ref, target.at[pl.ds(part * half, half)]) for part, ref in enumerate(sources)]
    copies = [
        pltpu.make_async_copy(source, target, sems.at[index])
        for index, (source, target) in enumerate(pairs)
    ]
    for copy in copies:
        copy.start()
    for copy in copies[:5]:
        copy.wait()
    places = jnp.concatenate(
        [jnp.concatenate([places_ref[i], errors_ref[i]], axis=0) for i in range(2 * half)], axis=1
    )
    n = places.shape[1]
    step = 64
    index = jnp.concatenate(
        [
            (first_ref[i] + lax.broadcasted_iota(jnp.int32, (1, local), 1)).astype(jnp.float32)
            for i in range(n // local)
        ],
        axis=1,
    )
    y_row = places[1:2, :]
    column_ref[...] = jnp.transpose(
        jnp.concatenate([y_row, index, jnp.zeros((6, n), jnp.float32)], axis=0)
    )

    def count(block, total):
        start = pl.multiple_of(block * step, step)
        y_column = jnp.broadcast_to(column_ref[pl.ds(start, step), 0:1], (step, n))
        index_column = jnp.broadcast_to(column_ref[pl.ds(start, step), 1:2], (step, n))
        before = (y_column < y_row) | ((y_column == y_row) & (index_column < index))
        return total + jnp.sum(jnp.where(before, 1.0, 0.0).reshape(step // 8, 8, n), axis=0)

    total = lax.fori_loop(0, n // step, count, jnp.zeros((8, n), jnp.float32))
    rank = jnp.sum(total, axis=0, keepdims=True).astype(jnp.int32)
    rank_out[...] = rank[:, :local]
    fill_order(first_ref[0], rank, order_ref, 0, local)
    for copy in copies[5:]:
        copy.wait()
    blocks = [blocks_ref[i] for i in range(2 * half)]
    everything = jnp.concatenate([jnp.concatenate(blocks, axis=1), places, jnp.zeros((4, n), jnp.float32)], axis=0)
    whole = add_parts(dot_nt(stacked_parts(everything), order_ref[...]))
    block_out[...] = whole[:columns]
    own_out[...] = whole[columns:]
    rounded_out[...] = whole[:columns].astype(jnp.bfloat16)
    lane = lax.broadcasted_iota(jnp.int32, (1, local), 1)
    flags = jnp.zeros((1, local), jnp.float32)
    for offset in range(owner_ref.shape[1]):
        flags = jnp.where((lane == offset) & (owned_ref[0, offset] >= 0), 1.0, flags)
    places_out[...] = jnp.concatenate([whole[columns : columns + 3], flags], axis=0)


def sort_region(first, tile_owner, near, far, near_error, far_error, block, other):
    local = near.shape[2]
    n = local * 2 * near.shape[0]
    columns = block.shape[1]
    smem = pl.BlockSpec(memory_space=pltpu.SMEM)
    return pl.pallas_call(
        sort_kernel,
        out_shape=(
            jax.ShapeDtypeStruct((columns, local), jnp.bfloat16),
            jax.ShapeDtypeStruct((4, local), jnp.float32),
            jax.ShapeDtypeStruct((8, local), jnp.float32),
            jax.ShapeDtypeStruct((columns, local), jnp.float32),
            jax.ShapeDtypeStruct((1, local), jnp.int32),
        ),
        in_specs=[smem] + [pl.BlockSpec(memory_space=pl.ANY)] * 7,
        out_specs=tuple(whole_vmem(5)),
        scratch_shapes=[
            pltpu.VMEM((local, n), jnp.bfloat16),
            pltpu.VMEM((n, 8), jnp.float32),
            pltpu.SMEM(tile_owner.shape, jnp.int32),
            pltpu.VMEM((n // local, 3, local), jnp.float32),
            pltpu.VMEM((n // local, 1, local), jnp.float32),
            pltpu.VMEM((n // local, columns, local), jnp.float32),
            pltpu.SemaphoreType.DMA((7,)),
        ],
        compiler_params=pltpu.CompilerParams(vmem_limit_bytes=VMEM),
        cost_estimate=pl.CostEstimate(
            flops=6 * n * local * (columns + 8), bytes_accessed=4 * n * local, transcendentals=0
        ),
        name="sort_region",
    )(first, in_hbm(tile_owner), in_hbm(near), far, in_hbm(near_error), far_error, in_hbm(block), other)


def unsort_kernel(first_ref, rank_ref, block_ref, block_out, order_ref):
    n, local = order_ref.shape
    for slot in range(n // local):
        fill_order(first_ref[slot], rank_ref[...], order_ref, slot * local, local)
    block_out[...] = add_parts(dot_nn(stacked_parts(block_ref[...]), order_ref[...]))


def unsort(first, rank, block):
    n = block.shape[1]
    local = rank.shape[1]
    return pl.pallas_call(
        unsort_kernel,
        out_shape=jax.ShapeDtypeStruct((block.shape[0], local), jnp.float32),
        in_specs=[pl.BlockSpec(memory_space=pltpu.SMEM)] + whole_vmem(2),
        out_specs=whole_vmem(1)[0],
        scratch_shapes=[pltpu.VMEM((n, local), jnp.bfloat16)],
        compiler_params=pltpu.CompilerParams(vmem_limit_bytes=VMEM),
        cost_estimate=pl.CostEstimate(
            flops=6 * n * local * block.shape[0], bytes_accessed=4 * n * local, transcendentals=0
        ),
        name="unsort",
    )(first, rank, block)


def plan_blocks(
    distance_ref, listed_ref, own_ref, far_ref, chunks, stage_ref, bounds_ref, ids_ref, count_ref, sem, prepare,
):
    places, local = far_ref.shape[0], own_ref.shape[1]
    reach = listed_ref.shape[1]
    blocks = local // ROWS
    lane = lax.broadcasted_iota(jnp.int32, (1, LANES), 1)

    lowest = jnp.zeros((1, LANES), jnp.float32)
    highest = lowest
    for block in range(blocks):
        here = (lane == block) | (lane == blocks + block)
        low = own_ref[1:2, block * ROWS : block * ROWS + 1]
        high = own_ref[1:2, (block + 1) * ROWS - 1 : (block + 1) * ROWS]
        lowest = jnp.where(here, 2.0 * (low - CUTOFF), lowest)
        highest = jnp.where(here, 2.0 * (high + CUTOFF), highest)
    y = far_ref[:, 1, :]
    first = jnp.zeros((places, LANES), jnp.int32)
    beyond = first
    for chunk in range(chunks):
        low = y[:, chunk * LANES : chunk * LANES + 1]
        high = y[:, (chunk + 1) * LANES - 1 : (chunk + 1) * LANES]
        first = first + (high < lowest).astype(jnp.int32)
        beyond = beyond + (low <= highest).astype(jnp.int32)
    distance = distance_ref[...]
    flags = jnp.where((lane == -distance) & (far_ref[:, 3, :LANES] > 0.0), 1.0, 0.0)
    for offset in range(reach):
        mine = jnp.where(listed_ref[0, offset] >= 0, 1.0, 0.0)
        flags = flags + jnp.where((lane == offset) & (distance == offset), mine, 0.0)
    listed = jnp.sum(flags, axis=1, keepdims=True) > 0.0
    found = jnp.where(listed, jnp.maximum(beyond - first, 0), 0)
    stage_ref[...] = jnp.where(lane < blocks, first, found)
    copy = pltpu.make_async_copy(stage_ref, bounds_ref, sem)
    copy.start()
    prepare()
    copy.wait()

    count = jnp.int32(0)
    for block in range(blocks):

        def add_place(place, count, block=block):
            entry = (block << ROW_SHIFT) + place * chunks + bounds_ref[place, block]
            for chunk in range(chunks):
                ids_ref[count + chunk] = entry + chunk
            return count + bounds_ref[place, blocks + block]

        count = lax.fori_loop(0, places, add_place, count, unroll=8)
        for extra in range(PAIR - 1):
            ids_ref[count + extra] = (block << ROW_SHIFT) + SKIP
        count = lax.div(count + PAIR - 1, PAIR) * PAIR
    for extra in range(BATCH - PAIR):
        ids_ref[count + extra] = SKIP
    count_ref[0] = lax.div(count + BATCH - 1, BATCH)


def gaspari_cohn(squared):
    squared = jnp.maximum(squared, 1e-12)
    inverse = lax.rsqrt(squared)
    scaled = squared * inverse
    near = (((-3.0 * scaled + 6.0) * scaled + 7.5) * scaled - 20.0) * squared + 12.0
    left = jnp.maximum(2.0 - scaled, 0.0)
    left = left * left
    far = (left * left) * (((scaled + 2.0) * scaled - 0.5) * inverse)
    return jnp.where(scaled <= 1.0, near, far)


def locate(ids_ref, batch, part, chunk_bits):
    entry = ids_ref[batch * BATCH + part]
    lane = pl.multiple_of((entry & ((1 << chunk_bits) - 1)) * LANES, LANES)
    start = pl.multiple_of(lax.shift_right_logical(entry, ROW_SHIFT) * ROWS, ROWS)
    place = lax.shift_right_logical(entry & (SKIP - 1), chunk_bits)
    return (entry & SKIP) == 0, place, pl.ds(lane, LANES), pl.ds(start, ROWS)


def build_kernel(
    kept, place_ref, distance_ref, listed_ref, own_ref, near_ref, other_ref,
    ids_ref, count_ref, tiles_ref,
    wide_ref, far_ref, stage_ref, bounds_ref, bounds_sem, *through,
):
    local = own_ref.shape[1]
    places = far_ref.shape[0]
    chunk_bits = (local // LANES).bit_length() - 1
    factor = jnp.where(lax.broadcasted_iota(jnp.int32, (4, 1), 0) < 2, 2.0, 1.0 / 12.0)
    for index in range(places):
        side_ref = near_ref if 2 * index < places else other_ref
        far_ref[index, 0:4, :] = factor * side_ref[place_ref[index]]

    def prepare():
        column = jnp.transpose(own_ref[...])
        for row in range(3):
            scale = 2.0 if row < 2 else 1.0
            wide_ref[row] = jnp.broadcast_to(scale * column[:, row : row + 1], (local, LANES))

    plan_blocks(
        distance_ref, listed_ref, own_ref, far_ref, 1 << chunk_bits,
        stage_ref, bounds_ref, ids_ref, count_ref, bounds_sem, prepare,
    )
    total = count_ref[0]
    held_ref, sems = (tiles_ref, None) if kept else through

    def copy_out(batch):
        return pltpu.make_async_copy(
            held_ref.at[batch], tiles_ref.at[batch], sems.at[lax.rem(batch, RING)]
        )

    def build_batch(batch, carry):
        if not kept:

            @pl.when(batch >= RING)
            def _():
                copy_out(batch - RING).wait()

        for part in range(BATCH):
            real, place, lanes, rows = locate(ids_ref, batch, part, chunk_bits)
            far = far_ref[place, :, lanes]
            across_x = wide_ref[0, rows, :] - far[0:1, :]
            across_y = wide_ref[1, rows, :] - far[1:2, :]
            value = gaspari_cohn(across_x * across_x + across_y * across_y)
            spread = jnp.where(real, far[2:3, :], 0.0)
            value = wide_ref[2, rows, :] * spread * value
            held_ref[batch, :, part * LANES : (part + 1) * LANES] = value.astype(jnp.bfloat16)
        if not kept:
            copy_out(batch).start()
        return carry

    lax.fori_loop(0, total, build_batch, 0)
    if not kept:

        def finish(batch, carry):
            copy_out(batch).wait()
            return carry

        lax.fori_loop(jnp.maximum(total - RING, 0), total, finish, 0)


def build_tiles(place, distance, tile_owner, own, near, far, capacity, kept):
    near, far = [piece.reshape((-1,) + piece.shape[2:]) for piece in (near, far)]
    places, local = place.shape[0], own.shape[1]
    smem = pl.BlockSpec(memory_space=pltpu.SMEM)
    sizes = (capacity * BATCH + local // LANES, 1)
    shape = (capacity, ROWS, BATCH * LANES)
    scratch = [
        pltpu.VMEM((3, local, LANES), jnp.float32),
        pltpu.VMEM((places, 8, local), jnp.float32),
        pltpu.VMEM((places, LANES), jnp.int32),
        pltpu.SMEM((places, LANES), jnp.int32),
        pltpu.SemaphoreType.DMA,
    ]
    if not kept:
        scratch += [pltpu.VMEM(shape, jnp.bfloat16), pltpu.SemaphoreType.DMA((RING,))]
    return pl.pallas_call(
        functools.partial(build_kernel, kept),
        out_shape=tuple(jax.ShapeDtypeStruct((size,), jnp.int32) for size in sizes)
        + ((pltpu.VMEM if kept else pltpu.HBM)(shape, jnp.bfloat16),),
        in_specs=[smem] + whole_vmem(1) + [smem] + whole_vmem(3),
        out_specs=(smem,) * 2 + (pl.BlockSpec(memory_space=pltpu.VMEM if kept else pltpu.HBM),),
        scratch_shapes=scratch,
        compiler_params=pltpu.CompilerParams(vmem_limit_bytes=VMEM),
        cost_estimate=pl.CostEstimate(
            flops=2 * local * local * 16000, bytes_accessed=16 * local * local, transcendentals=0
        ),
        name="build_kept" if kept else "build_passed",
    )(place, distance, tile_owner, own, near, far)


def apply_kernel(started, last, ids_ref, count_ref, near_ref, other_ref, tiles_ref, *refs):
    refs = list(refs)
    start_ref = refs.pop(0) if started else None
    if last:
        block_ref, scale_ref, out_ref, rounded_ref, gram_ref, all_ref, piece_sems, total_ref = refs
        held_ref = tiles_ref
    else:
        total_ref, all_ref, piece_sems, held_ref, sems = refs
    half, columns, local = near_ref.shape
    chunk_bits = (local // LANES).bit_length() - 1
    total = count_ref[0]
    groups = lax.div(total + UNROLL - 1, UNROLL)

    copies = [
        pltpu.make_async_copy(ref, all_ref.at[pl.ds(part * half, half)], piece_sems.at[part])
        for part, ref in enumerate((near_ref, other_ref))
    ]
    for copy in copies:
        copy.start()

    def copy_in(group):
        first = group * UNROLL
        return pltpu.make_async_copy(
            tiles_ref.at[pl.ds(first, UNROLL)], held_ref.at[pl.ds(first, UNROLL)], sems.at[group]
        )

    if not last:

        def start_copy(group, carry):
            copy_in(group).start()
            return carry

        lax.fori_loop(0, groups, start_copy, 0)
    if started:
        total_ref[...] = start_ref[...]
    else:
        total_ref[...] = jnp.zeros(total_ref.shape, jnp.float32)
    for copy in copies:
        copy.wait()

    def turn(group, carry):
        if not last:
            copy_in(group).wait()
        values = []
        for inner in range(UNROLL):
            batch = jnp.minimum(group * UNROLL + inner, total - 1)
            valid = group * UNROLL + inner < total
            for pair in range(BATCH // PAIR):
                sides = []
                for part in range(pair * PAIR, (pair + 1) * PAIR):
                    _, place, chunk, rows = locate(ids_ref, batch, part, chunk_bits)
                    sides.append(all_ref[place, :, chunk])
                side = jnp.concatenate(sides, axis=1)
                if inner:
                    side = jnp.where(valid, side, jnp.zeros_like(side))
                lanes = slice(pair * PAIR * LANES, (pair + 1) * PAIR * LANES)
                values.append((rows, dot_nt(held_ref[batch, :, lanes], side)))
        for rows, value in values:
            total_ref[rows, :] += value
        return carry

    lax.fori_loop(0, groups, turn, 0)
    if last:
        block = block_ref[...]
        result = jnp.transpose(total_ref[...]) + scale_ref[...] * block
        out_ref[...] = result
        rounded_ref[...] = result.astype(jnp.bfloat16)
        gram_ref[...] = dot_nt(block, jnp.concatenate([block, result], axis=0), HIGHEST)


def apply_tiles(plan, near, far, tiles, start, finish):
    near, far = [piece.reshape((-1,) + piece.shape[2:]) for piece in (near, far)]
    half, columns, local = near.shape
    last = finish is not None
    smem = pl.BlockSpec(memory_space=pltpu.SMEM)
    anywhere = pl.BlockSpec(memory_space=pl.ANY)
    operands = [*plan, near, far, tiles]
    in_specs = [smem] * 2 + [anywhere] * 2
    in_specs.append(pl.BlockSpec(memory_space=pltpu.VMEM if last else pltpu.HBM))
    if start is not None:
        operands.append(start)
        in_specs += whole_vmem(1)
    scratch = [
        pltpu.VMEM((2 * half, columns, local), jnp.bfloat16),
        pltpu.SemaphoreType.DMA((2,)),
    ]
    if last:
        operands += finish
        in_specs += whole_vmem(2)
        out_shape = (
            jax.ShapeDtypeStruct((columns, local), jnp.float32),
            jax.ShapeDtypeStruct((columns, local), jnp.bfloat16),
            jax.ShapeDtypeStruct((columns, 2 * columns), jnp.float32),
        )
        scratch.append(pltpu.VMEM((local, columns), jnp.float32))
    else:
        out_shape = (jax.ShapeDtypeStruct((local, columns), jnp.float32),)
        scratch.append(pltpu.VMEM(tiles.shape, jnp.bfloat16))
        scratch.append(pltpu.SemaphoreType.DMA((tiles.shape[0] // UNROLL,)))
    return pl.pallas_call(
        functools.partial(apply_kernel, start is not None, last),
        out_shape=out_shape,
        in_specs=in_specs,
        out_specs=tuple(whole_vmem(len(out_shape))),
        scratch_shapes=scratch,
        compiler_params=pltpu.CompilerParams(vmem_limit_bytes=VMEM),
        cost_estimate=pl.CostEstimate(
            flops=2 * local * local * 6000, bytes_accessed=16 * local * local, transcendentals=0
        ),
        name="apply_last" if last else "apply_first",
    )(*operands)


def reciprocal(value):
    root = lax.rsqrt(value)
    return root * root


def small_product(left, right):
    return [[sum(l * r[j] for l, r in zip(row, right)) for j in range(len(right[0]))] for row in left]


def small_difference(left, right):
    return [[l - r for l, r in zip(*rows)] for rows in zip(left, right)]


def small_inverse(matrix):
    (a, b), (c, d) = matrix
    scale = reciprocal(a * d - b * c)
    return [[d * scale, -b * scale], [-c * scale, a * scale]]


def solve_positive(matrix, target):
    n = matrix.shape[0]
    table = jnp.concatenate([0.5 * (matrix + jnp.transpose(matrix)), target], axis=1)
    bands = [table[k : k + 8, :] for k in range(0, n, 8)]
    row_index = lax.broadcasted_iota(jnp.int32, bands[0].shape, 0)
    for k in range(0, n, 4):
        own, row = k // 8, k % 8
        columns = [
            [jnp.broadcast_to(band[:, k + j : k + j + 1], band.shape) for band in bands] for j in range(4)
        ]
        pivot = [[columns[j][own][row + i : row + i + 1] for j in range(4)] for i in range(4)]
        upper, lower = pivot[:2], pivot[2:]
        top = small_inverse([r[:2] for r in upper])
        factor = small_product([r[:2] for r in lower], top)
        right = [r[2:] for r in upper]
        rest = small_inverse(small_difference([r[2:] for r in lower], small_product(factor, right)))
        rows = [[bands[own][row + i : row + i + 1]] for i in range(4)]
        last = small_product(rest, small_difference(rows[2:], small_product(factor, rows[:2])))
        first = small_product(top, small_difference(rows[:2], small_product(right, last)))
        new = [r[0] for r in first + last]
        bands = [
            band - ((columns[0][i] * new[0] + columns[1][i] * new[1]) + (columns[2][i] * new[2] + columns[3][i] * new[3]))
            for i, band in enumerate(bands)
        ]
        for i in range(4):
            bands[own] = jnp.where(row_index == row + i, new[i], bands[own])
    return jnp.concatenate([band[:, n:] for band in bands], axis=0)


def last_kernel(grams_ref, start_ref, images_ref, weights_ref, residual_ref):
    n = grams_ref.shape[1]
    squares, mixed = grams_ref[0, :, :n], grams_ref[0, :, n:]
    images, cross = grams_ref[1, :, :n], grams_ref[1, :, n:]
    solved = solve_positive(mixed, jnp.concatenate([squares, images], axis=1))
    step, carried = solved[:, :n], solved[:, n:]
    product = dot_nn(images, solved, HIGHEST)
    second = solve_positive(cross - product[:, n:], jnp.transpose(mixed) - product[:, :n])
    first = jnp.transpose(step - dot_nn(carried, second, HIGHEST))
    second = jnp.transpose(second)
    both = jnp.concatenate([first, second], axis=1)
    start, images = start_ref[...], images_ref[...]
    weights_ref[...] = dot_nn(both, jnp.concatenate([start, images[:n]], axis=0), HIGHEST)
    residual_ref[...] = start - dot_nn(both, images, HIGHEST)


def last_step(grams, start, images):
    return pl.pallas_call(
        last_kernel,
        out_shape=(jax.ShapeDtypeStruct(start.shape, jnp.float32),) * 2,
        in_specs=whole_vmem(3),
        out_specs=tuple(whole_vmem(2)),
        compiler_params=pltpu.CompilerParams(vmem_limit_bytes=VMEM),
        name="last_step",
    )(grams, start, images)


def shards(innovations, obs_geometry, obs_error, tile_owner):
    tiles_axis, regions = lax.axis_size("tile"), lax.axis_size("region")
    reach = tile_owner.shape[1]
    here, tile = lax.axis_index("region"), lax.axis_index("tile")
    columns, local = innovations.shape
    slot_tile = tile ^ jnp.arange(tiles_axis, dtype=jnp.int32)
    first = slot_tile * local
    even, odd = slot_offsets(regions)
    slot_region = here ^ jnp.where((slot_tile % 2 == 0)[:, None], even, odd)

    rounded, places, own, start, rank = sort_region(
        first,
        tile_owner,
        *halves(obs_geometry, "tile"),
        *halves(obs_error[None, :], "tile"),
        *halves(innovations, "tile"),
    )
    scale = own[3:4]
    everywhere = jnp.broadcast_to(places[None], (regions,) + places.shape)
    everywhere = lax.all_to_all(everywhere, "region", 0, 0)
    near_places, far_places = halves(everywhere, "tile")

    half_regions = regions // 2
    most = min(half_regions, 2 * reach - 1) * tiles_axis * (local // LANES)
    batches = -(-(local // ROWS) * -(-most // PAIR) * PAIR // BATCH) + 1
    capacity = -(-batches // UNROLL) * UNROLL
    stack = jnp.arange(tiles_axis, dtype=jnp.int32) % (tiles_axis // 2) * regions
    plans, tiles = [], []
    for part in range(2):
        inside = slot_region[:, part * half_regions : (part + 1) * half_regions]
        *plan, built = build_tiles(
            (stack[:, None] + inside).reshape(-1), (inside - here).reshape(-1, 1), tile_owner, own,
            near_places, far_places, capacity, part == 1,
        )
        plans.append(plan)
        tiles.append(built)

    def operate(sent, block, building):
        total = None
        for part, group in enumerate(exchange(sent)):
            if building:
                group, plans[part] = lax.optimization_barrier((group, plans[part]))
            elif part:
                group, total = lax.optimization_barrier((group, total))
            near, far = halves(group, "tile")
            results = apply_tiles(
                plans[part], near, far, tiles[part], total, (block, scale) if part else None
            )
            total = results[0]
        return results

    image, image_rounded, grams = operate(rounded, start, True)
    second, _, cross = operate(image_rounded, image, False)
    grams = jnp.stack([grams, cross])
    grams = sum_regions(sum_tiles(grams))
    near, far = halves(jnp.concatenate([image, second], axis=0), "tile")
    images = unsort(first, rank, jnp.concatenate([*near, *far], axis=1))
    return last_step(grams, innovations, images)


def solution(mesh):
    return jax.shard_map(
        shards,
        mesh=mesh,
        in_specs=(
            P(None, ("region", "tile")),
            P(None, ("region", "tile")),
            P(("region", "tile")),
            P("region", None),
        ),
        out_specs=(P(None, ("region", "tile")), P(None, ("region", "tile"))),
        check_vma=False,
    )
```

```python
import functools

import jax
import jax.numpy as jnp
from jax import lax
from jax.experimental import pallas as pl
from jax.experimental.pallas import tpu as pltpu
from jax.sharding import PartitionSpec as P

CUTOFF = 1.001
ROW_SHIFT, SKIP = 20, 1 << 19
LANES = 128
ROWS = 64
PAIR = 2
BATCH = 2 * PAIR
RING = 8
UNROLL = 4
VMEM = 16 * 1024 * 1024
HIGHEST = lax.Precision.HIGHEST


def whole_vmem(count):
    return [pl.BlockSpec(memory_space=pltpu.VMEM)] * count


def in_hbm(value):
    return pltpu.with_memory_space_constraint(value, pltpu.HBM)


def dot_nt(left, right, precision=None):
    return lax.dot_general(
        left, right, (((1,), (1,)), ((), ())), precision=precision, preferred_element_type=jnp.float32
    )


def dot_nn(left, right, precision=None):
    return lax.dot_general(
        left, right, (((1,), (0,)), ((), ())), precision=precision, preferred_element_type=jnp.float32
    )


def three_parts(value):
    high = value.astype(jnp.bfloat16)
    rest = value - high.astype(jnp.float32)
    middle = rest.astype(jnp.bfloat16)
    low = (rest - middle.astype(jnp.float32)).astype(jnp.bfloat16)
    return high, middle, low


def halves(block, axis):
    count = lax.axis_size(axis)
    block = block[None]
    bit = 1
    while 2 * bit < count:
        block = jnp.concatenate([block, swapped(block, axis, bit)], axis=0)
        bit *= 2
    return block, swapped(block, axis, bit)


def swapped(block, axis, bit):
    return lax.ppermute(block, axis, [(i, i ^ bit) for i in range(lax.axis_size(axis))])


def sum_tiles(block):
    bit = 1
    while bit < lax.axis_size("tile"):
        block = block + swapped(block, "tile", bit)
        bit *= 2
    return block


def swap_regions(block, even, odd):
    tiles = lax.axis_size("tile")
    route = [
        (region * tiles + tile, (region ^ (odd if tile % 2 else even)) * tiles + tile)
        for region in range(lax.axis_size("region"))
        for tile in range(tiles)
    ]
    return lax.ppermute(block, ("region", "tile"), route)


def sum_regions(block):
    bits, _ = region_orders(lax.axis_size("region"))
    middle = len(bits) // 2
    for even, odd in zip(bits, bits[middle:] + bits[:middle]):
        block = block + swap_regions(block, even, odd)
    return block


def region_orders(count):
    bits = []
    bit = count // 2
    while bit:
        bits.append(bit)
        bit //= 2
    return bits, bits[:1] + bits[-1:] + bits[1:-1] if len(bits) > 2 else bits[::-1]


def slot_offsets(count):
    table = []
    for bits in region_orders(count):
        offsets = [0]
        for bit in bits:
            offsets = offsets + [offset ^ bit for offset in offsets]
        table.append(offsets)
    return [jnp.array(offsets, jnp.int32) for offsets in table]


def exchange(block, *beside):
    regions = lax.axis_size("region")
    block = block[None]
    for even, odd in zip(*region_orders(regions)):
        other = swap_regions(block, even, odd)
        if 2 * block.shape[0] == regions:
            return block, other
        other, *beside = lax.optimization_barrier((other, *beside))
        block = jnp.concatenate([block, other], axis=0)


def stacked_parts(value):
    return jnp.concatenate([part.astype(jnp.float32) for part in three_parts(value)], axis=0).astype(
        jnp.bfloat16
    )


def add_parts(value):
    rows = value.shape[0] // 3
    return (value[2 * rows :] + value[rows : 2 * rows]) + value[:rows]


def fill_order(first, rank, order_ref, row, count):
    step = 64

    def fill(block, carry):
        start = pl.multiple_of(block * step, step)
        place = first + start + lax.broadcasted_iota(jnp.int32, (step, rank.shape[1]), 0)
        order_ref[pl.ds(pl.multiple_of(row + start, step), step), :] = jnp.where(
            place == rank, 1.0, 0.0
        ).astype(jnp.bfloat16)
        return carry

    lax.fori_loop(0, count // step, fill, 0)


def sort_kernel(
    first_ref, owner_ref, near_ref, far_ref, near_error_ref, far_error_ref, block_ref, other_ref,
    rounded_out, places_out, own_out, block_out, rank_out,
    order_ref, column_ref, rank_ref, owned_ref, places_ref, errors_ref, blocks_ref, sems,
):
    columns, local = block_out.shape
    half = block_ref.shape[0]
    pairs = [(owner_ref, owned_ref)]
    for sources, target in (
        ((near_ref, far_ref), places_ref),
        ((near_error_ref, far_error_ref), errors_ref),
        ((block_ref, other_ref), blocks_ref),
    ):
        pairs += [(ref, target.at[pl.ds(part * half, half)]) for part, ref in enumerate(sources)]
    copies = [
        pltpu.make_async_copy(source, target, sems.at[index])
        for index, (source, target) in enumerate(pairs)
    ]
    for copy in copies:
        copy.start()
    for copy in copies[:5]:
        copy.wait()
    places = jnp.concatenate(
        [jnp.concatenate([places_ref[i], errors_ref[i]], axis=0) for i in range(2 * half)], axis=1
    )
    n = places.shape[1]
    step = 64
    index = jnp.concatenate(
        [
            (first_ref[i] + lax.broadcasted_iota(jnp.int32, (1, local), 1)).astype(jnp.float32)
            for i in range(n // local)
        ],
        axis=1,
    )
    y_row = places[1:2, :]
    column_ref[...] = jnp.transpose(
        jnp.concatenate([y_row, index, jnp.zeros((6, n), jnp.float32)], axis=0)
    )

    def count(ties, block, total):
        start = pl.multiple_of(block * step, step)
        y_column = jnp.broadcast_to(column_ref[pl.ds(start, step), 0:1], (step, n))
        before = y_column < y_row
        if ties:
            index_column = jnp.broadcast_to(column_ref[pl.ds(start, step), 1:2], (step, n))
            before = before | ((y_column == y_row) & (index_column < index))
        return total + jnp.sum(jnp.where(before, 1.0, 0.0).reshape(step // 8, 8, n), axis=0)

    def ranks(ties):
        start = jnp.zeros((8, n), jnp.float32)
        total = lax.fori_loop(0, n // step, functools.partial(count, ties), start)
        rank_ref[...] = jnp.sum(total, axis=0, keepdims=True).astype(jnp.int32)

    ranks(False)

    @pl.when(jnp.sum(rank_ref[...]) != n * (n - 1) // 2)
    def _():
        ranks(True)

    rank = rank_ref[...]
    rank_out[...] = rank[:, :local]
    fill_order(first_ref[0], rank, order_ref, 0, local)
    for copy in copies[5:]:
        copy.wait()
    blocks = [blocks_ref[i] for i in range(2 * half)]
    everything = jnp.concatenate([jnp.concatenate(blocks, axis=1), places, jnp.zeros((4, n), jnp.float32)], axis=0)
    whole = add_parts(dot_nt(stacked_parts(everything), order_ref[...]))
    block_out[...] = whole[:columns]
    own_out[...] = whole[columns:]
    rounded_out[...] = whole[:columns].astype(jnp.bfloat16)
    lane = lax.broadcasted_iota(jnp.int32, (1, local), 1)
    flags = jnp.zeros((1, local), jnp.float32)
    for offset in range(owner_ref.shape[1]):
        flags = jnp.where((lane == offset) & (owned_ref[0, offset] >= 0), 1.0, flags)
    places_out[...] = jnp.concatenate([whole[columns : columns + 3], flags], axis=0)


def sort_region(first, tile_owner, near, far, near_error, far_error, block, other):
    local = near.shape[2]
    n = local * 2 * near.shape[0]
    columns = block.shape[1]
    smem = pl.BlockSpec(memory_space=pltpu.SMEM)
    return pl.pallas_call(
        sort_kernel,
        out_shape=(
            jax.ShapeDtypeStruct((columns, local), jnp.bfloat16),
            jax.ShapeDtypeStruct((4, local), jnp.float32),
            jax.ShapeDtypeStruct((8, local), jnp.float32),
            jax.ShapeDtypeStruct((columns, local), jnp.float32),
            jax.ShapeDtypeStruct((1, local), jnp.int32),
        ),
        in_specs=[smem] + [pl.BlockSpec(memory_space=pl.ANY)] * 7,
        out_specs=tuple(whole_vmem(5)),
        scratch_shapes=[
            pltpu.VMEM((local, n), jnp.bfloat16),
            pltpu.VMEM((n, 8), jnp.float32),
            pltpu.VMEM((1, n), jnp.int32),
            pltpu.SMEM(tile_owner.shape, jnp.int32),
            pltpu.VMEM((n // local, 3, local), jnp.float32),
            pltpu.VMEM((n // local, 1, local), jnp.float32),
            pltpu.VMEM((n // local, columns, local), jnp.float32),
            pltpu.SemaphoreType.DMA((7,)),
        ],
        compiler_params=pltpu.CompilerParams(vmem_limit_bytes=VMEM),
        cost_estimate=pl.CostEstimate(
            flops=6 * n * local * (columns + 8), bytes_accessed=4 * n * local, transcendentals=0
        ),
        name="sort_region",
    )(first, in_hbm(tile_owner), in_hbm(near), far, in_hbm(near_error), far_error, in_hbm(block), other)


def unsort_kernel(first_ref, rank_ref, block_ref, block_out, order_ref):
    n, local = order_ref.shape
    for slot in range(n // local):
        fill_order(first_ref[slot], rank_ref[...], order_ref, slot * local, local)
    block_out[...] = add_parts(dot_nn(stacked_parts(block_ref[...]), order_ref[...]))


def unsort(first, rank, block):
    n = block.shape[1]
    local = rank.shape[1]
    return pl.pallas_call(
        unsort_kernel,
        out_shape=jax.ShapeDtypeStruct((block.shape[0], local), jnp.float32),
        in_specs=[pl.BlockSpec(memory_space=pltpu.SMEM)] + whole_vmem(2),
        out_specs=whole_vmem(1)[0],
        scratch_shapes=[pltpu.VMEM((n, local), jnp.bfloat16)],
        compiler_params=pltpu.CompilerParams(vmem_limit_bytes=VMEM),
        cost_estimate=pl.CostEstimate(
            flops=6 * n * local * block.shape[0], bytes_accessed=4 * n * local, transcendentals=0
        ),
        name="unsort",
    )(first, rank, block)


def plan_blocks(
    distance_ref, listed_ref, own_ref, far_ref, chunks, stage_ref, bounds_ref, ids_ref, count_ref, sem, prepare,
):
    places, local = far_ref.shape[0], own_ref.shape[1]
    reach = listed_ref.shape[1]
    blocks = local // ROWS
    lane = lax.broadcasted_iota(jnp.int32, (1, LANES), 1)

    lowest = jnp.zeros((1, LANES), jnp.float32)
    highest = lowest
    for block in range(blocks):
        here = (lane == block) | (lane == blocks + block)
        low = own_ref[1:2, block * ROWS : block * ROWS + 1]
        high = own_ref[1:2, (block + 1) * ROWS - 1 : (block + 1) * ROWS]
        lowest = jnp.where(here, 2.0 * (low - CUTOFF), lowest)
        highest = jnp.where(here, 2.0 * (high + CUTOFF), highest)
    y = far_ref[:, 1, :]
    first = jnp.zeros((places, LANES), jnp.int32)
    beyond = first
    for chunk in range(chunks):
        low = y[:, chunk * LANES : chunk * LANES + 1]
        high = y[:, (chunk + 1) * LANES - 1 : (chunk + 1) * LANES]
        first = first + (high < lowest).astype(jnp.int32)
        beyond = beyond + (low <= highest).astype(jnp.int32)
    distance = distance_ref[...]
    flags = jnp.where((lane == -distance) & (far_ref[:, 3, :LANES] > 0.0), 1.0, 0.0)
    for offset in range(reach):
        mine = jnp.where(listed_ref[0, offset] >= 0, 1.0, 0.0)
        flags = flags + jnp.where((lane == offset) & (distance == offset), mine, 0.0)
    listed = jnp.sum(flags, axis=1, keepdims=True) > 0.0
    found = jnp.where(listed, jnp.maximum(beyond - first, 0), 0)
    stage_ref[...] = jnp.where(lane < blocks, first, found)
    copy = pltpu.make_async_copy(stage_ref, bounds_ref, sem)
    copy.start()
    prepare()
    copy.wait()

    count = jnp.int32(0)
    for block in range(blocks):

        def add_place(place, count, block=block):
            entry = (block << ROW_SHIFT) + place * chunks + bounds_ref[place, block]
            for chunk in range(chunks):
                ids_ref[count + chunk] = entry + chunk
            return count + bounds_ref[place, blocks + block]

        count = lax.fori_loop(0, places, add_place, count, unroll=8)
        for extra in range(PAIR - 1):
            ids_ref[count + extra] = (block << ROW_SHIFT) + SKIP
        count = lax.div(count + PAIR - 1, PAIR) * PAIR
    for extra in range(BATCH - PAIR):
        ids_ref[count + extra] = SKIP
    count_ref[0] = lax.div(count + BATCH - 1, BATCH)


def gaspari_cohn(squared):
    squared = jnp.maximum(squared, 1e-12)
    inverse = lax.rsqrt(squared)
    scaled = squared * inverse
    near = (((-3.0 * scaled + 6.0) * scaled + 7.5) * scaled - 20.0) * squared + 12.0
    left = jnp.maximum(2.0 - scaled, 0.0)
    left = left * left
    far = (left * left) * (((scaled + 2.0) * scaled - 0.5) * inverse)
    return jnp.where(scaled <= 1.0, near, far)


def locate(ids_ref, batch, part, chunk_bits):
    entry = ids_ref[batch * BATCH + part]
    lane = pl.multiple_of((entry & ((1 << chunk_bits) - 1)) * LANES, LANES)
    start = pl.multiple_of(lax.shift_right_logical(entry, ROW_SHIFT) * ROWS, ROWS)
    place = lax.shift_right_logical(entry & (SKIP - 1), chunk_bits)
    return (entry & SKIP) == 0, place, pl.ds(lane, LANES), pl.ds(start, ROWS)


def build_kernel(
    kept, place_ref, distance_ref, listed_ref, own_ref, near_ref, other_ref,
    ids_ref, count_ref, tiles_ref,
    wide_ref, far_ref, stage_ref, bounds_ref, bounds_sem, *through,
):
    local = own_ref.shape[1]
    places = far_ref.shape[0]
    chunk_bits = (local // LANES).bit_length() - 1
    factor = jnp.where(lax.broadcasted_iota(jnp.int32, (4, 1), 0) < 2, 2.0, 1.0 / 12.0)
    for index in range(places):
        side_ref = near_ref if 2 * index < places else other_ref
        far_ref[index, 0:4, :] = factor * side_ref[place_ref[index]]

    def prepare():
        column = jnp.transpose(own_ref[...])
        for row in range(3):
            scale = 2.0 if row < 2 else 1.0
            wide_ref[row] = jnp.broadcast_to(scale * column[:, row : row + 1], (local, LANES))

    plan_blocks(
        distance_ref, listed_ref, own_ref, far_ref, 1 << chunk_bits,
        stage_ref, bounds_ref, ids_ref, count_ref, bounds_sem, prepare,
    )
    total = count_ref[0]
    held_ref, sems = (tiles_ref, None) if kept else through

    def copy_out(batch):
        return pltpu.make_async_copy(
            held_ref.at[batch], tiles_ref.at[batch], sems.at[lax.rem(batch, RING)]
        )

    def build_batch(batch, carry):
        if not kept:

            @pl.when(batch >= RING)
            def _():
                copy_out(batch - RING).wait()

        for part in range(BATCH):
            real, place, lanes, rows = locate(ids_ref, batch, part, chunk_bits)
            far = far_ref[place, :, lanes]
            across_x = wide_ref[0, rows, :] - far[0:1, :]
            across_y = wide_ref[1, rows, :] - far[1:2, :]
            value = gaspari_cohn(across_x * across_x + across_y * across_y)
            spread = jnp.where(real, far[2:3, :], 0.0)
            value = wide_ref[2, rows, :] * spread * value
            held_ref[batch, :, part * LANES : (part + 1) * LANES] = value.astype(jnp.bfloat16)
        if not kept:
            copy_out(batch).start()
        return carry

    lax.fori_loop(0, total, build_batch, 0)
    if not kept:

        def finish(batch, carry):
            copy_out(batch).wait()
            return carry

        lax.fori_loop(jnp.maximum(total - RING, 0), total, finish, 0)


def build_tiles(place, distance, tile_owner, own, near, far, capacity, kept):
    near, far = [piece.reshape((-1,) + piece.shape[2:]) for piece in (near, far)]
    places, local = place.shape[0], own.shape[1]
    smem = pl.BlockSpec(memory_space=pltpu.SMEM)
    sizes = (capacity * BATCH + local // LANES, 1)
    shape = (capacity, ROWS, BATCH * LANES)
    scratch = [
        pltpu.VMEM((3, local, LANES), jnp.float32),
        pltpu.VMEM((places, 8, local), jnp.float32),
        pltpu.VMEM((places, LANES), jnp.int32),
        pltpu.SMEM((places, LANES), jnp.int32),
        pltpu.SemaphoreType.DMA,
    ]
    if not kept:
        scratch += [pltpu.VMEM(shape, jnp.bfloat16), pltpu.SemaphoreType.DMA((RING,))]
    return pl.pallas_call(
        functools.partial(build_kernel, kept),
        out_shape=tuple(jax.ShapeDtypeStruct((size,), jnp.int32) for size in sizes)
        + ((pltpu.VMEM if kept else pltpu.HBM)(shape, jnp.bfloat16),),
        in_specs=[smem] + whole_vmem(1) + [smem] + whole_vmem(3),
        out_specs=(smem,) * 2 + (pl.BlockSpec(memory_space=pltpu.VMEM if kept else pltpu.HBM),),
        scratch_shapes=scratch,
        compiler_params=pltpu.CompilerParams(vmem_limit_bytes=VMEM),
        cost_estimate=pl.CostEstimate(
            flops=2 * local * local * 16000, bytes_accessed=16 * local * local, transcendentals=0
        ),
        name="build_kept" if kept else "build_passed",
    )(place, distance, tile_owner, own, near, far)


def apply_kernel(started, last, grams, ids_ref, count_ref, near_ref, other_ref, tiles_ref, *refs):
    refs = list(refs)
    start_ref = refs.pop(0) if started else None
    if last:
        first_ref = refs.pop(2) if grams else None
        block_ref, scale_ref, out_ref, rounded_ref = refs[:4]
        all_ref, piece_sems, total_ref = refs[-3:]
        held_ref = tiles_ref
    else:
        total_ref, all_ref, piece_sems, held_ref, sems = refs
    half, columns, local = near_ref.shape
    chunk_bits = (local // LANES).bit_length() - 1
    total = count_ref[0]
    groups = lax.div(total + UNROLL - 1, UNROLL)

    copies = [
        pltpu.make_async_copy(ref, all_ref.at[pl.ds(part * half, half)], piece_sems.at[part])
        for part, ref in enumerate((near_ref, other_ref))
    ]
    for copy in copies:
        copy.start()

    def copy_in(group):
        first = group * UNROLL
        return pltpu.make_async_copy(
            tiles_ref.at[pl.ds(first, UNROLL)], held_ref.at[pl.ds(first, UNROLL)], sems.at[group]
        )

    if not last:

        def start_copy(group, carry):
            copy_in(group).start()
            return carry

        lax.fori_loop(0, groups, start_copy, 0)
    if started:
        total_ref[...] = start_ref[...]
    else:
        total_ref[...] = jnp.zeros(total_ref.shape, jnp.float32)
    for copy in copies:
        copy.wait()

    def turn(group, carry):
        if not last:
            copy_in(group).wait()
        values = []
        for inner in range(UNROLL):
            batch = jnp.minimum(group * UNROLL + inner, total - 1)
            valid = group * UNROLL + inner < total
            for pair in range(BATCH // PAIR):
                sides = []
                for part in range(pair * PAIR, (pair + 1) * PAIR):
                    _, place, chunk, rows = locate(ids_ref, batch, part, chunk_bits)
                    sides.append(all_ref[place, :, chunk])
                side = jnp.concatenate(sides, axis=1)
                if inner:
                    side = jnp.where(valid, side, jnp.zeros_like(side))
                lanes = slice(pair * PAIR * LANES, (pair + 1) * PAIR * LANES)
                values.append((rows, dot_nt(held_ref[batch, :, lanes], side)))
        for rows, value in values:
            total_ref[rows, :] += value
        return carry

    lax.fori_loop(0, groups, turn, 0)
    if last:
        block = block_ref[...]
        result = jnp.transpose(total_ref[...]) + scale_ref[...] * block
        out_ref[...] = result
        rounded_ref[...] = result.astype(jnp.bfloat16)
        if grams:
            refs[4][...] = jnp.concatenate([first_ref[...], packed_grams(block, result)], axis=1)


def apply_tiles(plan, near, far, tiles, start, finish):
    near, far = [piece.reshape((-1,) + piece.shape[2:]) for piece in (near, far)]
    half, columns, local = near.shape
    last = finish is not None
    grams = last and len(finish) > 2
    smem = pl.BlockSpec(memory_space=pltpu.SMEM)
    anywhere = pl.BlockSpec(memory_space=pl.ANY)
    operands = [*plan, near, far, tiles]
    in_specs = [smem] * 2 + [anywhere] * 2
    in_specs.append(pl.BlockSpec(memory_space=pltpu.VMEM if last else pltpu.HBM))
    if start is not None:
        operands.append(start)
        in_specs += whole_vmem(1)
    scratch = [
        pltpu.VMEM((2 * half, columns, local), jnp.bfloat16),
        pltpu.SemaphoreType.DMA((2,)),
    ]
    if last:
        operands += finish
        in_specs += whole_vmem(len(finish))
        out_shape = (
            jax.ShapeDtypeStruct((columns, local), jnp.float32),
            jax.ShapeDtypeStruct((columns, local), jnp.bfloat16),
        )
        if grams:
            out_shape += (jax.ShapeDtypeStruct((columns + 8, 2 * columns), jnp.float32),)
        scratch.append(pltpu.VMEM((local, columns), jnp.float32))
    else:
        out_shape = (jax.ShapeDtypeStruct((local, columns), jnp.float32),)
        scratch.append(pltpu.VMEM(tiles.shape, jnp.bfloat16))
        scratch.append(pltpu.SemaphoreType.DMA((tiles.shape[0] // UNROLL,)))
    return pl.pallas_call(
        functools.partial(apply_kernel, start is not None, last, grams),
        out_shape=out_shape,
        in_specs=in_specs,
        out_specs=tuple(whole_vmem(len(out_shape))),
        scratch_shapes=scratch,
        compiler_params=pltpu.CompilerParams(vmem_limit_bytes=VMEM),
        cost_estimate=pl.CostEstimate(
            flops=2 * local * local * 6000, bytes_accessed=16 * local * local, transcendentals=0
        ),
        name="apply_last" if last else "apply_first",
    )(*operands)


def packed_grams(left, right):
    n = left.shape[0]
    both = dot_nt(left, jnp.concatenate([left, right], axis=0), HIGHEST)
    square, mixed = both[:, :n], both[:, n:]
    mixed = 0.5 * (mixed + jnp.transpose(mixed))
    row, column = [lax.broadcasted_iota(jnp.int32, (n, n), axis) for axis in range(2)]
    diagonals = [
        jnp.sum(jnp.where(row == column, matrix, 0.0), axis=0, keepdims=True) for matrix in (square, mixed)
    ]
    rest = jnp.zeros((6, n), jnp.float32)
    return jnp.concatenate([jnp.where(row < column, square, mixed), *diagonals, rest], axis=0)


def unpacked_grams(packed):
    n = packed.shape[1]
    matrix = packed[:n]
    row, column = [lax.broadcasted_iota(jnp.int32, (n, n), axis) for axis in range(2)]
    upper = jnp.where(row < column, matrix, 0.0)
    lower = jnp.where(row > column, matrix, 0.0)
    diagonals = [jnp.where(row == column, packed[n + k : n + k + 1], 0.0) for k in range(2)]
    return upper + jnp.transpose(upper) + diagonals[0], lower + jnp.transpose(lower) + diagonals[1]


def grams_kernel(left_ref, right_ref, out_ref):
    out_ref[...] = packed_grams(left_ref[...], right_ref[...])


def first_grams(left, right):
    n = left.shape[0]
    return pl.pallas_call(
        grams_kernel,
        out_shape=jax.ShapeDtypeStruct((n + 8, n), jnp.float32),
        in_specs=whole_vmem(2),
        out_specs=whole_vmem(1)[0],
        compiler_params=pltpu.CompilerParams(vmem_limit_bytes=VMEM),
        cost_estimate=pl.CostEstimate(flops=2 * 10**9, bytes_accessed=8 * left.size, transcendentals=0),
        name="first_grams",
    )(left, right)


def reciprocal(value):
    root = lax.rsqrt(value)
    return root * root


def small_product(left, right):
    return [[sum(l * r[j] for l, r in zip(row, right)) for j in range(len(right[0]))] for row in left]


def small_difference(left, right):
    return [[l - r for l, r in zip(*rows)] for rows in zip(left, right)]


def small_inverse(matrix):
    (a, b), (c, d) = matrix
    scale = reciprocal(a * d - b * c)
    return [[d * scale, -b * scale], [-c * scale, a * scale]]


def solve_positive(matrix, target):
    n = matrix.shape[0]
    table = jnp.concatenate([0.5 * (matrix + jnp.transpose(matrix)), target], axis=1)
    bands = [table[k : k + 8, :] for k in range(0, n, 8)]
    row_index = lax.broadcasted_iota(jnp.int32, bands[0].shape, 0)
    for k in range(0, n, 4):
        own, row = k // 8, k % 8
        columns = [
            [jnp.broadcast_to(band[:, k + j : k + j + 1], band.shape) for band in bands] for j in range(4)
        ]
        pivot = [[columns[j][own][row + i : row + i + 1] for j in range(4)] for i in range(4)]
        upper, lower = pivot[:2], pivot[2:]
        top = small_inverse([r[:2] for r in upper])
        factor = small_product([r[:2] for r in lower], top)
        right = [r[2:] for r in upper]
        rest = small_inverse(small_difference([r[2:] for r in lower], small_product(factor, right)))
        rows = [[bands[own][row + i : row + i + 1]] for i in range(4)]
        last = small_product(rest, small_difference(rows[2:], small_product(factor, rows[:2])))
        first = small_product(top, small_difference(rows[:2], small_product(right, last)))
        new = [r[0] for r in first + last]
        bands = [
            band - ((columns[0][i] * new[0] + columns[1][i] * new[1]) + (columns[2][i] * new[2] + columns[3][i] * new[3]))
            for i, band in enumerate(bands)
        ]
        for i in range(4):
            bands[own] = jnp.where(row_index == row + i, new[i], bands[own])
    return jnp.concatenate([band[:, n:] for band in bands], axis=0)


def last_kernel(grams_ref, start_ref, images_ref, weights_ref, residual_ref):
    n = grams_ref.shape[1] // 2
    squares, mixed = unpacked_grams(grams_ref[:, :n])
    images, cross = unpacked_grams(grams_ref[:, n:])
    solved = solve_positive(mixed, jnp.concatenate([squares, images], axis=1))
    step, carried = solved[:, :n], solved[:, n:]
    product = dot_nn(images, solved, HIGHEST)
    second = solve_positive(cross - product[:, n:], mixed - product[:, :n])
    first = jnp.transpose(step - dot_nn(carried, second, HIGHEST))
    second = jnp.transpose(second)
    both = jnp.concatenate([first, second], axis=1)
    start, images = start_ref[...], images_ref[...]
    weights_ref[...] = dot_nn(both, jnp.concatenate([start, images[:n]], axis=0), HIGHEST)
    residual_ref[...] = start - dot_nn(both, images, HIGHEST)


def last_step(grams, start, images):
    return pl.pallas_call(
        last_kernel,
        out_shape=(jax.ShapeDtypeStruct(start.shape, jnp.float32),) * 2,
        in_specs=whole_vmem(3),
        out_specs=tuple(whole_vmem(2)),
        compiler_params=pltpu.CompilerParams(vmem_limit_bytes=VMEM),
        name="last_step",
    )(grams, start, images)


def shards(innovations, obs_geometry, obs_error, tile_owner):
    tiles_axis, regions = lax.axis_size("tile"), lax.axis_size("region")
    reach = tile_owner.shape[1]
    here, tile = lax.axis_index("region"), lax.axis_index("tile")
    columns, local = innovations.shape
    slot_tile = tile ^ jnp.arange(tiles_axis, dtype=jnp.int32)
    first = slot_tile * local
    even, odd = slot_offsets(regions)
    slot_region = here ^ jnp.where((slot_tile % 2 == 0)[:, None], even, odd)

    rounded, places, own, start, rank = sort_region(
        first,
        tile_owner,
        *halves(obs_geometry, "tile"),
        *halves(obs_error[None, :], "tile"),
        *halves(innovations, "tile"),
    )
    scale = own[3:4]
    everywhere = jnp.broadcast_to(places[None], (regions,) + places.shape)
    everywhere = lax.all_to_all(everywhere, "region", 0, 0)
    near_places, far_places = halves(everywhere, "tile")

    half_regions = regions // 2
    most = min(half_regions, 2 * reach - 1) * tiles_axis * (local // LANES)
    batches = -(-(local // ROWS) * -(-most // PAIR) * PAIR // BATCH) + 1
    capacity = -(-batches // UNROLL) * UNROLL
    stack = jnp.arange(tiles_axis, dtype=jnp.int32) % (tiles_axis // 2) * regions
    plans, tiles = [], []
    for part in range(2):
        inside = slot_region[:, part * half_regions : (part + 1) * half_regions]
        *plan, built = build_tiles(
            (stack[:, None] + inside).reshape(-1), (inside - here).reshape(-1, 1), tile_owner, own,
            near_places, far_places, capacity, part == 1,
        )
        plans.append(plan)
        tiles.append(built)

    def operate(sent, block, *grams):
        building = not grams
        total = None
        for part, group in enumerate(exchange(sent, *grams)):
            if building:
                group, plans[part] = lax.optimization_barrier((group, plans[part]))
            elif part:
                group, total = lax.optimization_barrier((group, total))
            near, far = halves(group, "tile")
            results = apply_tiles(
                plans[part], near, far, tiles[part], total, (block, scale, *grams) if part else None
            )
            total = results[0]
        return results

    image, image_rounded = operate(rounded, start)
    second, _, grams = operate(image_rounded, image, first_grams(start, image))
    grams = sum_regions(sum_tiles(grams))
    near, far = halves(jnp.concatenate([image, second], axis=0), "tile")
    images = unsort(first, rank, jnp.concatenate([*near, *far], axis=1))
    return last_step(grams, innovations, images)


def solution(mesh):
    return jax.shard_map(
        shards,
        mesh=mesh,
        in_specs=(
            P(None, ("region", "tile")),
            P(None, ("region", "tile")),
            P(("region", "tile")),
            P("region", None),
        ),
        out_specs=(P(None, ("region", "tile")), P(None, ("region", "tile"))),
        check_vma=False,
    )
```

```python
import functools

import jax
import jax.numpy as jnp
from jax import lax
from jax.experimental import pallas as pl
from jax.experimental.pallas import tpu as pltpu
from jax.sharding import PartitionSpec as P

CUTOFF = 1.001
ROW_SHIFT, SKIP = 20, 1 << 19
LANES = 128
ROWS = 64
PAIR = 2
BATCH = 2 * PAIR
UNROLL = 4
VMEM = 16 * 1024 * 1024
HIGHEST = lax.Precision.HIGHEST


def whole_vmem(count):
    return [pl.BlockSpec(memory_space=pltpu.VMEM)] * count


def in_hbm(value):
    return pltpu.with_memory_space_constraint(value, pltpu.HBM)


def dot_nt(left, right, precision=None):
    return lax.dot_general(
        left, right, (((1,), (1,)), ((), ())), precision=precision, preferred_element_type=jnp.float32
    )


def dot_nn(left, right, precision=None):
    return lax.dot_general(
        left, right, (((1,), (0,)), ((), ())), precision=precision, preferred_element_type=jnp.float32
    )


def three_parts(value):
    high = value.astype(jnp.bfloat16)
    rest = value - high.astype(jnp.float32)
    middle = rest.astype(jnp.bfloat16)
    low = (rest - middle.astype(jnp.float32)).astype(jnp.bfloat16)
    return high, middle, low


def halves(block, axis):
    count = lax.axis_size(axis)
    block = block[None]
    bit = 1
    while 2 * bit < count:
        block = jnp.concatenate([block, swapped(block, axis, bit)], axis=0)
        bit *= 2
    return block, swapped(block, axis, bit)


def swapped(block, axis, bit):
    return lax.ppermute(block, axis, [(i, i ^ bit) for i in range(lax.axis_size(axis))])


def sum_tiles(block):
    bit = 1
    while bit < lax.axis_size("tile"):
        block = block + swapped(block, "tile", bit)
        bit *= 2
    return block


def swap_regions(block, even, odd):
    tiles = lax.axis_size("tile")
    route = [
        (region * tiles + tile, (region ^ (odd if tile % 2 else even)) * tiles + tile)
        for region in range(lax.axis_size("region"))
        for tile in range(tiles)
    ]
    return lax.ppermute(block, ("region", "tile"), route)


def sum_regions(block):
    bits, _ = region_orders(lax.axis_size("region"))
    middle = len(bits) // 2
    for even, odd in zip(bits, bits[middle:] + bits[:middle]):
        block = block + swap_regions(block, even, odd)
    return block


def region_orders(count):
    bits = []
    bit = count // 2
    while bit:
        bits.append(bit)
        bit //= 2
    return bits, bits[:1] + bits[-1:] + bits[1:-1] if len(bits) > 2 else bits[::-1]


def slot_offsets(count):
    table = []
    for bits in region_orders(count):
        offsets = [0]
        for bit in bits:
            offsets = offsets + [offset ^ bit for offset in offsets]
        table.append(offsets)
    return [jnp.array(offsets, jnp.int32) for offsets in table]


def exchange(block, *beside):
    regions = lax.axis_size("region")
    block = block[None]
    for even, odd in zip(*region_orders(regions)):
        other = swap_regions(block, even, odd)
        if 2 * block.shape[0] == regions:
            return block, other
        other, *beside = lax.optimization_barrier((other, *beside))
        block = jnp.concatenate([block, other], axis=0)


def stacked_parts(value):
    return jnp.concatenate([part.astype(jnp.float32) for part in three_parts(value)], axis=0).astype(
        jnp.bfloat16
    )


def add_parts(value):
    rows = value.shape[0] // 3
    return (value[2 * rows :] + value[rows : 2 * rows]) + value[:rows]


def fill_order(first, rank, order_ref, row, count):
    step = 64

    def fill(block, carry):
        start = pl.multiple_of(block * step, step)
        place = first + start + lax.broadcasted_iota(jnp.int32, (step, rank.shape[1]), 0)
        order_ref[pl.ds(pl.multiple_of(row + start, step), step), :] = jnp.where(
            place == rank, 1.0, 0.0
        ).astype(jnp.bfloat16)
        return carry

    lax.fori_loop(0, count // step, fill, 0)


def sort_kernel(
    first_ref, owner_ref, near_ref, far_ref, near_error_ref, far_error_ref, block_ref, other_ref,
    rounded_out, places_out, own_out, block_out, rank_out,
    order_ref, column_ref, rank_ref, owned_ref, places_ref, errors_ref, blocks_ref, sems,
):
    columns, local = block_out.shape
    half = block_ref.shape[0]
    pairs = [(owner_ref, owned_ref)]
    for sources, target in (
        ((near_ref, far_ref), places_ref),
        ((near_error_ref, far_error_ref), errors_ref),
        ((block_ref, other_ref), blocks_ref),
    ):
        pairs += [(ref, target.at[pl.ds(part * half, half)]) for part, ref in enumerate(sources)]
    copies = [
        pltpu.make_async_copy(source, target, sems.at[index])
        for index, (source, target) in enumerate(pairs)
    ]
    for copy in copies:
        copy.start()
    for copy in copies[:5]:
        copy.wait()
    places = jnp.concatenate(
        [jnp.concatenate([places_ref[i], errors_ref[i]], axis=0) for i in range(2 * half)], axis=1
    )
    n = places.shape[1]
    step = 64
    index = jnp.concatenate(
        [
            (first_ref[i] + lax.broadcasted_iota(jnp.int32, (1, local), 1)).astype(jnp.float32)
            for i in range(n // local)
        ],
        axis=1,
    )
    y_row = places[1:2, :]
    column_ref[...] = jnp.transpose(
        jnp.concatenate([y_row, index, jnp.zeros((6, n), jnp.float32)], axis=0)
    )

    def count(ties, block, total):
        start = pl.multiple_of(block * step, step)
        y_column = jnp.broadcast_to(column_ref[pl.ds(start, step), 0:1], (step, n))
        before = y_column < y_row
        if ties:
            index_column = jnp.broadcast_to(column_ref[pl.ds(start, step), 1:2], (step, n))
            before = before | ((y_column == y_row) & (index_column < index))
        return total + jnp.sum(jnp.where(before, 1.0, 0.0).reshape(step // 8, 8, n), axis=0)

    def ranks(ties):
        start = jnp.zeros((8, n), jnp.float32)
        total = lax.fori_loop(0, n // step, functools.partial(count, ties), start)
        rank_ref[...] = jnp.sum(total, axis=0, keepdims=True).astype(jnp.int32)

    ranks(False)

    @pl.when(jnp.sum(rank_ref[...]) != n * (n - 1) // 2)
    def _():
        ranks(True)

    rank = rank_ref[...]
    rank_out[...] = rank[:, :local]
    fill_order(first_ref[0], rank, order_ref, 0, local)
    for copy in copies[5:]:
        copy.wait()
    block = jnp.concatenate([blocks_ref[i] for i in range(2 * half)], axis=1)
    everything = jnp.concatenate(
        [
            *[part.astype(jnp.float32) for part in three_parts(block)[:2]],
            *[part.astype(jnp.float32) for part in three_parts(places)],
            jnp.zeros((4, n), jnp.float32),
        ],
        axis=0,
    ).astype(jnp.bfloat16)
    parts = dot_nt(everything, order_ref[...])
    high, low = parts[:columns], parts[columns : 2 * columns]
    rounded_out[...] = high.astype(jnp.bfloat16)
    block_out[...] = high + low
    whole = (parts[2 * columns + 8 : 2 * columns + 12] + parts[2 * columns + 4 : 2 * columns + 8]) + parts[
        2 * columns : 2 * columns + 4
    ]
    lane = lax.broadcasted_iota(jnp.int32, (1, local), 1)
    flags = jnp.zeros((1, local), jnp.float32)
    for offset in range(owner_ref.shape[1]):
        flags = jnp.where((lane == offset) & (owned_ref[0, offset] >= 0), 1.0, flags)
    own_out[...] = jnp.concatenate([whole, flags, jnp.zeros((3, local), jnp.float32)], axis=0)
    places_out[...] = jnp.concatenate([whole[:3], flags], axis=0)


def sort_region(first, tile_owner, near, far, near_error, far_error, block, other):
    local = near.shape[2]
    n = local * 2 * near.shape[0]
    columns = block.shape[1]
    smem = pl.BlockSpec(memory_space=pltpu.SMEM)
    return pl.pallas_call(
        sort_kernel,
        out_shape=(
            jax.ShapeDtypeStruct((columns, local), jnp.bfloat16),
            jax.ShapeDtypeStruct((4, local), jnp.float32),
            jax.ShapeDtypeStruct((8, local), jnp.float32),
            jax.ShapeDtypeStruct((columns, local), jnp.float32),
            jax.ShapeDtypeStruct((1, local), jnp.int32),
        ),
        in_specs=[smem] + [pl.BlockSpec(memory_space=pl.ANY)] * 7,
        out_specs=tuple(whole_vmem(5)),
        scratch_shapes=[
            pltpu.VMEM((local, n), jnp.bfloat16),
            pltpu.VMEM((n, 8), jnp.float32),
            pltpu.VMEM((1, n), jnp.int32),
            pltpu.SMEM(tile_owner.shape, jnp.int32),
            pltpu.VMEM((n // local, 3, local), jnp.float32),
            pltpu.VMEM((n // local, 1, local), jnp.float32),
            pltpu.VMEM((n // local, columns, local), jnp.float32),
            pltpu.SemaphoreType.DMA((7,)),
        ],
        compiler_params=pltpu.CompilerParams(vmem_limit_bytes=VMEM),
        cost_estimate=pl.CostEstimate(
            flops=6 * n * local * (columns + 8), bytes_accessed=4 * n * local, transcendentals=0
        ),
        name="sort_region",
    )(first, in_hbm(tile_owner), in_hbm(near), far, in_hbm(near_error), far_error, in_hbm(block), other)


def unsort_kernel(first_ref, rank_ref, block_ref, block_out, order_ref):
    n, local = order_ref.shape
    for slot in range(n // local):
        fill_order(first_ref[slot], rank_ref[...], order_ref, slot * local, local)
    block_out[...] = add_parts(dot_nn(stacked_parts(block_ref[...]), order_ref[...]))


def unsort(first, rank, block):
    n = block.shape[1]
    local = rank.shape[1]
    return pl.pallas_call(
        unsort_kernel,
        out_shape=jax.ShapeDtypeStruct((block.shape[0], local), jnp.float32),
        in_specs=[pl.BlockSpec(memory_space=pltpu.SMEM)] + whole_vmem(2),
        out_specs=whole_vmem(1)[0],
        scratch_shapes=[pltpu.VMEM((n, local), jnp.bfloat16)],
        compiler_params=pltpu.CompilerParams(vmem_limit_bytes=VMEM),
        cost_estimate=pl.CostEstimate(
            flops=6 * n * local * block.shape[0], bytes_accessed=4 * n * local, transcendentals=0
        ),
        name="unsort",
    )(first, rank, block)


def plan_blocks(
    distance_ref, own_ref, far_ref, chunks, stage_ref, bounds_ref, ids_ref, count_ref, sem, prepare,
):
    places, local = far_ref.shape[0], own_ref.shape[1]
    blocks = local // ROWS
    lane = lax.broadcasted_iota(jnp.int32, (1, LANES), 1)

    lowest = jnp.zeros((1, LANES), jnp.float32)
    highest = lowest
    for block in range(blocks):
        here = (lane == block) | (lane == blocks + block)
        low = own_ref[1:2, block * ROWS : block * ROWS + 1]
        high = own_ref[1:2, (block + 1) * ROWS - 1 : (block + 1) * ROWS]
        lowest = jnp.where(here, 2.0 * (low - CUTOFF), lowest)
        highest = jnp.where(here, 2.0 * (high + CUTOFF), highest)
    y = far_ref[:, 1, :]
    first = jnp.zeros((places, LANES), jnp.int32)
    beyond = first
    for chunk in range(chunks):
        low = y[:, chunk * LANES : chunk * LANES + 1]
        high = y[:, (chunk + 1) * LANES - 1 : (chunk + 1) * LANES]
        first = first + (high < lowest).astype(jnp.int32)
        beyond = beyond + (low <= highest).astype(jnp.int32)
    distance = distance_ref[...]
    flags = jnp.where((lane == -distance) & (far_ref[:, 3, :LANES] > 0.0), 1.0, 0.0)
    flags = flags + jnp.where(lane == distance, own_ref[4:5, :LANES], 0.0)
    listed = jnp.sum(flags, axis=1, keepdims=True) > 0.0
    found = jnp.where(listed, jnp.maximum(beyond - first, 0), 0)
    stage_ref[...] = jnp.where(lane < blocks, first, found)
    copy = pltpu.make_async_copy(stage_ref, bounds_ref, sem)
    copy.start()
    prepare()
    copy.wait()

    count = jnp.int32(0)
    for block in range(blocks):

        def add_place(place, count, block=block):
            entry = (block << ROW_SHIFT) + place * chunks + bounds_ref[place, block]
            for chunk in range(chunks):
                ids_ref[count + chunk] = entry + chunk
            return count + bounds_ref[place, blocks + block]

        count = lax.fori_loop(0, places, add_place, count, unroll=8)
        for extra in range(PAIR - 1):
            ids_ref[count + extra] = (block << ROW_SHIFT) + SKIP
        count = lax.div(count + PAIR - 1, PAIR) * PAIR
    for extra in range(BATCH - PAIR):
        ids_ref[count + extra] = SKIP
    count_ref[0] = lax.div(count + BATCH - 1, BATCH)


def gaspari_cohn(squared):
    squared = jnp.maximum(squared, 1e-12)
    inverse = lax.rsqrt(squared)
    scaled = squared * inverse
    near = (((-3.0 * scaled + 6.0) * scaled + 7.5) * scaled - 20.0) * squared + 12.0
    left = jnp.maximum(2.0 - scaled, 0.0)
    left = left * left
    far = (left * left) * (((scaled + 2.0) * scaled - 0.5) * inverse)
    return jnp.where(scaled <= 1.0, near, far)


def locate(ids_ref, batch, part, chunk_bits):
    entry = ids_ref[batch * BATCH + part]
    lane = pl.multiple_of((entry & ((1 << chunk_bits) - 1)) * LANES, LANES)
    start = pl.multiple_of(lax.shift_right_logical(entry, ROW_SHIFT) * ROWS, ROWS)
    place = lax.shift_right_logical(entry & (SKIP - 1), chunk_bits)
    return (entry & SKIP) == 0, place, pl.ds(lane, LANES), pl.ds(start, ROWS)


def build_kernel(
    place_ref, distance_ref, own_ref, near_ref, other_ref,
    ids_ref, count_ref, tiles_ref,
    wide_ref, far_ref, stage_ref, bounds_ref, bounds_sem,
):
    local = own_ref.shape[1]
    places = far_ref.shape[0]
    chunk_bits = (local // LANES).bit_length() - 1
    factor = jnp.where(lax.broadcasted_iota(jnp.int32, (4, 1), 0) < 2, 2.0, 1.0 / 12.0)
    for index in range(places):
        side_ref = near_ref if 2 * index < places else other_ref
        far_ref[index, 0:4, :] = factor * side_ref[place_ref[index]]

    def prepare():
        column = jnp.transpose(own_ref[...])
        for row in range(3):
            scale = 2.0 if row < 2 else 1.0
            wide_ref[row] = jnp.broadcast_to(scale * column[:, row : row + 1], (local, LANES))

    plan_blocks(
        distance_ref, own_ref, far_ref, 1 << chunk_bits,
        stage_ref, bounds_ref, ids_ref, count_ref, bounds_sem, prepare,
    )
    total = count_ref[0]

    def build_batch(batch, carry):
        for part in range(BATCH):
            real, place, lanes, rows = locate(ids_ref, batch, part, chunk_bits)
            far = far_ref[place, :, lanes]
            across_x = wide_ref[0, rows, :] - far[0:1, :]
            across_y = wide_ref[1, rows, :] - far[1:2, :]
            value = gaspari_cohn(across_x * across_x + across_y * across_y)
            spread = jnp.where(real, far[2:3, :], 0.0)
            value = wide_ref[2, rows, :] * spread * value
            tiles_ref[batch, :, part * LANES : (part + 1) * LANES] = value.astype(jnp.bfloat16)
        return carry

    lax.fori_loop(0, total, build_batch, 0)


def build_tiles(place, distance, own, near, far, capacity):
    near, far = [piece.reshape((-1,) + piece.shape[2:]) for piece in (near, far)]
    places, local = place.shape[0], own.shape[1]
    smem = pl.BlockSpec(memory_space=pltpu.SMEM)
    sizes = (capacity * BATCH + local // LANES, 1)
    shape = (capacity, ROWS, BATCH * LANES)
    scratch = [
        pltpu.VMEM((3, local, LANES), jnp.float32),
        pltpu.VMEM((places, 8, local), jnp.float32),
        pltpu.VMEM((places, LANES), jnp.int32),
        pltpu.SMEM((places, LANES), jnp.int32),
        pltpu.SemaphoreType.DMA,
    ]
    return pl.pallas_call(
        build_kernel,
        out_shape=tuple(jax.ShapeDtypeStruct((size,), jnp.int32) for size in sizes)
        + (pltpu.VMEM(shape, jnp.bfloat16),),
        in_specs=[smem] + whole_vmem(4),
        out_specs=(smem,) * 2 + (pl.BlockSpec(memory_space=pltpu.VMEM),),
        scratch_shapes=scratch,
        compiler_params=pltpu.CompilerParams(vmem_limit_bytes=VMEM),
        cost_estimate=pl.CostEstimate(
            flops=2 * local * local * 16000, bytes_accessed=16 * local * local, transcendentals=0
        ),
        name="build_tiles",
    )(place, distance, own, near, far)


def apply_kernel(started, last, grams, ids_ref, count_ref, near_ref, other_ref, tiles_ref, *refs):
    refs = list(refs)
    start_ref = refs.pop(0) if started else None
    if last:
        first_ref = refs.pop(2) if grams else None
        block_ref, scale_ref, out_ref, rounded_ref = refs[:4]
        total_ref = refs[-1]
    else:
        (total_ref,) = refs
    half, columns, local = near_ref.shape
    chunk_bits = (local // LANES).bit_length() - 1
    total = count_ref[0]
    groups = lax.div(total + UNROLL - 1, UNROLL)

    if started:
        total_ref[...] = start_ref[...]
    else:
        total_ref[...] = jnp.zeros(total_ref.shape, jnp.float32)

    def turn(group, carry):
        values = []
        for inner in range(UNROLL):
            batch = jnp.minimum(group * UNROLL + inner, total - 1)
            valid = group * UNROLL + inner < total
            for pair in range(BATCH // PAIR):
                sides = []
                for part in range(pair * PAIR, (pair + 1) * PAIR):
                    _, place, chunk, rows = locate(ids_ref, batch, part, chunk_bits)
                    inside = jnp.where(place < half, place, place - half)
                    sides.append(
                        jnp.where(place < half, near_ref[inside, :, chunk], other_ref[inside, :, chunk])
                    )
                side = jnp.concatenate(sides, axis=1)
                if inner:
                    side = jnp.where(valid, side, jnp.zeros_like(side))
                lanes = slice(pair * PAIR * LANES, (pair + 1) * PAIR * LANES)
                values.append((rows, dot_nt(tiles_ref[batch, :, lanes], side)))
        for rows, value in values:
            total_ref[rows, :] += value
        return carry

    lax.fori_loop(0, groups, turn, 0)
    if last:
        block = block_ref[...]
        result = jnp.transpose(total_ref[...]) + scale_ref[...] * block
        out_ref[...] = result
        rounded_ref[...] = result.astype(jnp.bfloat16)
        if grams:
            refs[4][...] = jnp.concatenate([first_ref[...], packed_grams(block, result)], axis=1)


def apply_tiles(plan, near, far, tiles, start, finish):
    near, far = [piece.reshape((-1,) + piece.shape[2:]) for piece in (near, far)]
    half, columns, local = near.shape
    last = finish is not None
    grams = last and len(finish) > 2
    smem = pl.BlockSpec(memory_space=pltpu.SMEM)
    operands = [*plan, near, far, tiles]
    in_specs = [smem] * 2 + whole_vmem(3)
    if start is not None:
        operands.append(start)
        in_specs += whole_vmem(1)
    scratch = []
    if last:
        operands += finish
        in_specs += whole_vmem(len(finish))
        out_shape = (
            jax.ShapeDtypeStruct((columns, local), jnp.float32),
            jax.ShapeDtypeStruct((columns, local), jnp.bfloat16),
        )
        if grams:
            out_shape += (jax.ShapeDtypeStruct((columns + 8, 2 * columns), jnp.float32),)
        scratch.append(pltpu.VMEM((local, columns), jnp.float32))
    else:
        out_shape = (jax.ShapeDtypeStruct((local, columns), jnp.float32),)
    return pl.pallas_call(
        functools.partial(apply_kernel, start is not None, last, grams),
        out_shape=out_shape,
        in_specs=in_specs,
        out_specs=tuple(whole_vmem(len(out_shape))),
        scratch_shapes=scratch,
        compiler_params=pltpu.CompilerParams(vmem_limit_bytes=VMEM),
        cost_estimate=pl.CostEstimate(
            flops=2 * local * local * 6000, bytes_accessed=16 * local * local, transcendentals=0
        ),
        name="apply_last" if last else "apply_first",
    )(*operands)


def packed_grams(left, right):
    n = left.shape[0]
    both = dot_nt(left, jnp.concatenate([left, right], axis=0), HIGHEST)
    square, mixed = both[:, :n], both[:, n:]
    mixed = 0.5 * (mixed + jnp.transpose(mixed))
    row, column = [lax.broadcasted_iota(jnp.int32, (n, n), axis) for axis in range(2)]
    diagonals = [
        jnp.sum(jnp.where(row == column, matrix, 0.0), axis=0, keepdims=True) for matrix in (square, mixed)
    ]
    rest = jnp.zeros((6, n), jnp.float32)
    return jnp.concatenate([jnp.where(row < column, square, mixed), *diagonals, rest], axis=0)


def unpacked_grams(packed):
    n = packed.shape[1]
    matrix = packed[:n]
    row, column = [lax.broadcasted_iota(jnp.int32, (n, n), axis) for axis in range(2)]
    upper = jnp.where(row < column, matrix, 0.0)
    lower = jnp.where(row > column, matrix, 0.0)
    diagonals = [jnp.where(row == column, packed[n + k : n + k + 1], 0.0) for k in range(2)]
    return upper + jnp.transpose(upper) + diagonals[0], lower + jnp.transpose(lower) + diagonals[1]


def grams_kernel(left_ref, right_ref, out_ref):
    out_ref[...] = packed_grams(left_ref[...], right_ref[...])


def first_grams(left, right):
    n = left.shape[0]
    return pl.pallas_call(
        grams_kernel,
        out_shape=jax.ShapeDtypeStruct((n + 8, n), jnp.float32),
        in_specs=whole_vmem(2),
        out_specs=whole_vmem(1)[0],
        compiler_params=pltpu.CompilerParams(vmem_limit_bytes=VMEM),
        cost_estimate=pl.CostEstimate(flops=2 * 10**9, bytes_accessed=8 * left.size, transcendentals=0),
        name="first_grams",
    )(left, right)


def reciprocal(value):
    root = lax.rsqrt(value)
    return root * root


def small_product(left, right):
    return [[sum(l * r[j] for l, r in zip(row, right)) for j in range(len(right[0]))] for row in left]


def small_difference(left, right):
    return [[l - r for l, r in zip(*rows)] for rows in zip(left, right)]


def small_inverse(matrix):
    (a, b), (c, d) = matrix
    scale = reciprocal(a * d - b * c)
    return [[d * scale, -b * scale], [-c * scale, a * scale]]


def solve_positive(matrix, target):
    n = matrix.shape[0]
    table = jnp.concatenate([0.5 * (matrix + jnp.transpose(matrix)), target], axis=1)
    bands = [table[k : k + 8, :] for k in range(0, n, 8)]
    row_index = lax.broadcasted_iota(jnp.int32, bands[0].shape, 0)
    for k in range(0, n, 4):
        own, row = k // 8, k % 8
        columns = [
            [jnp.broadcast_to(band[:, k + j : k + j + 1], band.shape) for band in bands] for j in range(4)
        ]
        pivot = [[columns[j][own][row + i : row + i + 1] for j in range(4)] for i in range(4)]
        upper, lower = pivot[:2], pivot[2:]
        top = small_inverse([r[:2] for r in upper])
        factor = small_product([r[:2] for r in lower], top)
        right = [r[2:] for r in upper]
        rest = small_inverse(small_difference([r[2:] for r in lower], small_product(factor, right)))
        rows = [[bands[own][row + i : row + i + 1]] for i in range(4)]
        last = small_product(rest, small_difference(rows[2:], small_product(factor, rows[:2])))
        first = small_product(top, small_difference(rows[:2], small_product(right, last)))
        new = [r[0] for r in first + last]
        bands = [
            band - ((columns[0][i] * new[0] + columns[1][i] * new[1]) + (columns[2][i] * new[2] + columns[3][i] * new[3]))
            for i, band in enumerate(bands)
        ]
        for i in range(4):
            bands[own] = jnp.where(row_index == row + i, new[i], bands[own])
    return jnp.concatenate([band[:, n:] for band in bands], axis=0)


def last_kernel(grams_ref, start_ref, images_ref, weights_ref, residual_ref):
    n = grams_ref.shape[1] // 2
    squares, mixed = unpacked_grams(grams_ref[:, :n])
    images, cross = unpacked_grams(grams_ref[:, n:])
    solved = solve_positive(mixed, jnp.concatenate([squares, images], axis=1))
    step, carried = solved[:, :n], solved[:, n:]
    product = dot_nn(images, solved, HIGHEST)
    second = solve_positive(cross - product[:, n:], mixed - product[:, :n])
    first = jnp.transpose(step - dot_nn(carried, second, HIGHEST))
    second = jnp.transpose(second)
    both = jnp.concatenate([first, second], axis=1)
    start, images = start_ref[...], images_ref[...]
    weights_ref[...] = dot_nn(both, jnp.concatenate([start, images[:n]], axis=0), HIGHEST)
    residual_ref[...] = start - dot_nn(both, images, HIGHEST)


def last_step(grams, start, images):
    return pl.pallas_call(
        last_kernel,
        out_shape=(jax.ShapeDtypeStruct(start.shape, jnp.float32),) * 2,
        in_specs=whole_vmem(3),
        out_specs=tuple(whole_vmem(2)),
        compiler_params=pltpu.CompilerParams(vmem_limit_bytes=VMEM),
        name="last_step",
    )(grams, start, images)


def shards(innovations, obs_geometry, obs_error, tile_owner):
    tiles_axis, regions = lax.axis_size("tile"), lax.axis_size("region")
    reach = tile_owner.shape[1]
    here, tile = lax.axis_index("region"), lax.axis_index("tile")
    columns, local = innovations.shape
    slot_tile = tile ^ jnp.arange(tiles_axis, dtype=jnp.int32)
    first = slot_tile * local
    even, odd = slot_offsets(regions)
    slot_region = here ^ jnp.where((slot_tile % 2 == 0)[:, None], even, odd)

    rounded, places, own, start, rank = sort_region(
        first,
        tile_owner,
        *halves(obs_geometry, "tile"),
        *halves(obs_error[None, :], "tile"),
        *halves(innovations, "tile"),
    )
    scale = own[3:4]
    everywhere = jnp.broadcast_to(places[None], (regions,) + places.shape)
    everywhere = lax.all_to_all(everywhere, "region", 0, 0)
    near_places, far_places = halves(everywhere, "tile")

    half_regions = regions // 2
    most = min(half_regions, 2 * reach - 1) * tiles_axis * (local // LANES)
    batches = -(-(local // ROWS) * -(-most // PAIR) * PAIR // BATCH) + 1
    capacity = -(-batches // UNROLL) * UNROLL
    stack = jnp.arange(tiles_axis, dtype=jnp.int32) % (tiles_axis // 2) * regions
    plans, tiles = [], []
    for part in range(2):
        inside = slot_region[:, part * half_regions : (part + 1) * half_regions]
        *plan, built = build_tiles(
            (stack[:, None] + inside).reshape(-1), (inside - here).reshape(-1, 1), own,
            near_places, far_places, capacity,
        )
        plans.append(plan)
        tiles.append(built)

    def operate(sent, block, *grams):
        building = not grams
        total = None
        for part, group in enumerate(exchange(sent, *grams)):
            if building:
                group, plans[part] = lax.optimization_barrier((group, plans[part]))
            elif part:
                group, total = lax.optimization_barrier((group, total))
            near, far = halves(group, "tile")
            results = apply_tiles(
                plans[part], near, far, tiles[part], total, (block, scale, *grams) if part else None
            )
            total = results[0]
        return results

    image, image_rounded = operate(rounded, start)
    second, _, grams = operate(image_rounded, image, first_grams(start, image))
    grams = sum_regions(sum_tiles(grams))
    near, far = halves(jnp.concatenate([image, second], axis=0), "tile")
    images = unsort(first, rank, jnp.concatenate([*near, *far], axis=1))
    return last_step(grams, innovations, images)


def solution(mesh):
    return jax.shard_map(
        shards,
        mesh=mesh,
        in_specs=(
            P(None, ("region", "tile")),
            P(None, ("region", "tile")),
            P(("region", "tile")),
            P("region", None),
        ),
        out_specs=(P(None, ("region", "tile")), P(None, ("region", "tile"))),
        check_vma=False,
    )
```

```python
import functools

import jax
import jax.numpy as jnp
from jax import lax
from jax.experimental import pallas as pl
from jax.experimental.pallas import tpu as pltpu
from jax.sharding import PartitionSpec as P

CUTOFF = 1.001
ROW_SHIFT, SKIP = 20, 1 << 19
LANES = 128
ROWS = 64
PAIR = 2
BATCH = 2 * PAIR
UNROLL = 8
VMEM = 16 * 1024 * 1024
HIGHEST = lax.Precision.HIGHEST


def whole_vmem(count):
    return [pl.BlockSpec(memory_space=pltpu.VMEM)] * count


def in_hbm(value):
    return pltpu.with_memory_space_constraint(value, pltpu.HBM)


def dot_nt(left, right, precision=None):
    return lax.dot_general(
        left, right, (((1,), (1,)), ((), ())), precision=precision, preferred_element_type=jnp.float32
    )


def dot_nn(left, right, precision=None):
    return lax.dot_general(
        left, right, (((1,), (0,)), ((), ())), precision=precision, preferred_element_type=jnp.float32
    )


def three_parts(value):
    high = value.astype(jnp.bfloat16)
    rest = value - high.astype(jnp.float32)
    middle = rest.astype(jnp.bfloat16)
    low = (rest - middle.astype(jnp.float32)).astype(jnp.bfloat16)
    return high, middle, low


def halves(block, axis):
    count = lax.axis_size(axis)
    block = block[None]
    bit = 1
    while 2 * bit < count:
        block = jnp.concatenate([block, swapped(block, axis, bit)], axis=0)
        bit *= 2
    return block, swapped(block, axis, bit)


def swapped(block, axis, bit):
    return lax.ppermute(block, axis, [(i, i ^ bit) for i in range(lax.axis_size(axis))])


def sum_tiles(block):
    bit = 1
    while bit < lax.axis_size("tile"):
        block = block + swapped(block, "tile", bit)
        bit *= 2
    return block


def swap_regions(block, even, odd):
    tiles = lax.axis_size("tile")
    route = [
        (region * tiles + tile, (region ^ (odd if tile % 2 else even)) * tiles + tile)
        for region in range(lax.axis_size("region"))
        for tile in range(tiles)
    ]
    return lax.ppermute(block, ("region", "tile"), route)


def sum_regions(block):
    bits, _ = region_orders(lax.axis_size("region"))
    middle = len(bits) // 2
    for even, odd in zip(bits, bits[middle:] + bits[:middle]):
        block = block + swap_regions(block, even, odd)
    return block


def region_orders(count):
    bits = []
    bit = count // 2
    while bit:
        bits.append(bit)
        bit //= 2
    return bits, bits[:1] + bits[-1:] + bits[1:-1] if len(bits) > 2 else bits[::-1]


def slot_offsets(count):
    table = []
    for bits in region_orders(count):
        offsets = [0]
        for bit in bits:
            offsets = offsets + [offset ^ bit for offset in offsets]
        table.append(offsets)
    return table


def exchange(block, *beside):
    regions = lax.axis_size("region")
    block = block[None]
    for even, odd in zip(*region_orders(regions)):
        other = swap_regions(block, even, odd)
        if 2 * block.shape[0] == regions:
            return block, other
        other, *beside = lax.optimization_barrier((other, *beside))
        block = jnp.concatenate([block, other], axis=0)


def stacked_parts(value):
    return jnp.concatenate([part.astype(jnp.float32) for part in three_parts(value)], axis=0).astype(
        jnp.bfloat16
    )


def add_parts(value):
    rows = value.shape[0] // 3
    return (value[2 * rows :] + value[rows : 2 * rows]) + value[:rows]


def fill_order(first, rank, order_ref, row, count):
    step = 64

    def fill(block, carry):
        start = pl.multiple_of(block * step, step)
        place = first + start + lax.broadcasted_iota(jnp.int32, (step, rank.shape[1]), 0)
        order_ref[pl.ds(pl.multiple_of(row + start, step), step), :] = jnp.where(
            place == rank, 1.0, 0.0
        ).astype(jnp.bfloat16)
        return carry

    lax.fori_loop(0, count // step, fill, 0)


def sort_kernel(
    device_ref, owner_ref, near_ref, far_ref, near_error_ref, far_error_ref, block_ref, other_ref,
    rounded_out, places_out, own_out, block_out, rank_out,
    order_ref, column_ref, rank_ref, owned_ref, places_ref, errors_ref, blocks_ref, sems,
):
    columns, local = block_out.shape
    half = block_ref.shape[0]
    tile = lax.rem(device_ref[0], 2 * half)
    pairs = [(owner_ref, owned_ref)]
    for sources, target in (
        ((near_ref, far_ref), places_ref),
        ((near_error_ref, far_error_ref), errors_ref),
        ((block_ref, other_ref), blocks_ref),
    ):
        pairs += [(ref, target.at[pl.ds(part * half, half)]) for part, ref in enumerate(sources)]
    copies = [
        pltpu.make_async_copy(source, target, sems.at[index])
        for index, (source, target) in enumerate(pairs)
    ]
    for copy in copies:
        copy.start()
    for copy in copies[:5]:
        copy.wait()
    places = jnp.concatenate(
        [jnp.concatenate([places_ref[i], errors_ref[i]], axis=0) for i in range(2 * half)], axis=1
    )
    n = places.shape[1]
    step = 64
    index = jnp.concatenate(
        [
            ((tile ^ i) * local + lax.broadcasted_iota(jnp.int32, (1, local), 1)).astype(jnp.float32)
            for i in range(n // local)
        ],
        axis=1,
    )
    y_row = places[1:2, :]
    column_ref[...] = jnp.transpose(
        jnp.concatenate([y_row, index, jnp.zeros((6, n), jnp.float32)], axis=0)
    )

    def count(ties, block, total):
        start = pl.multiple_of(block * step, step)
        y_column = jnp.broadcast_to(column_ref[pl.ds(start, step), 0:1], (step, n))
        before = y_column < y_row
        if ties:
            index_column = jnp.broadcast_to(column_ref[pl.ds(start, step), 1:2], (step, n))
            before = before | ((y_column == y_row) & (index_column < index))
        return total + jnp.sum(jnp.where(before, 1.0, 0.0).reshape(step // 8, 8, n), axis=0)

    def ranks(ties):
        start = jnp.zeros((8, n), jnp.float32)
        total = lax.fori_loop(0, n // step, functools.partial(count, ties), start)
        rank_ref[...] = jnp.sum(total, axis=0, keepdims=True).astype(jnp.int32)

    ranks(False)

    @pl.when(jnp.sum(rank_ref[...]) != n * (n - 1) // 2)
    def _():
        ranks(True)

    rank = rank_ref[...]
    rank_out[...] = rank[:, :local]
    fill_order(tile * local, rank, order_ref, 0, local)
    for copy in copies[5:]:
        copy.wait()
    block = jnp.concatenate([blocks_ref[i] for i in range(2 * half)], axis=1)
    everything = jnp.concatenate(
        [
            *[part.astype(jnp.float32) for part in three_parts(block)[:2]],
            *[part.astype(jnp.float32) for part in three_parts(places)],
            jnp.zeros((4, n), jnp.float32),
        ],
        axis=0,
    ).astype(jnp.bfloat16)
    parts = dot_nt(everything, order_ref[...])
    high, low = parts[:columns], parts[columns : 2 * columns]
    rounded_out[...] = high.astype(jnp.bfloat16)
    block_out[...] = high + low
    whole = (parts[2 * columns + 8 : 2 * columns + 12] + parts[2 * columns + 4 : 2 * columns + 8]) + parts[
        2 * columns : 2 * columns + 4
    ]
    lane = lax.broadcasted_iota(jnp.int32, (1, local), 1)
    flags = jnp.zeros((1, local), jnp.float32)
    for offset in range(owner_ref.shape[1]):
        flags = jnp.where((lane == offset) & (owned_ref[0, offset] >= 0), 1.0, flags)
    own_out[...] = jnp.concatenate([whole, flags, jnp.zeros((3, local), jnp.float32)], axis=0)
    places_out[...] = jnp.concatenate([whole[:3], flags], axis=0)


def sort_region(device, tile_owner, near, far, near_error, far_error, block, other):
    local = near.shape[2]
    n = local * 2 * near.shape[0]
    columns = block.shape[1]
    smem = pl.BlockSpec(memory_space=pltpu.SMEM)
    return pl.pallas_call(
        sort_kernel,
        out_shape=(
            jax.ShapeDtypeStruct((columns, local), jnp.bfloat16),
            jax.ShapeDtypeStruct((4, local), jnp.float32),
            jax.ShapeDtypeStruct((8, local), jnp.float32),
            jax.ShapeDtypeStruct((columns, local), jnp.float32),
            jax.ShapeDtypeStruct((1, local), jnp.int32),
        ),
        in_specs=[smem] + [pl.BlockSpec(memory_space=pl.ANY)] * 7,
        out_specs=tuple(whole_vmem(5)),
        scratch_shapes=[
            pltpu.VMEM((local, n), jnp.bfloat16),
            pltpu.VMEM((n, 8), jnp.float32),
            pltpu.VMEM((1, n), jnp.int32),
            pltpu.SMEM(tile_owner.shape, jnp.int32),
            pltpu.VMEM((n // local, 3, local), jnp.float32),
            pltpu.VMEM((n // local, 1, local), jnp.float32),
            pltpu.VMEM((n // local, columns, local), jnp.float32),
            pltpu.SemaphoreType.DMA((7,)),
        ],
        compiler_params=pltpu.CompilerParams(vmem_limit_bytes=VMEM),
        cost_estimate=pl.CostEstimate(
            flops=6 * n * local * (columns + 8), bytes_accessed=4 * n * local, transcendentals=0
        ),
        name="sort_region",
    )(device, in_hbm(tile_owner), in_hbm(near), far, in_hbm(near_error), far_error, in_hbm(block), other)


def unsort_kernel(device_ref, rank_ref, block_ref, block_out, order_ref):
    n, local = order_ref.shape
    tile = lax.rem(device_ref[0], n // local)
    for slot in range(n // local):
        fill_order((tile ^ slot) * local, rank_ref[...], order_ref, slot * local, local)
    block_out[...] = add_parts(dot_nn(stacked_parts(block_ref[...]), order_ref[...]))


def unsort(device, rank, block):
    n = block.shape[1]
    local = rank.shape[1]
    return pl.pallas_call(
        unsort_kernel,
        out_shape=jax.ShapeDtypeStruct((block.shape[0], local), jnp.float32),
        in_specs=[pl.BlockSpec(memory_space=pltpu.SMEM)] + whole_vmem(2),
        out_specs=whole_vmem(1)[0],
        scratch_shapes=[pltpu.VMEM((n, local), jnp.bfloat16)],
        compiler_params=pltpu.CompilerParams(vmem_limit_bytes=VMEM),
        cost_estimate=pl.CostEstimate(
            flops=6 * n * local * block.shape[0], bytes_accessed=4 * n * local, transcendentals=0
        ),
        name="unsort",
    )(device, rank, block)


def plan_blocks(
    distance_ref, own_ref, far_ref, chunks, stage_ref, bounds_ref, ids_ref, count_ref, sem, prepare,
):
    places, local = far_ref.shape[0], own_ref.shape[1]
    blocks = local // ROWS
    lane = lax.broadcasted_iota(jnp.int32, (1, LANES), 1)

    lowest = jnp.zeros((1, LANES), jnp.float32)
    highest = lowest
    for block in range(blocks):
        here = (lane == block) | (lane == blocks + block)
        low = own_ref[1:2, block * ROWS : block * ROWS + 1]
        high = own_ref[1:2, (block + 1) * ROWS - 1 : (block + 1) * ROWS]
        lowest = jnp.where(here, 2.0 * (low - CUTOFF), lowest)
        highest = jnp.where(here, 2.0 * (high + CUTOFF), highest)
    y = far_ref[:, 1, :]
    first = jnp.zeros((places, LANES), jnp.int32)
    beyond = first
    for chunk in range(chunks):
        low = y[:, chunk * LANES : chunk * LANES + 1]
        high = y[:, (chunk + 1) * LANES - 1 : (chunk + 1) * LANES]
        first = first + (high < lowest).astype(jnp.int32)
        beyond = beyond + (low <= highest).astype(jnp.int32)
    distance = distance_ref[...]
    flags = jnp.where((lane == -distance) & (far_ref[:, 3, :LANES] > 0.0), 1.0, 0.0)
    flags = flags + jnp.where(lane == distance, own_ref[4:5, :LANES], 0.0)
    listed = jnp.sum(flags, axis=1, keepdims=True) > 0.0
    found = jnp.where(listed, jnp.maximum(beyond - first, 0), 0)
    stage_ref[...] = jnp.where(lane < blocks, first, found)
    copy = pltpu.make_async_copy(stage_ref, bounds_ref, sem)
    copy.start()
    prepare()
    copy.wait()

    count = jnp.int32(0)
    for block in range(blocks):

        def add_place(place, count, block=block):
            entry = (block << ROW_SHIFT) + place * chunks + bounds_ref[place, block]
            for chunk in range(chunks):
                ids_ref[count + chunk] = entry + chunk
            return count + bounds_ref[place, blocks + block]

        count = lax.fori_loop(0, places, add_place, count, unroll=8)
        for extra in range(PAIR - 1):
            ids_ref[count + extra] = (block << ROW_SHIFT) + SKIP
        count = lax.div(count + PAIR - 1, PAIR) * PAIR
    for extra in range(BATCH - PAIR):
        ids_ref[count + extra] = SKIP
    count_ref[0] = lax.div(count + BATCH - 1, BATCH)


def gaspari_cohn(squared):
    squared = jnp.maximum(squared, 1e-12)
    inverse = lax.rsqrt(squared)
    scaled = squared * inverse
    near = (((-3.0 * scaled + 6.0) * scaled + 7.5) * scaled - 20.0) * squared + 12.0
    left = jnp.maximum(2.0 - scaled, 0.0)
    left = left * left
    far = (left * left) * (((scaled + 2.0) * scaled - 0.5) * inverse)
    return jnp.where(scaled <= 1.0, near, far)


def locate(ids_ref, batch, part, chunk_bits):
    entry = ids_ref[batch * BATCH + part]
    lane = pl.multiple_of((entry & ((1 << chunk_bits) - 1)) * LANES, LANES)
    start = pl.multiple_of(lax.shift_right_logical(entry, ROW_SHIFT) * ROWS, ROWS)
    place = lax.shift_right_logical(entry & (SKIP - 1), chunk_bits)
    return (entry & SKIP) == 0, place, pl.ds(lane, LANES), pl.ds(start, ROWS)


def build_kernel(
    part, device_ref, own_ref, near_ref, other_ref,
    ids_ref, count_ref, tiles_ref,
    wide_ref, far_ref, stage_ref, bounds_ref, bounds_sem, distance_ref,
):
    local = own_ref.shape[1]
    places = far_ref.shape[0]
    chunk_bits = (local // LANES).bit_length() - 1
    factor = jnp.where(lax.broadcasted_iota(jnp.int32, (4, 1), 0) < 2, 2.0, 1.0 / 12.0)
    tiles, regions = 2 * near_ref.shape[0], near_ref.shape[1]
    here, tile = lax.div(device_ref[0], tiles), lax.rem(device_ref[0], tiles)
    even, odd = slot_offsets(regions)
    size = regions // 2
    for index in range(places):
        other, slot = index // size, part * size + index % size
        offset = jnp.where((tile ^ other) & 1 == 0, even[slot], odd[slot])
        region = here ^ offset
        side_ref = near_ref if 2 * other < tiles else other_ref
        far_ref[index, 0:4, :] = factor * side_ref[other % (tiles // 2), region]
        distance_ref[index : index + 1, :] = jnp.full((1, LANES), region - here, jnp.int32)

    def prepare():
        column = jnp.transpose(own_ref[...])
        for row in range(3):
            scale = 2.0 if row < 2 else 1.0
            wide_ref[row] = jnp.broadcast_to(scale * column[:, row : row + 1], (local, LANES))

    plan_blocks(
        distance_ref, own_ref, far_ref, 1 << chunk_bits,
        stage_ref, bounds_ref, ids_ref, count_ref, bounds_sem, prepare,
    )
    total = count_ref[0]

    def build_batch(batch, carry):
        for part in range(BATCH):
            real, place, lanes, rows = locate(ids_ref, batch, part, chunk_bits)
            far = far_ref[place, :, lanes]
            across_x = wide_ref[0, rows, :] - far[0:1, :]
            across_y = wide_ref[1, rows, :] - far[1:2, :]
            value = gaspari_cohn(across_x * across_x + across_y * across_y)
            spread = jnp.where(real, far[2:3, :], 0.0)
            value = wide_ref[2, rows, :] * spread * value
            tiles_ref[batch, :, part * LANES : (part + 1) * LANES] = value.astype(jnp.bfloat16)
        return carry

    lax.fori_loop(0, total, build_batch, 0)


def build_tiles(part, device, own, near, far, capacity):
    places, local = near.shape[0] * near.shape[1], own.shape[1]
    smem = pl.BlockSpec(memory_space=pltpu.SMEM)
    sizes = (capacity * BATCH + local // LANES, 1)
    shape = (capacity, ROWS, BATCH * LANES)
    scratch = [
        pltpu.VMEM((3, local, LANES), jnp.float32),
        pltpu.VMEM((places, 8, local), jnp.float32),
        pltpu.VMEM((places, LANES), jnp.int32),
        pltpu.SMEM((places, LANES), jnp.int32),
        pltpu.SemaphoreType.DMA,
        pltpu.VMEM((places, LANES), jnp.int32),
    ]
    return pl.pallas_call(
        functools.partial(build_kernel, part),
        out_shape=tuple(jax.ShapeDtypeStruct((size,), jnp.int32) for size in sizes)
        + (pltpu.VMEM(shape, jnp.bfloat16),),
        in_specs=[smem] + whole_vmem(3),
        out_specs=(smem,) * 2 + (pl.BlockSpec(memory_space=pltpu.VMEM),),
        scratch_shapes=scratch,
        compiler_params=pltpu.CompilerParams(vmem_limit_bytes=VMEM),
        cost_estimate=pl.CostEstimate(
            flops=2 * local * local * 16000, bytes_accessed=16 * local * local, transcendentals=0
        ),
        name="build_tiles",
    )(device, own, near, far)


def apply_kernel(started, last, grams, ids_ref, count_ref, near_ref, other_ref, tiles_ref, *refs):
    refs = list(refs)
    start_ref = refs.pop(0) if started else None
    if last:
        first_ref = refs.pop(2) if grams else None
        block_ref, scale_ref, out_ref, rounded_ref = refs[:4]
        total_ref = refs[-1]
    else:
        (total_ref,) = refs
    half, columns, local = near_ref.shape
    chunk_bits = (local // LANES).bit_length() - 1
    total = count_ref[0]
    groups = lax.div(total + UNROLL - 1, UNROLL)

    if started:
        total_ref[...] = start_ref[...]
    else:
        total_ref[...] = jnp.zeros(total_ref.shape, jnp.float32)

    def turn(group, carry):
        values = []
        for inner in range(UNROLL):
            batch = jnp.minimum(group * UNROLL + inner, total - 1)
            valid = group * UNROLL + inner < total
            for pair in range(BATCH // PAIR):
                sides = []
                for part in range(pair * PAIR, (pair + 1) * PAIR):
                    _, place, chunk, rows = locate(ids_ref, batch, part, chunk_bits)
                    inside = jnp.where(place < half, place, place - half)
                    sides.append(
                        jnp.where(place < half, near_ref[inside, :, chunk], other_ref[inside, :, chunk])
                    )
                side = jnp.concatenate(sides, axis=1)
                if inner:
                    side = jnp.where(valid, side, jnp.zeros_like(side))
                lanes = slice(pair * PAIR * LANES, (pair + 1) * PAIR * LANES)
                values.append((rows, dot_nt(tiles_ref[batch, :, lanes], side)))
        for rows, value in values:
            total_ref[rows, :] += value
        return carry

    lax.fori_loop(0, groups, turn, 0)
    if last:
        block = block_ref[...]
        result = jnp.transpose(total_ref[...]) + scale_ref[...] * block
        out_ref[...] = result
        rounded_ref[...] = result.astype(jnp.bfloat16)
        if grams:
            refs[4][...] = jnp.concatenate([first_ref[...], packed_grams(block, result)], axis=1)


def apply_tiles(plan, near, far, tiles, start, finish):
    near, far = [piece.reshape((-1,) + piece.shape[2:]) for piece in (near, far)]
    half, columns, local = near.shape
    last = finish is not None
    grams = last and len(finish) > 2
    smem = pl.BlockSpec(memory_space=pltpu.SMEM)
    operands = [*plan, near, far, tiles]
    in_specs = [smem] * 2 + whole_vmem(3)
    if start is not None:
        operands.append(start)
        in_specs += whole_vmem(1)
    scratch = []
    if last:
        operands += finish
        in_specs += whole_vmem(len(finish))
        out_shape = (
            jax.ShapeDtypeStruct((columns, local), jnp.float32),
            jax.ShapeDtypeStruct((columns, local), jnp.bfloat16),
        )
        if grams:
            out_shape += (jax.ShapeDtypeStruct((columns + 8, 2 * columns), jnp.float32),)
        scratch.append(pltpu.VMEM((local, columns), jnp.float32))
    else:
        out_shape = (jax.ShapeDtypeStruct((local, columns), jnp.float32),)
    return pl.pallas_call(
        functools.partial(apply_kernel, start is not None, last, grams),
        out_shape=out_shape,
        in_specs=in_specs,
        out_specs=tuple(whole_vmem(len(out_shape))),
        scratch_shapes=scratch,
        compiler_params=pltpu.CompilerParams(vmem_limit_bytes=VMEM),
        cost_estimate=pl.CostEstimate(
            flops=2 * local * local * 6000, bytes_accessed=16 * local * local, transcendentals=0
        ),
        name="apply_last" if last else "apply_first",
    )(*operands)


def packed_grams(left, right):
    n = left.shape[0]
    both = dot_nt(left, jnp.concatenate([left, right], axis=0), HIGHEST)
    square, mixed = both[:, :n], both[:, n:]
    mixed = 0.5 * (mixed + jnp.transpose(mixed))
    row, column = [lax.broadcasted_iota(jnp.int32, (n, n), axis) for axis in range(2)]
    diagonals = [
        jnp.sum(jnp.where(row == column, matrix, 0.0), axis=0, keepdims=True) for matrix in (square, mixed)
    ]
    rest = jnp.zeros((6, n), jnp.float32)
    return jnp.concatenate([jnp.where(row < column, square, mixed), *diagonals, rest], axis=0)


def unpacked_grams(packed):
    n = packed.shape[1]
    matrix = packed[:n]
    row, column = [lax.broadcasted_iota(jnp.int32, (n, n), axis) for axis in range(2)]
    upper = jnp.where(row < column, matrix, 0.0)
    lower = jnp.where(row > column, matrix, 0.0)
    diagonals = [jnp.where(row == column, packed[n + k : n + k + 1], 0.0) for k in range(2)]
    return upper + jnp.transpose(upper) + diagonals[0], lower + jnp.transpose(lower) + diagonals[1]


def grams_kernel(left_ref, right_ref, out_ref):
    out_ref[...] = packed_grams(left_ref[...], right_ref[...])


def first_grams(left, right):
    n = left.shape[0]
    return pl.pallas_call(
        grams_kernel,
        out_shape=jax.ShapeDtypeStruct((n + 8, n), jnp.float32),
        in_specs=whole_vmem(2),
        out_specs=whole_vmem(1)[0],
        compiler_params=pltpu.CompilerParams(vmem_limit_bytes=VMEM),
        cost_estimate=pl.CostEstimate(flops=2 * 10**9, bytes_accessed=8 * left.size, transcendentals=0),
        name="first_grams",
    )(left, right)


def reciprocal(value):
    root = lax.rsqrt(value)
    return root * root


def small_product(left, right):
    return [[sum(l * r[j] for l, r in zip(row, right)) for j in range(len(right[0]))] for row in left]


def small_difference(left, right):
    return [[l - r for l, r in zip(*rows)] for rows in zip(left, right)]


def small_inverse(matrix):
    (a, b), (c, d) = matrix
    scale = reciprocal(a * d - b * c)
    return [[d * scale, -b * scale], [-c * scale, a * scale]]


def solve_positive(matrix, target):
    n = matrix.shape[0]
    table = jnp.concatenate([0.5 * (matrix + jnp.transpose(matrix)), target], axis=1)
    bands = [table[k : k + 8, :] for k in range(0, n, 8)]
    row_index = lax.broadcasted_iota(jnp.int32, bands[0].shape, 0)
    for k in range(0, n, 4):
        own, row = k // 8, k % 8
        columns = [
            [jnp.broadcast_to(band[:, k + j : k + j + 1], band.shape) for band in bands] for j in range(4)
        ]
        pivot = [[columns[j][own][row + i : row + i + 1] for j in range(4)] for i in range(4)]
        upper, lower = pivot[:2], pivot[2:]
        top = small_inverse([r[:2] for r in upper])
        factor = small_product([r[:2] for r in lower], top)
        right = [r[2:] for r in upper]
        rest = small_inverse(small_difference([r[2:] for r in lower], small_product(factor, right)))
        rows = [[bands[own][row + i : row + i + 1]] for i in range(4)]
        last = small_product(rest, small_difference(rows[2:], small_product(factor, rows[:2])))
        first = small_product(top, small_difference(rows[:2], small_product(right, last)))
        new = [r[0] for r in first + last]
        bands = [
            band - ((columns[0][i] * new[0] + columns[1][i] * new[1]) + (columns[2][i] * new[2] + columns[3][i] * new[3]))
            for i, band in enumerate(bands)
        ]
        for i in range(4):
            bands[own] = jnp.where(row_index == row + i, new[i], bands[own])
    return jnp.concatenate([band[:, n:] for band in bands], axis=0)


def last_kernel(grams_ref, start_ref, images_ref, weights_ref, residual_ref):
    n = grams_ref.shape[1] // 2
    squares, mixed = unpacked_grams(grams_ref[:, :n])
    images, cross = unpacked_grams(grams_ref[:, n:])
    solved = solve_positive(mixed, jnp.concatenate([squares, images], axis=1))
    step, carried = solved[:, :n], solved[:, n:]
    product = dot_nn(images, solved, HIGHEST)
    second = solve_positive(cross - product[:, n:], mixed - product[:, :n])
    first = jnp.transpose(step - dot_nn(carried, second, HIGHEST))
    second = jnp.transpose(second)
    both = jnp.concatenate([first, second], axis=1)
    start, images = start_ref[...], images_ref[...]
    weights_ref[...] = dot_nn(both, jnp.concatenate([start, images[:n]], axis=0), HIGHEST)
    residual_ref[...] = start - dot_nn(both, images, HIGHEST)


def last_step(grams, start, images):
    return pl.pallas_call(
        last_kernel,
        out_shape=(jax.ShapeDtypeStruct(start.shape, jnp.float32),) * 2,
        in_specs=whole_vmem(3),
        out_specs=tuple(whole_vmem(2)),
        compiler_params=pltpu.CompilerParams(vmem_limit_bytes=VMEM),
        name="last_step",
    )(grams, start, images)


def shards(innovations, obs_geometry, obs_error, tile_owner):
    tiles_axis, regions = lax.axis_size("tile"), lax.axis_size("region")
    reach = tile_owner.shape[1]
    columns, local = innovations.shape
    device = lax.axis_index(("region", "tile")).astype(jnp.int32).reshape(1)
    rounded, places, own, start, rank = sort_region(
        device,
        tile_owner,
        *halves(obs_geometry, "tile"),
        *halves(obs_error[None, :], "tile"),
        *halves(innovations, "tile"),
    )
    scale = own[3:4]
    everywhere = jnp.broadcast_to(places[None], (regions,) + places.shape)
    everywhere = lax.all_to_all(everywhere, "region", 0, 0)
    near_places, far_places = halves(everywhere, "tile")

    half_regions = regions // 2
    most = min(half_regions, 2 * reach - 1) * tiles_axis * (local // LANES)
    batches = -(-(local // ROWS) * -(-most // PAIR) * PAIR // BATCH) + 1
    capacity = -(-batches // UNROLL) * UNROLL
    plans, tiles = [], []
    for part in range(2):
        *plan, built = build_tiles(part, device, own, near_places, far_places, capacity)
        plans.append(plan)
        tiles.append(built)

    def operate(sent, block, *grams):
        building = not grams
        total = None
        for part, group in enumerate(exchange(sent, *grams)):
            if building:
                group, plans[part] = lax.optimization_barrier((group, plans[part]))
            elif part:
                group, total = lax.optimization_barrier((group, total))
            near, far = halves(group, "tile")
            results = apply_tiles(
                plans[part], near, far, tiles[part], total, (block, scale, *grams) if part else None
            )
            total = results[0]
        return results

    image, image_rounded = operate(rounded, start)
    second, _, grams = operate(image_rounded, image, first_grams(start, image))
    grams = sum_regions(sum_tiles(grams))
    near, far = halves(jnp.concatenate([image, second], axis=0), "tile")
    images = unsort(device, rank, jnp.concatenate([*near, *far], axis=1))
    return last_step(grams, innovations, images)


def solution(mesh):
    return jax.shard_map(
        shards,
        mesh=mesh,
        in_specs=(
            P(None, ("region", "tile")),
            P(None, ("region", "tile")),
            P(("region", "tile")),
            P("region", None),
        ),
        out_specs=(P(None, ("region", "tile")), P(None, ("region", "tile"))),
        check_vma=False,
    )
```

```python
import functools

import jax
import jax.numpy as jnp
from jax import lax
from jax.experimental import pallas as pl
from jax.experimental.pallas import tpu as pltpu
from jax.sharding import PartitionSpec as P

CUTOFF = 1.001
ROW_SHIFT, SKIP = 20, 1 << 19
LANES = 128
ROWS = 64
PAIR = 2
BATCH = 2 * PAIR
UNROLL = 8
VMEM = 16 * 1024 * 1024
HIGHEST = lax.Precision.HIGHEST


def whole_vmem(count):
    return [pl.BlockSpec(memory_space=pltpu.VMEM)] * count


def in_hbm(value):
    return pltpu.with_memory_space_constraint(value, pltpu.HBM)


def dot_nt(left, right, precision=None):
    return lax.dot_general(
        left, right, (((1,), (1,)), ((), ())), precision=precision, preferred_element_type=jnp.float32
    )


def dot_nn(left, right, precision=None):
    return lax.dot_general(
        left, right, (((1,), (0,)), ((), ())), precision=precision, preferred_element_type=jnp.float32
    )


def three_parts(value):
    high = value.astype(jnp.bfloat16)
    rest = value - high.astype(jnp.float32)
    middle = rest.astype(jnp.bfloat16)
    low = (rest - middle.astype(jnp.float32)).astype(jnp.bfloat16)
    return high, middle, low


def halves(block, axis):
    count = lax.axis_size(axis)
    block = block[None]
    bit = 1
    while 2 * bit < count:
        block = jnp.concatenate([block, swapped(block, axis, bit)], axis=0)
        bit *= 2
    return block, swapped(block, axis, bit)


def swapped(block, axis, bit):
    return lax.ppermute(block, axis, [(i, i ^ bit) for i in range(lax.axis_size(axis))])


def sum_tiles(block):
    bit = 1
    while bit < lax.axis_size("tile"):
        block = block + swapped(block, "tile", bit)
        bit *= 2
    return block


def swap_regions(block, even, odd):
    tiles = lax.axis_size("tile")
    route = [
        (region * tiles + tile, (region ^ (odd if tile % 2 else even)) * tiles + tile)
        for region in range(lax.axis_size("region"))
        for tile in range(tiles)
    ]
    return lax.ppermute(block, ("region", "tile"), route)


def sum_regions(block, later):
    bits, _ = region_orders(lax.axis_size("region"))
    middle = len(bits) // 2
    for step, (even, odd) in enumerate(zip(bits, bits[middle:] + bits[:middle])):
        if step == len(bits) - 1:
            block, later = lax.optimization_barrier((block, later))
        block = block + swap_regions(block, even, odd)
    return block, later


def region_orders(count):
    bits = []
    bit = count // 2
    while bit:
        bits.append(bit)
        bit //= 2
    return bits, bits[:1] + bits[-1:] + bits[1:-1] if len(bits) > 2 else bits[::-1]


def slot_offsets(count):
    table = []
    for bits in region_orders(count):
        offsets = [0]
        for bit in bits:
            offsets = offsets + [offset ^ bit for offset in offsets]
        table.append(offsets)
    return table


def exchange(block, *beside):
    regions = lax.axis_size("region")
    block = block[None]
    for even, odd in zip(*region_orders(regions)):
        other = swap_regions(block, even, odd)
        if 2 * block.shape[0] == regions:
            return block, other
        other, *beside = lax.optimization_barrier((other, *beside))
        block = jnp.concatenate([block, other], axis=0)


def stacked_parts(value):
    return jnp.concatenate([part.astype(jnp.float32) for part in three_parts(value)], axis=0).astype(
        jnp.bfloat16
    )


def add_parts(value):
    rows = value.shape[0] // 3
    return (value[2 * rows :] + value[rows : 2 * rows]) + value[:rows]


def fill_order(first, rank, order_ref, row, count):
    step = 64

    def fill(block, carry):
        start = pl.multiple_of(block * step, step)
        place = first + start + lax.broadcasted_iota(jnp.int32, (step, rank.shape[1]), 0)
        order_ref[pl.ds(pl.multiple_of(row + start, step), step), :] = jnp.where(
            place == rank, 1.0, 0.0
        ).astype(jnp.bfloat16)
        return carry

    lax.fori_loop(0, count // step, fill, 0)


def sort_kernel(
    device_ref, owner_ref, near_ref, far_ref, near_error_ref, far_error_ref, block_ref, other_ref,
    rounded_out, places_out, own_out, block_out, rank_out,
    order_ref, column_ref, rank_ref, owned_ref, places_ref, errors_ref, blocks_ref, sems,
):
    columns, local = block_out.shape
    half = block_ref.shape[0]
    tile = lax.rem(device_ref[0], 2 * half)
    pairs = [(owner_ref, owned_ref)]
    for sources, target in (
        ((near_ref, far_ref), places_ref),
        ((near_error_ref, far_error_ref), errors_ref),
        ((block_ref, other_ref), blocks_ref),
    ):
        pairs += [(ref, target.at[pl.ds(part * half, half)]) for part, ref in enumerate(sources)]
    copies = [
        pltpu.make_async_copy(source, target, sems.at[index])
        for index, (source, target) in enumerate(pairs)
    ]
    for copy in copies:
        copy.start()
    for copy in copies[:5]:
        copy.wait()
    places = jnp.concatenate(
        [jnp.concatenate([places_ref[i], errors_ref[i]], axis=0) for i in range(2 * half)], axis=1
    )
    n = places.shape[1]
    step = 64
    index = jnp.concatenate(
        [
            ((tile ^ i) * local + lax.broadcasted_iota(jnp.int32, (1, local), 1)).astype(jnp.float32)
            for i in range(n // local)
        ],
        axis=1,
    )
    y_row = places[1:2, :]
    column_ref[...] = jnp.transpose(
        jnp.concatenate([y_row, index, jnp.zeros((6, n), jnp.float32)], axis=0)
    )

    def count(ties, block, total):
        start = pl.multiple_of(block * step, step)
        y_column = jnp.broadcast_to(column_ref[pl.ds(start, step), 0:1], (step, n))
        before = y_column < y_row
        if ties:
            index_column = jnp.broadcast_to(column_ref[pl.ds(start, step), 1:2], (step, n))
            before = before | ((y_column == y_row) & (index_column < index))
        return total + jnp.sum(jnp.where(before, 1.0, 0.0).reshape(step // 8, 8, n), axis=0)

    def ranks(ties):
        start = jnp.zeros((8, n), jnp.float32)
        total = lax.fori_loop(0, n // step, functools.partial(count, ties), start)
        rank_ref[...] = jnp.sum(total, axis=0, keepdims=True).astype(jnp.int32)

    ranks(False)

    @pl.when(jnp.sum(rank_ref[...]) != n * (n - 1) // 2)
    def _():
        ranks(True)

    rank = rank_ref[...]
    rank_out[...] = rank[:, :local]
    fill_order(tile * local, rank, order_ref, 0, local)
    for copy in copies[5:]:
        copy.wait()
    block = jnp.concatenate([blocks_ref[i] for i in range(2 * half)], axis=1)
    everything = jnp.concatenate(
        [
            *[part.astype(jnp.float32) for part in three_parts(block)[:2]],
            *[part.astype(jnp.float32) for part in three_parts(places)],
            jnp.zeros((4, n), jnp.float32),
        ],
        axis=0,
    ).astype(jnp.bfloat16)
    parts = dot_nt(everything, order_ref[...])
    high, low = parts[:columns], parts[columns : 2 * columns]
    rounded_out[...] = high.astype(jnp.bfloat16)
    block_out[...] = high + low
    whole = (parts[2 * columns + 8 : 2 * columns + 12] + parts[2 * columns + 4 : 2 * columns + 8]) + parts[
        2 * columns : 2 * columns + 4
    ]
    lane = lax.broadcasted_iota(jnp.int32, (1, local), 1)
    flags = jnp.zeros((1, local), jnp.float32)
    for offset in range(owner_ref.shape[1]):
        flags = jnp.where((lane == offset) & (owned_ref[0, offset] >= 0), 1.0, flags)
    own_out[...] = jnp.concatenate([whole, flags, jnp.zeros((3, local), jnp.float32)], axis=0)
    places_out[...] = jnp.concatenate([whole[:3], flags], axis=0)


def sort_region(device, tile_owner, near, far, near_error, far_error, block, other):
    local = near.shape[2]
    n = local * 2 * near.shape[0]
    columns = block.shape[1]
    smem = pl.BlockSpec(memory_space=pltpu.SMEM)
    return pl.pallas_call(
        sort_kernel,
        out_shape=(
            jax.ShapeDtypeStruct((columns, local), jnp.bfloat16),
            jax.ShapeDtypeStruct((4, local), jnp.float32),
            jax.ShapeDtypeStruct((8, local), jnp.float32),
            jax.ShapeDtypeStruct((columns, local), jnp.float32),
            jax.ShapeDtypeStruct((1, local), jnp.int32),
        ),
        in_specs=[smem] + [pl.BlockSpec(memory_space=pl.ANY)] * 7,
        out_specs=tuple(whole_vmem(5)),
        scratch_shapes=[
            pltpu.VMEM((local, n), jnp.bfloat16),
            pltpu.VMEM((n, 8), jnp.float32),
            pltpu.VMEM((1, n), jnp.int32),
            pltpu.SMEM(tile_owner.shape, jnp.int32),
            pltpu.VMEM((n // local, 3, local), jnp.float32),
            pltpu.VMEM((n // local, 1, local), jnp.float32),
            pltpu.VMEM((n // local, columns, local), jnp.float32),
            pltpu.SemaphoreType.DMA((7,)),
        ],
        compiler_params=pltpu.CompilerParams(vmem_limit_bytes=VMEM),
        cost_estimate=pl.CostEstimate(
            flops=6 * n * local * (columns + 8), bytes_accessed=4 * n * local, transcendentals=0
        ),
        name="sort_region",
    )(device, in_hbm(tile_owner), in_hbm(near), far, in_hbm(near_error), far_error, in_hbm(block), other)


def unsort_kernel(device_ref, rank_ref, block_ref, block_out, order_ref):
    n, local = order_ref.shape
    tile = lax.rem(device_ref[0], n // local)
    for slot in range(n // local):
        fill_order((tile ^ slot) * local, rank_ref[...], order_ref, slot * local, local)
    block_out[...] = add_parts(dot_nn(stacked_parts(block_ref[...]), order_ref[...]))


def unsort(device, rank, block):
    n = block.shape[1]
    local = rank.shape[1]
    return pl.pallas_call(
        unsort_kernel,
        out_shape=jax.ShapeDtypeStruct((block.shape[0], local), jnp.float32),
        in_specs=[pl.BlockSpec(memory_space=pltpu.SMEM)] + whole_vmem(2),
        out_specs=whole_vmem(1)[0],
        scratch_shapes=[pltpu.VMEM((n, local), jnp.bfloat16)],
        compiler_params=pltpu.CompilerParams(vmem_limit_bytes=VMEM),
        cost_estimate=pl.CostEstimate(
            flops=20 * n * local * block.shape[0], bytes_accessed=4 * n * local, transcendentals=0
        ),
        name="unsort",
    )(device, rank, block)


def plan_blocks(
    distance_ref, own_ref, far_ref, chunks, stage_ref, bounds_ref, ids_ref, count_ref, sem, prepare,
):
    places, local = far_ref.shape[0], own_ref.shape[1]
    blocks = local // ROWS
    lane = lax.broadcasted_iota(jnp.int32, (1, LANES), 1)

    lowest = jnp.zeros((1, LANES), jnp.float32)
    highest = lowest
    for block in range(blocks):
        here = (lane == block) | (lane == blocks + block)
        low = own_ref[1:2, block * ROWS : block * ROWS + 1]
        high = own_ref[1:2, (block + 1) * ROWS - 1 : (block + 1) * ROWS]
        lowest = jnp.where(here, 2.0 * (low - CUTOFF), lowest)
        highest = jnp.where(here, 2.0 * (high + CUTOFF), highest)
    y = far_ref[:, 1, :]
    first = jnp.zeros((places, LANES), jnp.int32)
    beyond = first
    for chunk in range(chunks):
        low = y[:, chunk * LANES : chunk * LANES + 1]
        high = y[:, (chunk + 1) * LANES - 1 : (chunk + 1) * LANES]
        first = first + (high < lowest).astype(jnp.int32)
        beyond = beyond + (low <= highest).astype(jnp.int32)
    distance = distance_ref[...]
    flags = jnp.where((lane == -distance) & (far_ref[:, 3, :LANES] > 0.0), 1.0, 0.0)
    flags = flags + jnp.where(lane == distance, own_ref[4:5, :LANES], 0.0)
    listed = jnp.sum(flags, axis=1, keepdims=True) > 0.0
    found = jnp.where(listed, jnp.maximum(beyond - first, 0), 0)
    stage_ref[...] = jnp.where(lane < blocks, first, found)
    copy = pltpu.make_async_copy(stage_ref, bounds_ref, sem)
    copy.start()
    prepare()
    copy.wait()

    count = jnp.int32(0)
    for block in range(blocks):

        def add_place(place, count, block=block):
            entry = (block << ROW_SHIFT) + place * chunks + bounds_ref[place, block]
            for chunk in range(chunks):
                ids_ref[count + chunk] = entry + chunk
            return count + bounds_ref[place, blocks + block]

        count = lax.fori_loop(0, places, add_place, count, unroll=8)
        for extra in range(PAIR - 1):
            ids_ref[count + extra] = (block << ROW_SHIFT) + SKIP
        count = lax.div(count + PAIR - 1, PAIR) * PAIR
    for extra in range(BATCH - PAIR):
        ids_ref[count + extra] = SKIP
    count_ref[0] = lax.div(count + BATCH - 1, BATCH)


def gaspari_cohn(squared):
    squared = jnp.maximum(squared, 1e-12)
    inverse = lax.rsqrt(squared)
    scaled = squared * inverse
    near = (((-3.0 * scaled + 6.0) * scaled + 7.5) * scaled - 20.0) * squared + 12.0
    left = jnp.maximum(2.0 - scaled, 0.0)
    left = left * left
    far = (left * left) * (((scaled + 2.0) * scaled - 0.5) * inverse)
    return jnp.where(scaled <= 1.0, near, far)


def locate(ids_ref, batch, part, chunk_bits):
    entry = ids_ref[batch * BATCH + part]
    lane = pl.multiple_of((entry & ((1 << chunk_bits) - 1)) * LANES, LANES)
    start = pl.multiple_of(lax.shift_right_logical(entry, ROW_SHIFT) * ROWS, ROWS)
    place = lax.shift_right_logical(entry & (SKIP - 1), chunk_bits)
    return (entry & SKIP) == 0, place, pl.ds(lane, LANES), pl.ds(start, ROWS)


def build_kernel(
    part, device_ref, own_ref, near_ref, other_ref,
    ids_ref, count_ref, tiles_ref,
    wide_ref, far_ref, stage_ref, bounds_ref, bounds_sem, distance_ref,
):
    local = own_ref.shape[1]
    places = far_ref.shape[0]
    chunk_bits = (local // LANES).bit_length() - 1
    factor = jnp.where(lax.broadcasted_iota(jnp.int32, (4, 1), 0) < 2, 2.0, 1.0 / 12.0)
    tiles, regions = 2 * near_ref.shape[0], near_ref.shape[1]
    here, tile = lax.div(device_ref[0], tiles), lax.rem(device_ref[0], tiles)
    even, odd = slot_offsets(regions)
    size = regions // 2
    for index in range(places):
        other, slot = index // size, part * size + index % size
        offset = jnp.where((tile ^ other) & 1 == 0, even[slot], odd[slot])
        region = here ^ offset
        side_ref = near_ref if 2 * other < tiles else other_ref
        far_ref[index, 0:4, :] = factor * side_ref[other % (tiles // 2), region]
        distance_ref[index : index + 1, :] = jnp.full((1, LANES), region - here, jnp.int32)

    def prepare():
        column = jnp.transpose(own_ref[...])
        for row in range(3):
            scale = 2.0 if row < 2 else 1.0
            wide_ref[row] = jnp.broadcast_to(scale * column[:, row : row + 1], (local, LANES))

    plan_blocks(
        distance_ref, own_ref, far_ref, 1 << chunk_bits,
        stage_ref, bounds_ref, ids_ref, count_ref, bounds_sem, prepare,
    )
    total = count_ref[0]

    def build_batch(batch, carry):
        for part in range(BATCH):
            real, place, lanes, rows = locate(ids_ref, batch, part, chunk_bits)
            far = far_ref[place, :, lanes]
            across_x = wide_ref[0, rows, :] - far[0:1, :]
            across_y = wide_ref[1, rows, :] - far[1:2, :]
            value = gaspari_cohn(across_x * across_x + across_y * across_y)
            spread = jnp.where(real, far[2:3, :], 0.0)
            value = wide_ref[2, rows, :] * spread * value
            tiles_ref[batch, :, part * LANES : (part + 1) * LANES] = value.astype(jnp.bfloat16)
        return carry

    lax.fori_loop(0, total, build_batch, 0)


def build_tiles(part, device, own, near, far, capacity):
    places, local = near.shape[0] * near.shape[1], own.shape[1]
    smem = pl.BlockSpec(memory_space=pltpu.SMEM)
    sizes = (capacity * BATCH + local // LANES, 1)
    shape = (capacity, ROWS, BATCH * LANES)
    scratch = [
        pltpu.VMEM((3, local, LANES), jnp.float32),
        pltpu.VMEM((places, 8, local), jnp.float32),
        pltpu.VMEM((places, LANES), jnp.int32),
        pltpu.SMEM((places, LANES), jnp.int32),
        pltpu.SemaphoreType.DMA,
        pltpu.VMEM((places, LANES), jnp.int32),
    ]
    return pl.pallas_call(
        functools.partial(build_kernel, part),
        out_shape=tuple(jax.ShapeDtypeStruct((size,), jnp.int32) for size in sizes)
        + (pltpu.VMEM(shape, jnp.bfloat16),),
        in_specs=[smem] + whole_vmem(3),
        out_specs=(smem,) * 2 + (pl.BlockSpec(memory_space=pltpu.VMEM),),
        scratch_shapes=scratch,
        compiler_params=pltpu.CompilerParams(vmem_limit_bytes=VMEM),
        cost_estimate=pl.CostEstimate(
            flops=2 * local * local * 16000, bytes_accessed=16 * local * local, transcendentals=0
        ),
        name="build_tiles",
    )(device, own, near, far)


def apply_kernel(started, last, grams, ids_ref, count_ref, near_ref, other_ref, tiles_ref, *refs):
    refs = list(refs)
    start_ref = refs.pop(0) if started else None
    if last:
        first_ref = refs.pop(2) if grams else None
        block_ref, scale_ref, out_ref, rounded_ref = refs[:4]
        total_ref = refs[-1]
    else:
        (total_ref,) = refs
    half, columns, local = near_ref.shape
    chunk_bits = (local // LANES).bit_length() - 1
    total = count_ref[0]
    groups = lax.div(total + UNROLL - 1, UNROLL)

    if started:
        total_ref[...] = start_ref[...]
    else:
        total_ref[...] = jnp.zeros(total_ref.shape, jnp.float32)

    def turn(group, carry):
        values = []
        for inner in range(UNROLL):
            batch = jnp.minimum(group * UNROLL + inner, total - 1)
            valid = group * UNROLL + inner < total
            for pair in range(BATCH // PAIR):
                sides = []
                for part in range(pair * PAIR, (pair + 1) * PAIR):
                    _, place, chunk, rows = locate(ids_ref, batch, part, chunk_bits)
                    inside = jnp.where(place < half, place, place - half)
                    sides.append(
                        jnp.where(place < half, near_ref[inside, :, chunk], other_ref[inside, :, chunk])
                    )
                side = jnp.concatenate(sides, axis=1)
                if inner:
                    side = jnp.where(valid, side, jnp.zeros_like(side))
                lanes = slice(pair * PAIR * LANES, (pair + 1) * PAIR * LANES)
                values.append((rows, dot_nt(tiles_ref[batch, :, lanes], side)))
        for rows, value in values:
            total_ref[rows, :] += value
        return carry

    lax.fori_loop(0, groups, turn, 0)
    if last:
        block = block_ref[...]
        result = jnp.transpose(total_ref[...]) + scale_ref[...] * block
        out_ref[...] = result
        rounded_ref[...] = result.astype(jnp.bfloat16)
        if grams:
            refs[4][...] = jnp.concatenate([first_ref[...], packed_grams(block, result)], axis=1)


def apply_tiles(plan, near, far, tiles, start, finish):
    near, far = [piece.reshape((-1,) + piece.shape[2:]) for piece in (near, far)]
    half, columns, local = near.shape
    last = finish is not None
    grams = last and len(finish) > 2
    smem = pl.BlockSpec(memory_space=pltpu.SMEM)
    operands = [*plan, near, far, tiles]
    in_specs = [smem] * 2 + whole_vmem(3)
    if start is not None:
        operands.append(start)
        in_specs += whole_vmem(1)
    scratch = []
    if last:
        operands += finish
        in_specs += whole_vmem(len(finish))
        out_shape = (
            jax.ShapeDtypeStruct((columns, local), jnp.float32),
            jax.ShapeDtypeStruct((columns, local), jnp.bfloat16),
        )
        if grams:
            out_shape += (jax.ShapeDtypeStruct((columns + 8, 2 * columns), jnp.float32),)
        scratch.append(pltpu.VMEM((local, columns), jnp.float32))
    else:
        out_shape = (jax.ShapeDtypeStruct((local, columns), jnp.float32),)
    return pl.pallas_call(
        functools.partial(apply_kernel, start is not None, last, grams),
        out_shape=out_shape,
        in_specs=in_specs,
        out_specs=tuple(whole_vmem(len(out_shape))),
        scratch_shapes=scratch,
        compiler_params=pltpu.CompilerParams(vmem_limit_bytes=VMEM),
        cost_estimate=pl.CostEstimate(
            flops=2 * local * local * 6000, bytes_accessed=16 * local * local, transcendentals=0
        ),
        name="apply_last" if last else "apply_first",
    )(*operands)


def packed_grams(left, right):
    n = left.shape[0]
    both = dot_nt(left, jnp.concatenate([left, right], axis=0), HIGHEST)
    square, mixed = both[:, :n], both[:, n:]
    mixed = 0.5 * (mixed + jnp.transpose(mixed))
    row, column = [lax.broadcasted_iota(jnp.int32, (n, n), axis) for axis in range(2)]
    diagonals = [
        jnp.sum(jnp.where(row == column, matrix, 0.0), axis=0, keepdims=True) for matrix in (square, mixed)
    ]
    rest = jnp.zeros((6, n), jnp.float32)
    return jnp.concatenate([jnp.where(row < column, square, mixed), *diagonals, rest], axis=0)


def unpacked_grams(packed):
    n = packed.shape[1]
    matrix = packed[:n]
    row, column = [lax.broadcasted_iota(jnp.int32, (n, n), axis) for axis in range(2)]
    upper = jnp.where(row < column, matrix, 0.0)
    lower = jnp.where(row > column, matrix, 0.0)
    diagonals = [jnp.where(row == column, packed[n + k : n + k + 1], 0.0) for k in range(2)]
    return upper + jnp.transpose(upper) + diagonals[0], lower + jnp.transpose(lower) + diagonals[1]


def grams_kernel(left_ref, right_ref, out_ref):
    out_ref[...] = packed_grams(left_ref[...], right_ref[...])


def first_grams(left, right):
    n = left.shape[0]
    return pl.pallas_call(
        grams_kernel,
        out_shape=jax.ShapeDtypeStruct((n + 8, n), jnp.float32),
        in_specs=whole_vmem(2),
        out_specs=whole_vmem(1)[0],
        compiler_params=pltpu.CompilerParams(vmem_limit_bytes=VMEM),
        cost_estimate=pl.CostEstimate(flops=2 * 10**9, bytes_accessed=8 * left.size, transcendentals=0),
        name="first_grams",
    )(left, right)


def small_product(left, right):
    return [[sum(l * r[j] for l, r in zip(row, right)) for j in range(len(right[0]))] for row in left]


def small_difference(left, right):
    return [[l - r for l, r in zip(*rows)] for rows in zip(left, right)]


def small_inverse(matrix):
    (a, b), (c, d) = matrix
    scale = 1.0 / (a * d - b * c)
    return [[d * scale, -b * scale], [-c * scale, a * scale]]


def solve_positive(matrix, target):
    n = matrix.shape[0]
    table = jnp.concatenate([0.5 * (matrix + jnp.transpose(matrix)), target], axis=1)
    bands = [table[k : k + 8, :] for k in range(0, n, 8)]
    row_index = lax.broadcasted_iota(jnp.int32, bands[0].shape, 0)
    for k in range(0, n, 4):
        own, row = k // 8, k % 8
        columns = [
            [jnp.broadcast_to(band[:, k + j : k + j + 1], band.shape) for band in bands] for j in range(4)
        ]
        pivot = [[columns[j][own][row + i : row + i + 1] for j in range(4)] for i in range(4)]
        upper, lower = pivot[:2], pivot[2:]
        top = small_inverse([r[:2] for r in upper])
        factor = small_product([r[:2] for r in lower], top)
        right = [r[2:] for r in upper]
        rest = small_inverse(small_difference([r[2:] for r in lower], small_product(factor, right)))
        rows = [[bands[own][row + i : row + i + 1]] for i in range(4)]
        last = small_product(rest, small_difference(rows[2:], small_product(factor, rows[:2])))
        first = small_product(top, small_difference(rows[:2], small_product(right, last)))
        new = [r[0] for r in first + last]
        bands = [
            band - ((columns[0][i] * new[0] + columns[1][i] * new[1]) + (columns[2][i] * new[2] + columns[3][i] * new[3]))
            for i, band in enumerate(bands)
        ]
        for i in range(4):
            bands[own] = jnp.where(row_index == row + i, new[i], bands[own])
    return jnp.concatenate([band[:, n:] for band in bands], axis=0)


def last_kernel(grams_ref, start_ref, images_ref, weights_ref, residual_ref):
    n = grams_ref.shape[1] // 2
    squares, mixed = unpacked_grams(grams_ref[:, :n])
    images, cross = unpacked_grams(grams_ref[:, n:])
    solved = solve_positive(mixed, jnp.concatenate([squares, images], axis=1))
    step, carried = solved[:, :n], solved[:, n:]
    product = dot_nn(images, solved, HIGHEST)
    second = solve_positive(cross - product[:, n:], mixed - product[:, :n])
    first = jnp.transpose(step - dot_nn(carried, second, HIGHEST))
    second = jnp.transpose(second)
    both = jnp.concatenate([first, second], axis=1)
    start, images = start_ref[...], images_ref[...]
    weights_ref[...] = dot_nn(both, jnp.concatenate([start, images[:n]], axis=0), HIGHEST)
    residual_ref[...] = start - dot_nn(both, images, HIGHEST)


def last_step(grams, start, images):
    return pl.pallas_call(
        last_kernel,
        out_shape=(jax.ShapeDtypeStruct(start.shape, jnp.float32),) * 2,
        in_specs=whole_vmem(3),
        out_specs=tuple(whole_vmem(2)),
        compiler_params=pltpu.CompilerParams(vmem_limit_bytes=VMEM),
        name="last_step",
    )(grams, start, images)


def shards(innovations, obs_geometry, obs_error, tile_owner):
    tiles_axis, regions = lax.axis_size("tile"), lax.axis_size("region")
    reach = tile_owner.shape[1]
    columns, local = innovations.shape
    device = lax.axis_index(("region", "tile")).astype(jnp.int32).reshape(1)
    rounded, places, own, start, rank = sort_region(
        device,
        tile_owner,
        *halves(obs_geometry, "tile"),
        *halves(obs_error[None, :], "tile"),
        *halves(innovations, "tile"),
    )
    scale = own[3:4]
    everywhere = jnp.broadcast_to(places[None], (regions,) + places.shape)
    everywhere = lax.all_to_all(everywhere, "region", 0, 0)
    near_places, far_places = halves(everywhere, "tile")

    half_regions = regions // 2
    most = min(half_regions, 2 * reach - 1) * tiles_axis * (local // LANES)
    batches = -(-(local // ROWS) * -(-most // PAIR) * PAIR // BATCH) + 1
    capacity = -(-batches // UNROLL) * UNROLL
    plans, tiles = [], []
    for part in range(2):
        *plan, built = build_tiles(part, device, own, near_places, far_places, capacity)
        plans.append(plan)
        tiles.append(built)

    def operate(sent, block, *grams):
        building = not grams
        total = None
        for part, group in enumerate(exchange(sent, *grams)):
            if building:
                group, plans[part] = lax.optimization_barrier((group, plans[part]))
            elif part:
                group, total = lax.optimization_barrier((group, total))
            near, far = halves(group, "tile")
            results = apply_tiles(
                plans[part], near, far, tiles[part], total, (block, scale, *grams) if part else None
            )
            total = results[0]
        return results

    image, image_rounded = operate(rounded, start)
    second, _, grams = operate(image_rounded, image, first_grams(start, image))
    near, far = halves(jnp.concatenate([image, second], axis=0), "tile")
    images = jnp.concatenate([*near, *far], axis=1)
    grams, images = sum_regions(sum_tiles(grams), images)
    return last_step(grams, innovations, unsort(device, rank, images))


def solution(mesh):
    return jax.shard_map(
        shards,
        mesh=mesh,
        in_specs=(
            P(None, ("region", "tile")),
            P(None, ("region", "tile")),
            P(("region", "tile")),
            P("region", None),
        ),
        out_specs=(P(None, ("region", "tile")), P(None, ("region", "tile"))),
        check_vma=False,
    )
```

```python
import functools

import jax
import jax.numpy as jnp
from jax import lax
from jax.experimental import pallas as pl
from jax.experimental.pallas import tpu as pltpu
from jax.sharding import PartitionSpec as P

CUTOFF = 1.001
ROW_SHIFT, SKIP = 20, 1 << 19
LANES = 128
ROWS = 64
PAIR = 2
BATCH = 2 * PAIR
UNROLL = 8
VMEM = 16 * 1024 * 1024
HIGHEST = lax.Precision.HIGHEST


def whole_vmem(count):
    return [pl.BlockSpec(memory_space=pltpu.VMEM)] * count


def in_hbm(value):
    return pltpu.with_memory_space_constraint(value, pltpu.HBM)


def dot_nt(left, right, precision=None):
    return lax.dot_general(
        left, right, (((1,), (1,)), ((), ())), precision=precision, preferred_element_type=jnp.float32
    )


def dot_nn(left, right, precision=None):
    return lax.dot_general(
        left, right, (((1,), (0,)), ((), ())), precision=precision, preferred_element_type=jnp.float32
    )


def three_parts(value):
    high = value.astype(jnp.bfloat16)
    rest = value - high.astype(jnp.float32)
    middle = rest.astype(jnp.bfloat16)
    low = (rest - middle.astype(jnp.float32)).astype(jnp.bfloat16)
    return high, middle, low


def halves(block, axis):
    count = lax.axis_size(axis)
    block = block[None]
    bit = 1
    while 2 * bit < count:
        block = jnp.concatenate([block, swapped(block, axis, bit)], axis=0)
        bit *= 2
    return block, swapped(block, axis, bit)


def swapped(block, axis, bit):
    return lax.ppermute(block, axis, [(i, i ^ bit) for i in range(lax.axis_size(axis))])


def sum_tiles(block):
    bit = 1
    while bit < lax.axis_size("tile"):
        block = block + swapped(block, "tile", bit)
        bit *= 2
    return block


def swap_regions(block, even, odd):
    tiles = lax.axis_size("tile")
    route = [
        (region * tiles + tile, (region ^ (odd if tile % 2 else even)) * tiles + tile)
        for region in range(lax.axis_size("region"))
        for tile in range(tiles)
    ]
    return lax.ppermute(block, ("region", "tile"), route)


def sum_regions(block, later):
    bits, _ = region_orders(lax.axis_size("region"))
    middle = len(bits) // 2
    for step, (even, odd) in enumerate(zip(bits[::-1], (bits[middle:] + bits[:middle])[::-1])):
        if step == len(bits) - 1:
            block, later = lax.optimization_barrier((block, later))
        block = block + swap_regions(block, even, odd)
    return block, later


def region_orders(count):
    bits = []
    bit = count // 2
    while bit:
        bits.append(bit)
        bit //= 2
    return bits, bits[:1] + bits[-1:] + bits[1:-1] if len(bits) > 2 else bits[::-1]


def slot_offsets(count):
    table = []
    for bits in region_orders(count):
        offsets = [0]
        for bit in bits:
            offsets = offsets + [offset ^ bit for offset in offsets]
        table.append(offsets)
    return table


def exchange(block, *beside):
    regions = lax.axis_size("region")
    block = block[None]
    for even, odd in zip(*region_orders(regions)):
        other = swap_regions(block, even, odd)
        if 2 * block.shape[0] == regions:
            return block, other
        other, *beside = lax.optimization_barrier((other, *beside))
        block = jnp.concatenate([block, other], axis=0)


def stacked_parts(value):
    return jnp.concatenate([part.astype(jnp.float32) for part in three_parts(value)], axis=0).astype(
        jnp.bfloat16
    )


def add_parts(value):
    rows = value.shape[0] // 3
    return (value[2 * rows :] + value[rows : 2 * rows]) + value[:rows]


def fill_order(first, rank, order_ref, row, count):
    step = 64

    def fill(block, carry):
        start = pl.multiple_of(block * step, step)
        place = first + start + lax.broadcasted_iota(jnp.int32, (step, rank.shape[1]), 0)
        order_ref[pl.ds(pl.multiple_of(row + start, step), step), :] = jnp.where(
            place == rank, 1.0, 0.0
        ).astype(jnp.bfloat16)
        return carry

    lax.fori_loop(0, count // step, fill, 0)


def sort_kernel(
    device_ref, owner_ref, near_ref, far_ref, near_error_ref, far_error_ref, block_ref, other_ref,
    rounded_out, places_out, own_out, block_out, rank_out,
    order_ref, column_ref, rank_ref, owned_ref, places_ref, errors_ref, blocks_ref, sems,
):
    columns, local = block_out.shape
    half = block_ref.shape[0]
    tile = lax.rem(device_ref[0], 2 * half)
    pairs = [(owner_ref, owned_ref)]
    for sources, target in (
        ((near_ref, far_ref), places_ref),
        ((near_error_ref, far_error_ref), errors_ref),
        ((block_ref, other_ref), blocks_ref),
    ):
        pairs += [(ref, target.at[pl.ds(part * half, half)]) for part, ref in enumerate(sources)]
    copies = [
        pltpu.make_async_copy(source, target, sems.at[index])
        for index, (source, target) in enumerate(pairs)
    ]
    for copy in copies:
        copy.start()
    for copy in copies[:5]:
        copy.wait()
    places = jnp.concatenate(
        [jnp.concatenate([places_ref[i], errors_ref[i]], axis=0) for i in range(2 * half)], axis=1
    )
    n = places.shape[1]
    step = 64
    index = jnp.concatenate(
        [
            ((tile ^ i) * local + lax.broadcasted_iota(jnp.int32, (1, local), 1)).astype(jnp.float32)
            for i in range(n // local)
        ],
        axis=1,
    )
    y_row = places[1:2, :]
    column_ref[...] = jnp.transpose(
        jnp.concatenate([y_row, index, jnp.zeros((6, n), jnp.float32)], axis=0)
    )

    def count(ties, block, total):
        start = pl.multiple_of(block * step, step)
        y_column = jnp.broadcast_to(column_ref[pl.ds(start, step), 0:1], (step, n))
        before = y_column < y_row
        if ties:
            index_column = jnp.broadcast_to(column_ref[pl.ds(start, step), 1:2], (step, n))
            before = before | ((y_column == y_row) & (index_column < index))
        return total + jnp.sum(jnp.where(before, 1.0, 0.0).reshape(step // 8, 8, n), axis=0)

    def ranks(ties):
        start = jnp.zeros((8, n), jnp.float32)
        total = lax.fori_loop(0, n // step, functools.partial(count, ties), start)
        rank_ref[...] = jnp.sum(total, axis=0, keepdims=True).astype(jnp.int32)

    ranks(False)

    @pl.when(jnp.sum(rank_ref[...]) != n * (n - 1) // 2)
    def _():
        ranks(True)

    rank = rank_ref[...]
    rank_out[...] = rank[:, :local]
    fill_order(tile * local, rank, order_ref, 0, local)
    for copy in copies[5:]:
        copy.wait()
    block = jnp.concatenate([blocks_ref[i] for i in range(2 * half)], axis=1)
    everything = jnp.concatenate(
        [
            *[part.astype(jnp.float32) for part in three_parts(block)[:2]],
            *[part.astype(jnp.float32) for part in three_parts(places)],
            jnp.zeros((4, n), jnp.float32),
        ],
        axis=0,
    ).astype(jnp.bfloat16)
    parts = dot_nt(everything, order_ref[...])
    high, low = parts[:columns], parts[columns : 2 * columns]
    rounded_out[...] = high.astype(jnp.bfloat16)
    block_out[...] = high + low
    whole = (parts[2 * columns + 8 : 2 * columns + 12] + parts[2 * columns + 4 : 2 * columns + 8]) + parts[
        2 * columns : 2 * columns + 4
    ]
    lane = lax.broadcasted_iota(jnp.int32, (1, local), 1)
    flags = jnp.zeros((1, local), jnp.float32)
    for offset in range(owner_ref.shape[1]):
        flags = jnp.where((lane == offset) & (owned_ref[0, offset] >= 0), 1.0, flags)
    own_out[...] = jnp.concatenate([whole, flags, jnp.zeros((3, local), jnp.float32)], axis=0)
    places_out[...] = jnp.concatenate([whole[:3], flags], axis=0)


def sort_region(device, tile_owner, near, far, near_error, far_error, block, other):
    local = near.shape[2]
    n = local * 2 * near.shape[0]
    columns = block.shape[1]
    smem = pl.BlockSpec(memory_space=pltpu.SMEM)
    return pl.pallas_call(
        sort_kernel,
        out_shape=(
            jax.ShapeDtypeStruct((columns, local), jnp.bfloat16),
            jax.ShapeDtypeStruct((4, local), jnp.float32),
            jax.ShapeDtypeStruct((8, local), jnp.float32),
            jax.ShapeDtypeStruct((columns, local), jnp.float32),
            jax.ShapeDtypeStruct((1, local), jnp.int32),
        ),
        in_specs=[smem] + [pl.BlockSpec(memory_space=pl.ANY)] * 7,
        out_specs=tuple(whole_vmem(5)),
        scratch_shapes=[
            pltpu.VMEM((local, n), jnp.bfloat16),
            pltpu.VMEM((n, 8), jnp.float32),
            pltpu.VMEM((1, n), jnp.int32),
            pltpu.SMEM(tile_owner.shape, jnp.int32),
            pltpu.VMEM((n // local, 3, local), jnp.float32),
            pltpu.VMEM((n // local, 1, local), jnp.float32),
            pltpu.VMEM((n // local, columns, local), jnp.float32),
            pltpu.SemaphoreType.DMA((7,)),
        ],
        compiler_params=pltpu.CompilerParams(vmem_limit_bytes=VMEM),
        cost_estimate=pl.CostEstimate(
            flops=6 * n * local * (columns + 8), bytes_accessed=4 * n * local, transcendentals=0
        ),
        name="sort_region",
    )(device, in_hbm(tile_owner), in_hbm(near), far, in_hbm(near_error), far_error, in_hbm(block), other)


def unsort_kernel(device_ref, rank_ref, block_ref, block_out, order_ref):
    n, local = order_ref.shape
    tile = lax.rem(device_ref[0], n // local)
    for slot in range(n // local):
        fill_order((tile ^ slot) * local, rank_ref[...], order_ref, slot * local, local)
    block_out[...] = add_parts(dot_nn(stacked_parts(block_ref[...]), order_ref[...]))


def unsort(device, rank, block):
    n = block.shape[1]
    local = rank.shape[1]
    return pl.pallas_call(
        unsort_kernel,
        out_shape=jax.ShapeDtypeStruct((block.shape[0], local), jnp.float32),
        in_specs=[pl.BlockSpec(memory_space=pltpu.SMEM)] + whole_vmem(2),
        out_specs=whole_vmem(1)[0],
        scratch_shapes=[pltpu.VMEM((n, local), jnp.bfloat16)],
        compiler_params=pltpu.CompilerParams(vmem_limit_bytes=VMEM),
        cost_estimate=pl.CostEstimate(
            flops=20 * n * local * block.shape[0], bytes_accessed=4 * n * local, transcendentals=0
        ),
        name="unsort",
    )(device, rank, block)


def plan_blocks(
    distance_ref, own_ref, far_ref, chunks, stage_ref, bounds_ref, ids_ref, count_ref, sem, prepare,
):
    places, local = far_ref.shape[0], own_ref.shape[1]
    blocks = local // ROWS
    lane = lax.broadcasted_iota(jnp.int32, (1, LANES), 1)

    lowest = jnp.zeros((1, LANES), jnp.float32)
    highest = lowest
    for block in range(blocks):
        here = (lane == block) | (lane == blocks + block)
        low = own_ref[1:2, block * ROWS : block * ROWS + 1]
        high = own_ref[1:2, (block + 1) * ROWS - 1 : (block + 1) * ROWS]
        lowest = jnp.where(here, 2.0 * (low - CUTOFF), lowest)
        highest = jnp.where(here, 2.0 * (high + CUTOFF), highest)
    y = far_ref[:, 1, :]
    first = jnp.zeros((places, LANES), jnp.int32)
    beyond = first
    for chunk in range(chunks):
        low = y[:, chunk * LANES : chunk * LANES + 1]
        high = y[:, (chunk + 1) * LANES - 1 : (chunk + 1) * LANES]
        first = first + (high < lowest).astype(jnp.int32)
        beyond = beyond + (low <= highest).astype(jnp.int32)
    distance = distance_ref[...]
    flags = jnp.where((lane == -distance) & (far_ref[:, 3, :LANES] > 0.0), 1.0, 0.0)
    flags = flags + jnp.where(lane == distance, own_ref[4:5, :LANES], 0.0)
    listed = jnp.sum(flags, axis=1, keepdims=True) > 0.0
    found = jnp.where(listed, jnp.maximum(beyond - first, 0), 0)
    stage_ref[...] = jnp.where(lane < blocks, first, found)
    copy = pltpu.make_async_copy(stage_ref, bounds_ref, sem)
    copy.start()
    prepare()
    copy.wait()

    count = jnp.int32(0)
    for block in range(blocks):

        def add_place(place, count, block=block):
            entry = (block << ROW_SHIFT) + place * chunks + bounds_ref[place, block]
            for chunk in range(chunks):
                ids_ref[count + chunk] = entry + chunk
            return count + bounds_ref[place, blocks + block]

        count = lax.fori_loop(0, places, add_place, count, unroll=8)
        for extra in range(PAIR - 1):
            ids_ref[count + extra] = (block << ROW_SHIFT) + SKIP
        count = lax.div(count + PAIR - 1, PAIR) * PAIR
    for extra in range(BATCH - PAIR):
        ids_ref[count + extra] = SKIP
    count_ref[0] = lax.div(count + BATCH - 1, BATCH)


def gaspari_cohn(squared):
    squared = jnp.maximum(squared, 1e-12)
    inverse = lax.rsqrt(squared)
    scaled = squared * inverse
    near = (((-3.0 * scaled + 6.0) * scaled + 7.5) * scaled - 20.0) * squared + 12.0
    left = jnp.maximum(2.0 - scaled, 0.0)
    left = left * left
    far = (left * left) * (((scaled + 2.0) * scaled - 0.5) * inverse)
    return jnp.where(scaled <= 1.0, near, far)


def locate(ids_ref, batch, part, chunk_bits):
    entry = ids_ref[batch * BATCH + part]
    lane = pl.multiple_of((entry & ((1 << chunk_bits) - 1)) * LANES, LANES)
    start = pl.multiple_of(lax.shift_right_logical(entry, ROW_SHIFT) * ROWS, ROWS)
    place = lax.shift_right_logical(entry & (SKIP - 1), chunk_bits)
    return (entry & SKIP) == 0, place, pl.ds(lane, LANES), pl.ds(start, ROWS)


def build_kernel(
    part, device_ref, own_ref, near_ref, other_ref,
    ids_ref, count_ref, tiles_ref,
    wide_ref, far_ref, stage_ref, bounds_ref, bounds_sem, distance_ref,
):
    local = own_ref.shape[1]
    places = far_ref.shape[0]
    chunk_bits = (local // LANES).bit_length() - 1
    factor = jnp.where(lax.broadcasted_iota(jnp.int32, (4, 1), 0) < 2, 2.0, 1.0 / 12.0)
    tiles, regions = 2 * near_ref.shape[0], near_ref.shape[1]
    here, tile = lax.div(device_ref[0], tiles), lax.rem(device_ref[0], tiles)
    even, odd = slot_offsets(regions)
    size = regions // 2
    for index in range(places):
        other, slot = index // size, part * size + index % size
        offset = jnp.where((tile ^ other) & 1 == 0, even[slot], odd[slot])
        region = here ^ offset
        side_ref = near_ref if 2 * other < tiles else other_ref
        far_ref[index, 0:4, :] = factor * side_ref[other % (tiles // 2), region]
        distance_ref[index : index + 1, :] = jnp.full((1, LANES), region - here, jnp.int32)

    def prepare():
        column = jnp.transpose(own_ref[...])
        for row in range(3):
            scale = 2.0 if row < 2 else 1.0
            wide_ref[row] = jnp.broadcast_to(scale * column[:, row : row + 1], (local, LANES))

    plan_blocks(
        distance_ref, own_ref, far_ref, 1 << chunk_bits,
        stage_ref, bounds_ref, ids_ref, count_ref, bounds_sem, prepare,
    )
    total = count_ref[0]

    def build_batch(batch, carry):
        for part in range(BATCH):
            real, place, lanes, rows = locate(ids_ref, batch, part, chunk_bits)
            far = far_ref[place, :, lanes]
            across_x = wide_ref[0, rows, :] - far[0:1, :]
            across_y = wide_ref[1, rows, :] - far[1:2, :]
            value = gaspari_cohn(across_x * across_x + across_y * across_y)
            spread = jnp.where(real, far[2:3, :], 0.0)
            value = wide_ref[2, rows, :] * spread * value
            tiles_ref[batch, :, part * LANES : (part + 1) * LANES] = value.astype(jnp.bfloat16)
        return carry

    lax.fori_loop(0, total, build_batch, 0)


def build_tiles(part, device, own, near, far, capacity):
    places, local = near.shape[0] * near.shape[1], own.shape[1]
    smem = pl.BlockSpec(memory_space=pltpu.SMEM)
    sizes = (capacity * BATCH + local // LANES, 1)
    shape = (capacity, ROWS, BATCH * LANES)
    scratch = [
        pltpu.VMEM((3, local, LANES), jnp.float32),
        pltpu.VMEM((places, 8, local), jnp.float32),
        pltpu.VMEM((places, LANES), jnp.int32),
        pltpu.SMEM((places, LANES), jnp.int32),
        pltpu.SemaphoreType.DMA,
        pltpu.VMEM((places, LANES), jnp.int32),
    ]
    return pl.pallas_call(
        functools.partial(build_kernel, part),
        out_shape=tuple(jax.ShapeDtypeStruct((size,), jnp.int32) for size in sizes)
        + (pltpu.VMEM(shape, jnp.bfloat16),),
        in_specs=[smem] + whole_vmem(3),
        out_specs=(smem,) * 2 + (pl.BlockSpec(memory_space=pltpu.VMEM),),
        scratch_shapes=scratch,
        compiler_params=pltpu.CompilerParams(vmem_limit_bytes=VMEM),
        cost_estimate=pl.CostEstimate(
            flops=2 * local * local * 16000, bytes_accessed=16 * local * local, transcendentals=0
        ),
        name="build_tiles",
    )(device, own, near, far)


def apply_kernel(started, last, grams, ids_ref, count_ref, near_ref, other_ref, tiles_ref, *refs):
    refs = list(refs)
    start_ref = refs.pop(0) if started else None
    if last:
        first_ref = refs.pop(2) if grams else None
        block_ref, scale_ref, out_ref, rounded_ref = refs[:4]
        gram_ref = rounded_ref
        total_ref = refs[-1]
    else:
        (total_ref,) = refs
    half, columns, local = near_ref.shape
    chunk_bits = (local // LANES).bit_length() - 1
    total = count_ref[0]
    groups = lax.div(total + UNROLL - 1, UNROLL)

    if started:
        total_ref[...] = start_ref[...]
    else:
        total_ref[...] = jnp.zeros(total_ref.shape, jnp.float32)

    def turn(group, carry):
        values = []
        for inner in range(UNROLL):
            batch = jnp.minimum(group * UNROLL + inner, total - 1)
            valid = group * UNROLL + inner < total
            for pair in range(BATCH // PAIR):
                sides = []
                for part in range(pair * PAIR, (pair + 1) * PAIR):
                    _, place, chunk, rows = locate(ids_ref, batch, part, chunk_bits)
                    inside = jnp.where(place < half, place, place - half)
                    sides.append(
                        jnp.where(place < half, near_ref[inside, :, chunk], other_ref[inside, :, chunk])
                    )
                side = jnp.concatenate(sides, axis=1)
                if inner:
                    side = jnp.where(valid, side, jnp.zeros_like(side))
                lanes = slice(pair * PAIR * LANES, (pair + 1) * PAIR * LANES)
                values.append((rows, dot_nt(tiles_ref[batch, :, lanes], side)))
        for rows, value in values:
            total_ref[rows, :] += value
        return carry

    lax.fori_loop(0, groups, turn, 0)
    if last:
        block = block_ref[...]
        result = jnp.transpose(total_ref[...]) + scale_ref[...] * block
        out_ref[...] = result
        if not grams:
            rounded_ref[...] = result.astype(jnp.bfloat16)
        else:
            gram_ref[...] = jnp.concatenate([first_ref[...], packed_grams(block, result)], axis=1)


def apply_tiles(plan, near, far, tiles, start, finish):
    near, far = [piece.reshape((-1,) + piece.shape[2:]) for piece in (near, far)]
    half, columns, local = near.shape
    last = finish is not None
    grams = last and len(finish) > 2
    smem = pl.BlockSpec(memory_space=pltpu.SMEM)
    operands = [*plan, near, far, tiles]
    in_specs = [smem] * 2 + whole_vmem(3)
    if start is not None:
        operands.append(start)
        in_specs += whole_vmem(1)
    scratch = []
    if last:
        operands += finish
        in_specs += whole_vmem(len(finish))
        out_shape = (
            jax.ShapeDtypeStruct((columns, local), jnp.float32),
            jax.ShapeDtypeStruct((columns + 8, 2 * columns), jnp.float32)
            if grams
            else jax.ShapeDtypeStruct((columns, local), jnp.bfloat16),
        )
        scratch.append(pltpu.VMEM((local, columns), jnp.float32))
    else:
        out_shape = (jax.ShapeDtypeStruct((local, columns), jnp.float32),)
    return pl.pallas_call(
        functools.partial(apply_kernel, start is not None, last, grams),
        out_shape=out_shape,
        in_specs=in_specs,
        out_specs=tuple(whole_vmem(len(out_shape))),
        scratch_shapes=scratch,
        compiler_params=pltpu.CompilerParams(vmem_limit_bytes=VMEM),
        cost_estimate=pl.CostEstimate(
            flops=2 * local * local * 6000, bytes_accessed=16 * local * local, transcendentals=0
        ),
        name="apply_last" if last else "apply_first",
    )(*operands)


def packed_grams(left, right):
    n = left.shape[0]
    both = dot_nt(left, jnp.concatenate([left, right], axis=0), HIGHEST)
    square, mixed = both[:, :n], both[:, n:]
    mixed = 0.5 * (mixed + jnp.transpose(mixed))
    row, column = [lax.broadcasted_iota(jnp.int32, (n, n), axis) for axis in range(2)]
    diagonals = [
        jnp.sum(jnp.where(row == column, matrix, 0.0), axis=0, keepdims=True) for matrix in (square, mixed)
    ]
    rest = jnp.zeros((6, n), jnp.float32)
    return jnp.concatenate([jnp.where(row < column, square, mixed), *diagonals, rest], axis=0)


def unpacked_grams(packed):
    n = packed.shape[1]
    matrix = packed[:n]
    row, column = [lax.broadcasted_iota(jnp.int32, (n, n), axis) for axis in range(2)]
    upper = jnp.where(row < column, matrix, 0.0)
    lower = jnp.where(row > column, matrix, 0.0)
    diagonals = [jnp.where(row == column, packed[n + k : n + k + 1], 0.0) for k in range(2)]
    return upper + jnp.transpose(upper) + diagonals[0], lower + jnp.transpose(lower) + diagonals[1]


def grams_kernel(left_ref, right_ref, out_ref):
    out_ref[...] = packed_grams(left_ref[...], right_ref[...])


def first_grams(left, right):
    n = left.shape[0]
    return pl.pallas_call(
        grams_kernel,
        out_shape=jax.ShapeDtypeStruct((n + 8, n), jnp.float32),
        in_specs=whole_vmem(2),
        out_specs=whole_vmem(1)[0],
        compiler_params=pltpu.CompilerParams(vmem_limit_bytes=VMEM),
        cost_estimate=pl.CostEstimate(flops=2 * 10**9, bytes_accessed=8 * left.size, transcendentals=0),
        name="first_grams",
    )(left, right)


def small_product(left, right):
    return [[sum(l * r[j] for l, r in zip(row, right)) for j in range(len(right[0]))] for row in left]


def small_difference(left, right):
    return [[l - r for l, r in zip(*rows)] for rows in zip(left, right)]


def small_inverse(matrix):
    (a, b), (c, d) = matrix
    scale = 1.0 / (a * d - b * c)
    return [[d * scale, -b * scale], [-c * scale, a * scale]]


def solve_positive(matrix, target):
    n = matrix.shape[0]
    table = jnp.concatenate([0.5 * (matrix + jnp.transpose(matrix)), target], axis=1)
    bands = [table[k : k + 8, :] for k in range(0, n, 8)]
    row_index = lax.broadcasted_iota(jnp.int32, bands[0].shape, 0)
    for k in range(0, n, 4):
        own, row = k // 8, k % 8
        columns = [
            [jnp.broadcast_to(band[:, k + j : k + j + 1], band.shape) for band in bands] for j in range(4)
        ]
        pivot = [[columns[j][own][row + i : row + i + 1] for j in range(4)] for i in range(4)]
        upper, lower = pivot[:2], pivot[2:]
        top = small_inverse([r[:2] for r in upper])
        factor = small_product([r[:2] for r in lower], top)
        right = [r[2:] for r in upper]
        rest = small_inverse(small_difference([r[2:] for r in lower], small_product(factor, right)))
        rows = [[bands[own][row + i : row + i + 1]] for i in range(4)]
        last = small_product(rest, small_difference(rows[2:], small_product(factor, rows[:2])))
        first = small_product(top, small_difference(rows[:2], small_product(right, last)))
        new = [r[0] for r in first + last]
        bands = [
            band - ((columns[0][i] * new[0] + columns[1][i] * new[1]) + (columns[2][i] * new[2] + columns[3][i] * new[3]))
            for i, band in enumerate(bands)
        ]
        for i in range(4):
            bands[own] = jnp.where(row_index == row + i, new[i], bands[own])
    return jnp.concatenate([band[:, n:] for band in bands], axis=0)


def last_kernel(grams_ref, start_ref, images_ref, weights_ref, residual_ref):
    n = grams_ref.shape[1] // 2
    squares, mixed = unpacked_grams(grams_ref[:, :n])
    images, cross = unpacked_grams(grams_ref[:, n:])
    solved = solve_positive(mixed, jnp.concatenate([squares, images], axis=1))
    step, carried = solved[:, :n], solved[:, n:]
    product = dot_nn(images, solved, HIGHEST)
    second = solve_positive(cross - product[:, n:], mixed - product[:, :n])
    first = jnp.transpose(step - dot_nn(carried, second, HIGHEST))
    second = jnp.transpose(second)
    both = jnp.concatenate([first, second], axis=1)
    start, images = start_ref[...], images_ref[...]
    weights_ref[...] = dot_nn(both, jnp.concatenate([start, images[:n]], axis=0), HIGHEST)
    residual_ref[...] = start - dot_nn(both, images, HIGHEST)


def last_step(grams, start, images):
    return pl.pallas_call(
        last_kernel,
        out_shape=(jax.ShapeDtypeStruct(start.shape, jnp.float32),) * 2,
        in_specs=whole_vmem(3),
        out_specs=tuple(whole_vmem(2)),
        compiler_params=pltpu.CompilerParams(vmem_limit_bytes=VMEM),
        name="last_step",
    )(grams, start, images)


def shards(innovations, obs_geometry, obs_error, tile_owner):
    tiles_axis, regions = lax.axis_size("tile"), lax.axis_size("region")
    reach = tile_owner.shape[1]
    columns, local = innovations.shape
    device = lax.axis_index(("region", "tile")).astype(jnp.int32).reshape(1)
    rounded, places, own, start, rank = sort_region(
        device,
        tile_owner,
        *halves(obs_geometry, "tile"),
        *halves(obs_error[None, :], "tile"),
        *halves(innovations, "tile"),
    )
    scale = own[3:4]
    everywhere = jnp.broadcast_to(places[None], (regions,) + places.shape)
    everywhere = lax.all_to_all(everywhere, "region", 0, 0)
    near_places, far_places = halves(everywhere, "tile")

    half_regions = regions // 2
    most = min(half_regions, 2 * reach - 1) * tiles_axis * (local // LANES)
    batches = -(-(local // ROWS) * -(-most // PAIR) * PAIR // BATCH) + 1
    capacity = -(-batches // UNROLL) * UNROLL
    plans, tiles = [], []
    for part in range(2):
        *plan, built = build_tiles(part, device, own, near_places, far_places, capacity)
        plans.append(plan)
        tiles.append(built)

    def operate(sent, block, *grams):
        building = not grams
        total = None
        for part, group in enumerate(exchange(sent, *grams)):
            if building:
                group, plans[part] = lax.optimization_barrier((group, plans[part]))
            elif part:
                group, total = lax.optimization_barrier((group, total))
            near, far = halves(group, "tile")
            results = apply_tiles(
                plans[part], near, far, tiles[part], total, (block, scale, *grams) if part else None
            )
            total = results[0]
        return results

    image, image_rounded = operate(rounded, start)
    second, grams = operate(image_rounded, image, first_grams(start, image))
    near, far = halves(jnp.concatenate([image, second], axis=0), "tile")
    images = jnp.concatenate([*near, *far], axis=1)
    grams, images = sum_regions(sum_tiles(grams), images)
    return last_step(grams, innovations, unsort(device, rank, images))


def solution(mesh):
    return jax.shard_map(
        shards,
        mesh=mesh,
        in_specs=(
            P(None, ("region", "tile")),
            P(None, ("region", "tile")),
            P(("region", "tile")),
            P("region", None),
        ),
        out_specs=(P(None, ("region", "tile")), P(None, ("region", "tile"))),
        check_vma=False,
    )
```

```python
import functools

import jax
import jax.numpy as jnp
from jax import lax
from jax.experimental import pallas as pl
from jax.experimental.pallas import tpu as pltpu
from jax.sharding import PartitionSpec as P

CUTOFF = 1.001
ROW_SHIFT, SKIP = 20, 1 << 19
LANES = 128
ROWS = 64
PAIR = 2
BATCH = 2 * PAIR
UNROLL = 16
VMEM = 16 * 1024 * 1024
HIGHEST = lax.Precision.HIGHEST


def whole_vmem(count):
    return [pl.BlockSpec(memory_space=pltpu.VMEM)] * count


def in_hbm(value):
    return pltpu.with_memory_space_constraint(value, pltpu.HBM)


def dot_nt(left, right, precision=None):
    return lax.dot_general(
        left, right, (((1,), (1,)), ((), ())), precision=precision, preferred_element_type=jnp.float32
    )


def dot_nn(left, right, precision=None):
    return lax.dot_general(
        left, right, (((1,), (0,)), ((), ())), precision=precision, preferred_element_type=jnp.float32
    )


def three_parts(value):
    high = value.astype(jnp.bfloat16)
    rest = value - high.astype(jnp.float32)
    middle = rest.astype(jnp.bfloat16)
    low = (rest - middle.astype(jnp.float32)).astype(jnp.bfloat16)
    return high, middle, low


def halves(block, axis):
    count = lax.axis_size(axis)
    block = block[None]
    bit = 1
    while 2 * bit < count:
        block = jnp.concatenate([block, swapped(block, axis, bit)], axis=0)
        bit *= 2
    return block, swapped(block, axis, bit)


def swapped(block, axis, bit):
    return lax.ppermute(block, axis, [(i, i ^ bit) for i in range(lax.axis_size(axis))])


def sum_tiles(block):
    bit = 1
    while bit < lax.axis_size("tile"):
        block = block + swapped(block, "tile", bit)
        bit *= 2
    return block


def swap_regions(block, even, odd):
    tiles = lax.axis_size("tile")
    route = [
        (region * tiles + tile, (region ^ (odd if tile % 2 else even)) * tiles + tile)
        for region in range(lax.axis_size("region"))
        for tile in range(tiles)
    ]
    return lax.ppermute(block, ("region", "tile"), route)


def sum_regions(block, later):
    bits, _ = region_orders(lax.axis_size("region"))
    middle = len(bits) // 2
    for step, (even, odd) in enumerate(zip(bits, bits[middle:] + bits[:middle])):
        if step == len(bits) - 1:
            block, later = lax.optimization_barrier((block, later))
        block = block + swap_regions(block, even, odd)
    return block, later


def region_orders(count):
    bits = []
    bit = count // 2
    while bit:
        bits.append(bit)
        bit //= 2
    return bits, bits[:1] + bits[-1:] + bits[1:-1] if len(bits) > 2 else bits[::-1]


def slot_offsets(count):
    table = []
    for bits in region_orders(count):
        offsets = [0]
        for bit in bits:
            offsets = offsets + [offset ^ bit for offset in offsets]
        table.append(offsets)
    return table


def exchange(block, *beside):
    regions = lax.axis_size("region")
    block = block[None]
    for even, odd in zip(*region_orders(regions)):
        other = swap_regions(block, even, odd)
        if 2 * block.shape[0] == regions:
            return block, other
        other, *beside = lax.optimization_barrier((other, *beside))
        block = jnp.concatenate([block, other], axis=0)


def stacked_parts(value):
    return jnp.concatenate([part.astype(jnp.float32) for part in three_parts(value)], axis=0).astype(
        jnp.bfloat16
    )


def add_parts(value):
    rows = value.shape[0] // 3
    return (value[2 * rows :] + value[rows : 2 * rows]) + value[:rows]


def fill_order(first, rank, order_ref, row, count):
    step = 64

    def fill(block, carry):
        start = pl.multiple_of(block * step, step)
        place = first + start + lax.broadcasted_iota(jnp.int32, (step, rank.shape[1]), 0)
        order_ref[pl.ds(pl.multiple_of(row + start, step), step), :] = jnp.where(
            place == rank, 1.0, 0.0
        ).astype(jnp.bfloat16)
        return carry

    lax.fori_loop(0, count // step, fill, 0)


def sort_kernel(
    device_ref, owner_ref, near_ref, far_ref, near_error_ref, far_error_ref, block_ref, other_ref,
    rounded_out, places_out, own_out, block_out, rank_out,
    order_ref, column_ref, rank_ref, owned_ref, places_ref, errors_ref, blocks_ref, sems,
):
    columns, local = block_out.shape
    half = block_ref.shape[0]
    tile = lax.rem(device_ref[0], 2 * half)
    pairs = [(owner_ref, owned_ref)]
    for sources, target in (
        ((near_ref, far_ref), places_ref),
        ((near_error_ref, far_error_ref), errors_ref),
        ((block_ref, other_ref), blocks_ref),
    ):
        pairs += [(ref, target.at[pl.ds(part * half, half)]) for part, ref in enumerate(sources)]
    copies = [
        pltpu.make_async_copy(source, target, sems.at[index])
        for index, (source, target) in enumerate(pairs)
    ]
    for copy in copies:
        copy.start()
    for copy in copies[:5]:
        copy.wait()
    places = jnp.concatenate(
        [jnp.concatenate([places_ref[i], errors_ref[i]], axis=0) for i in range(2 * half)], axis=1
    )
    n = places.shape[1]
    step = 64
    index = jnp.concatenate(
        [
            ((tile ^ i) * local + lax.broadcasted_iota(jnp.int32, (1, local), 1)).astype(jnp.float32)
            for i in range(n // local)
        ],
        axis=1,
    )
    y_row = places[1:2, :]
    column_ref[...] = jnp.transpose(
        jnp.concatenate([y_row, index, jnp.zeros((6, n), jnp.float32)], axis=0)
    )

    def count(ties, block, total):
        start = pl.multiple_of(block * step, step)
        y_column = jnp.broadcast_to(column_ref[pl.ds(start, step), 0:1], (step, n))
        before = y_column < y_row
        if ties:
            index_column = jnp.broadcast_to(column_ref[pl.ds(start, step), 1:2], (step, n))
            before = before | ((y_column == y_row) & (index_column < index))
        return total + jnp.sum(jnp.where(before, 1.0, 0.0).reshape(step // 8, 8, n), axis=0)

    def ranks(ties):
        start = jnp.zeros((8, n), jnp.float32)
        total = lax.fori_loop(0, n // step, functools.partial(count, ties), start)
        rank_ref[...] = jnp.sum(total, axis=0, keepdims=True).astype(jnp.int32)

    ranks(False)

    @pl.when(jnp.sum(rank_ref[...]) != n * (n - 1) // 2)
    def _():
        ranks(True)

    rank = rank_ref[...]
    rank_out[...] = rank[:, :local]
    fill_order(tile * local, rank, order_ref, 0, local)
    for copy in copies[5:]:
        copy.wait()
    block = jnp.concatenate([blocks_ref[i] for i in range(2 * half)], axis=1)
    everything = jnp.concatenate(
        [
            *[part.astype(jnp.float32) for part in three_parts(block)[:2]],
            *[part.astype(jnp.float32) for part in three_parts(places)],
            jnp.zeros((4, n), jnp.float32),
        ],
        axis=0,
    ).astype(jnp.bfloat16)
    parts = dot_nt(everything, order_ref[...])
    high, low = parts[:columns], parts[columns : 2 * columns]
    rounded_out[...] = high.astype(jnp.bfloat16)
    block_out[...] = high + low
    whole = (parts[2 * columns + 8 : 2 * columns + 12] + parts[2 * columns + 4 : 2 * columns + 8]) + parts[
        2 * columns : 2 * columns + 4
    ]
    lane = lax.broadcasted_iota(jnp.int32, (1, local), 1)
    flags = jnp.zeros((1, local), jnp.float32)
    for offset in range(owner_ref.shape[1]):
        flags = jnp.where((lane == offset) & (owned_ref[0, offset] >= 0), 1.0, flags)
    own_out[...] = jnp.concatenate([whole, flags, jnp.zeros((3, local), jnp.float32)], axis=0)
    places_out[...] = jnp.concatenate([whole[:3], flags], axis=0)


def sort_region(device, tile_owner, near, far, near_error, far_error, block, other):
    local = near.shape[2]
    n = local * 2 * near.shape[0]
    columns = block.shape[1]
    smem = pl.BlockSpec(memory_space=pltpu.SMEM)
    return pl.pallas_call(
        sort_kernel,
        out_shape=(
            jax.ShapeDtypeStruct((columns, local), jnp.bfloat16),
            jax.ShapeDtypeStruct((4, local), jnp.float32),
            jax.ShapeDtypeStruct((8, local), jnp.float32),
            jax.ShapeDtypeStruct((columns, local), jnp.float32),
            jax.ShapeDtypeStruct((1, local), jnp.int32),
        ),
        in_specs=[smem] + [pl.BlockSpec(memory_space=pl.ANY)] * 7,
        out_specs=tuple(whole_vmem(5)),
        scratch_shapes=[
            pltpu.VMEM((local, n), jnp.bfloat16),
            pltpu.VMEM((n, 8), jnp.float32),
            pltpu.VMEM((1, n), jnp.int32),
            pltpu.SMEM(tile_owner.shape, jnp.int32),
            pltpu.VMEM((n // local, 3, local), jnp.float32),
            pltpu.VMEM((n // local, 1, local), jnp.float32),
            pltpu.VMEM((n // local, columns, local), jnp.float32),
            pltpu.SemaphoreType.DMA((7,)),
        ],
        compiler_params=pltpu.CompilerParams(vmem_limit_bytes=VMEM),
        cost_estimate=pl.CostEstimate(
            flops=6 * n * local * (columns + 8), bytes_accessed=4 * n * local, transcendentals=0
        ),
        name="sort_region",
    )(device, in_hbm(tile_owner), in_hbm(near), far, in_hbm(near_error), far_error, in_hbm(block), other)


def unsort_kernel(device_ref, rank_ref, block_ref, block_out, order_ref):
    n, local = order_ref.shape
    tile = lax.rem(device_ref[0], n // local)
    for slot in range(n // local):
        fill_order((tile ^ slot) * local, rank_ref[...], order_ref, slot * local, local)
    block_out[...] = add_parts(dot_nn(stacked_parts(block_ref[...]), order_ref[...]))


def unsort(device, rank, block):
    n = block.shape[1]
    local = rank.shape[1]
    return pl.pallas_call(
        unsort_kernel,
        out_shape=jax.ShapeDtypeStruct((block.shape[0], local), jnp.float32),
        in_specs=[pl.BlockSpec(memory_space=pltpu.SMEM)] + whole_vmem(2),
        out_specs=whole_vmem(1)[0],
        scratch_shapes=[pltpu.VMEM((n, local), jnp.bfloat16)],
        compiler_params=pltpu.CompilerParams(vmem_limit_bytes=VMEM),
        cost_estimate=pl.CostEstimate(
            flops=20 * n * local * block.shape[0], bytes_accessed=4 * n * local, transcendentals=0
        ),
        name="unsort",
    )(device, rank, block)


def plan_blocks(
    distance_ref, own_ref, far_ref, chunks, stage_ref, bounds_ref, ids_ref, count_ref, sem, prepare,
):
    places, local = far_ref.shape[0], own_ref.shape[1]
    blocks = local // ROWS
    lane = lax.broadcasted_iota(jnp.int32, (1, LANES), 1)

    lowest = jnp.zeros((1, LANES), jnp.float32)
    highest = lowest
    for block in range(blocks):
        here = (lane == block) | (lane == blocks + block)
        low = own_ref[1:2, block * ROWS : block * ROWS + 1]
        high = own_ref[1:2, (block + 1) * ROWS - 1 : (block + 1) * ROWS]
        lowest = jnp.where(here, 2.0 * (low - CUTOFF), lowest)
        highest = jnp.where(here, 2.0 * (high + CUTOFF), highest)
    y = far_ref[:, 1, :]
    first = jnp.zeros((places, LANES), jnp.int32)
    beyond = first
    for chunk in range(chunks):
        low = y[:, chunk * LANES : chunk * LANES + 1]
        high = y[:, (chunk + 1) * LANES - 1 : (chunk + 1) * LANES]
        first = first + (high < lowest).astype(jnp.int32)
        beyond = beyond + (low <= highest).astype(jnp.int32)
    distance = distance_ref[...]
    flags = jnp.where((lane == -distance) & (far_ref[:, 3, :LANES] > 0.0), 1.0, 0.0)
    flags = flags + jnp.where(lane == distance, own_ref[4:5, :LANES], 0.0)
    listed = jnp.sum(flags, axis=1, keepdims=True) > 0.0
    found = jnp.where(listed, jnp.maximum(beyond - first, 0), 0)
    stage_ref[...] = jnp.where(lane < blocks, first, found)
    copy = pltpu.make_async_copy(stage_ref, bounds_ref, sem)
    copy.start()
    prepare()
    copy.wait()

    count = jnp.int32(0)
    for block in range(blocks):

        def add_place(place, count, block=block):
            entry = (block << ROW_SHIFT) + place * chunks + bounds_ref[place, block]
            for chunk in range(chunks):
                ids_ref[count + chunk] = entry + chunk
            return count + bounds_ref[place, blocks + block]

        count = lax.fori_loop(0, places, add_place, count, unroll=8)
        for extra in range(PAIR - 1):
            ids_ref[count + extra] = (block << ROW_SHIFT) + SKIP
        count = lax.div(count + PAIR - 1, PAIR) * PAIR
    for extra in range(BATCH - PAIR):
        ids_ref[count + extra] = SKIP
    count_ref[0] = lax.div(count + BATCH - 1, BATCH)


def gaspari_cohn(squared):
    squared = jnp.maximum(squared, 1e-12)
    inverse = lax.rsqrt(squared)
    scaled = squared * inverse
    near = (((-3.0 * scaled + 6.0) * scaled + 7.5) * scaled - 20.0) * squared + 12.0
    left = jnp.maximum(2.0 - scaled, 0.0)
    left = left * left
    far = (left * left) * (((scaled + 2.0) * scaled - 0.5) * inverse)
    return jnp.where(scaled <= 1.0, near, far)


def locate(ids_ref, batch, part, chunk_bits):
    entry = ids_ref[batch * BATCH + part]
    lane = pl.multiple_of((entry & ((1 << chunk_bits) - 1)) * LANES, LANES)
    start = pl.multiple_of(lax.shift_right_logical(entry, ROW_SHIFT) * ROWS, ROWS)
    place = lax.shift_right_logical(entry & (SKIP - 1), chunk_bits)
    return (entry & SKIP) == 0, place, pl.ds(lane, LANES), pl.ds(start, ROWS)


def build_kernel(
    part, device_ref, own_ref, near_ref, other_ref,
    ids_ref, count_ref, tiles_ref,
    wide_ref, far_ref, stage_ref, bounds_ref, bounds_sem, distance_ref,
):
    local = own_ref.shape[1]
    places = far_ref.shape[0]
    chunk_bits = (local // LANES).bit_length() - 1
    factor = jnp.where(lax.broadcasted_iota(jnp.int32, (4, 1), 0) < 2, 2.0, 1.0 / 12.0)
    tiles, regions = 2 * near_ref.shape[0], near_ref.shape[1]
    here, tile = lax.div(device_ref[0], tiles), lax.rem(device_ref[0], tiles)
    even, odd = slot_offsets(regions)
    size = regions // 2
    for index in range(places):
        other, slot = index // size, part * size + index % size
        offset = jnp.where((tile ^ other) & 1 == 0, even[slot], odd[slot])
        region = here ^ offset
        side_ref = near_ref if 2 * other < tiles else other_ref
        far_ref[index, 0:4, :] = factor * side_ref[other % (tiles // 2), region]
        distance_ref[index : index + 1, :] = jnp.full((1, LANES), region - here, jnp.int32)

    def prepare():
        column = jnp.transpose(own_ref[...])
        for row in range(3):
            scale = 2.0 if row < 2 else 1.0
            wide_ref[row] = jnp.broadcast_to(scale * column[:, row : row + 1], (local, LANES))

    plan_blocks(
        distance_ref, own_ref, far_ref, 1 << chunk_bits,
        stage_ref, bounds_ref, ids_ref, count_ref, bounds_sem, prepare,
    )
    total = count_ref[0]

    def build_batch(batch, carry):
        for part in range(BATCH):
            real, place, lanes, rows = locate(ids_ref, batch, part, chunk_bits)
            far = far_ref[place, :, lanes]
            across_x = wide_ref[0, rows, :] - far[0:1, :]
            across_y = wide_ref[1, rows, :] - far[1:2, :]
            value = gaspari_cohn(across_x * across_x + across_y * across_y)
            spread = jnp.where(real, far[2:3, :], 0.0)
            value = wide_ref[2, rows, :] * spread * value
            tiles_ref[batch, :, part * LANES : (part + 1) * LANES] = value.astype(jnp.bfloat16)
        return carry

    lax.fori_loop(0, total, build_batch, 0)


def build_tiles(part, device, own, near, far, capacity):
    places, local = near.shape[0] * near.shape[1], own.shape[1]
    smem = pl.BlockSpec(memory_space=pltpu.SMEM)
    sizes = (capacity * BATCH + local // LANES, 1)
    shape = (capacity, ROWS, BATCH * LANES)
    scratch = [
        pltpu.VMEM((3, local, LANES), jnp.float32),
        pltpu.VMEM((places, 8, local), jnp.float32),
        pltpu.VMEM((places, LANES), jnp.int32),
        pltpu.SMEM((places, LANES), jnp.int32),
        pltpu.SemaphoreType.DMA,
        pltpu.VMEM((places, LANES), jnp.int32),
    ]
    return pl.pallas_call(
        functools.partial(build_kernel, part),
        out_shape=tuple(jax.ShapeDtypeStruct((size,), jnp.int32) for size in sizes)
        + (pltpu.VMEM(shape, jnp.bfloat16),),
        in_specs=[smem] + whole_vmem(3),
        out_specs=(smem,) * 2 + (pl.BlockSpec(memory_space=pltpu.VMEM),),
        scratch_shapes=scratch,
        compiler_params=pltpu.CompilerParams(vmem_limit_bytes=VMEM),
        cost_estimate=pl.CostEstimate(
            flops=2 * local * local * 16000, bytes_accessed=16 * local * local, transcendentals=0
        ),
        name="build_tiles",
    )(device, own, near, far)


def apply_kernel(started, last, grams, ids_ref, count_ref, near_ref, other_ref, tiles_ref, *refs):
    refs = list(refs)
    start_ref = refs.pop(0) if started else None
    if last:
        first_ref = refs.pop(2) if grams else None
        block_ref, scale_ref, out_ref, rounded_ref = refs[:4]
        total_ref = refs[-1]
    else:
        (total_ref,) = refs
    half, columns, local = near_ref.shape
    chunk_bits = (local // LANES).bit_length() - 1
    total = count_ref[0]
    groups = lax.div(total + UNROLL - 1, UNROLL)

    if started:
        total_ref[...] = start_ref[...]
    else:
        total_ref[...] = jnp.zeros(total_ref.shape, jnp.float32)

    def turn(group, carry):
        values = []
        for inner in range(UNROLL):
            batch = jnp.minimum(group * UNROLL + inner, total - 1)
            valid = group * UNROLL + inner < total
            for pair in range(BATCH // PAIR):
                sides = []
                for part in range(pair * PAIR, (pair + 1) * PAIR):
                    _, place, chunk, rows = locate(ids_ref, batch, part, chunk_bits)
                    inside = jnp.where(place < half, place, place - half)
                    sides.append(
                        jnp.where(place < half, near_ref[inside, :, chunk], other_ref[inside, :, chunk])
                    )
                side = jnp.concatenate(sides, axis=1)
                if inner:
                    side = jnp.where(valid, side, jnp.zeros_like(side))
                lanes = slice(pair * PAIR * LANES, (pair + 1) * PAIR * LANES)
                values.append((rows, dot_nt(tiles_ref[batch, :, lanes], side)))
        for rows, value in values:
            total_ref[rows, :] += value
        return carry

    lax.fori_loop(0, groups, turn, 0)
    if last:
        block = block_ref[...]
        result = jnp.transpose(total_ref[...]) + scale_ref[...] * block
        out_ref[...] = result
        rounded_ref[...] = result.astype(jnp.bfloat16)
        if grams:
            refs[4][...] = jnp.concatenate([first_ref[...], packed_grams(block, result)], axis=1)


def apply_tiles(plan, near, far, tiles, start, finish):
    near, far = [piece.reshape((-1,) + piece.shape[2:]) for piece in (near, far)]
    half, columns, local = near.shape
    last = finish is not None
    grams = last and len(finish) > 2
    smem = pl.BlockSpec(memory_space=pltpu.SMEM)
    operands = [*plan, near, far, tiles]
    in_specs = [smem] * 2 + whole_vmem(3)
    if start is not None:
        operands.append(start)
        in_specs += whole_vmem(1)
    scratch = []
    if last:
        operands += finish
        in_specs += whole_vmem(len(finish))
        out_shape = (
            jax.ShapeDtypeStruct((columns, local), jnp.float32),
            jax.ShapeDtypeStruct((columns, local), jnp.bfloat16),
        )
        if grams:
            out_shape += (jax.ShapeDtypeStruct((columns + 8, 2 * columns), jnp.float32),)
        scratch.append(pltpu.VMEM((local, columns), jnp.float32))
    else:
        out_shape = (jax.ShapeDtypeStruct((local, columns), jnp.float32),)
    return pl.pallas_call(
        functools.partial(apply_kernel, start is not None, last, grams),
        out_shape=out_shape,
        in_specs=in_specs,
        out_specs=tuple(whole_vmem(len(out_shape))),
        scratch_shapes=scratch,
        compiler_params=pltpu.CompilerParams(vmem_limit_bytes=VMEM),
        cost_estimate=pl.CostEstimate(
            flops=2 * local * local * 6000, bytes_accessed=16 * local * local, transcendentals=0
        ),
        name="apply_last" if last else "apply_first",
    )(*operands)


def packed_grams(left, right):
    n = left.shape[0]
    both = dot_nt(left, jnp.concatenate([left, right], axis=0), HIGHEST)
    square, mixed = both[:, :n], both[:, n:]
    mixed = 0.5 * (mixed + jnp.transpose(mixed))
    row, column = [lax.broadcasted_iota(jnp.int32, (n, n), axis) for axis in range(2)]
    diagonals = [
        jnp.sum(jnp.where(row == column, matrix, 0.0), axis=0, keepdims=True) for matrix in (square, mixed)
    ]
    rest = jnp.zeros((6, n), jnp.float32)
    return jnp.concatenate([jnp.where(row < column, square, mixed), *diagonals, rest], axis=0)


def unpacked_grams(packed):
    n = packed.shape[1]
    matrix = packed[:n]
    row, column = [lax.broadcasted_iota(jnp.int32, (n, n), axis) for axis in range(2)]
    upper = jnp.where(row < column, matrix, 0.0)
    lower = jnp.where(row > column, matrix, 0.0)
    diagonals = [jnp.where(row == column, packed[n + k : n + k + 1], 0.0) for k in range(2)]
    return upper + jnp.transpose(upper) + diagonals[0], lower + jnp.transpose(lower) + diagonals[1]


def grams_kernel(left_ref, right_ref, out_ref):
    out_ref[...] = packed_grams(left_ref[...], right_ref[...])


def first_grams(left, right):
    n = left.shape[0]
    return pl.pallas_call(
        grams_kernel,
        out_shape=jax.ShapeDtypeStruct((n + 8, n), jnp.float32),
        in_specs=whole_vmem(2),
        out_specs=whole_vmem(1)[0],
        compiler_params=pltpu.CompilerParams(vmem_limit_bytes=VMEM),
        cost_estimate=pl.CostEstimate(flops=2 * 10**9, bytes_accessed=8 * left.size, transcendentals=0),
        name="first_grams",
    )(left, right)


def small_product(left, right):
    return [[sum(l * r[j] for l, r in zip(row, right)) for j in range(len(right[0]))] for row in left]


def small_difference(left, right):
    return [[l - r for l, r in zip(*rows)] for rows in zip(left, right)]


def small_inverse(matrix):
    (a, b), (c, d) = matrix
    scale = 1.0 / (a * d - b * c)
    return [[d * scale, -b * scale], [-c * scale, a * scale]]


def solve_positive(matrix, target):
    n = matrix.shape[0]
    table = jnp.concatenate([0.5 * (matrix + jnp.transpose(matrix)), target], axis=1)
    bands = [table[k : k + 8, :] for k in range(0, n, 8)]
    row_index = lax.broadcasted_iota(jnp.int32, bands[0].shape, 0)
    for k in range(0, n, 4):
        own, row = k // 8, k % 8
        columns = [
            [jnp.broadcast_to(band[:, k + j : k + j + 1], band.shape) for band in bands] for j in range(4)
        ]
        pivot = [[columns[j][own][row + i : row + i + 1] for j in range(4)] for i in range(4)]
        upper, lower = pivot[:2], pivot[2:]
        top = small_inverse([r[:2] for r in upper])
        factor = small_product([r[:2] for r in lower], top)
        right = [r[2:] for r in upper]
        rest = small_inverse(small_difference([r[2:] for r in lower], small_product(factor, right)))
        rows = [[bands[own][row + i : row + i + 1]] for i in range(4)]
        last = small_product(rest, small_difference(rows[2:], small_product(factor, rows[:2])))
        first = small_product(top, small_difference(rows[:2], small_product(right, last)))
        new = [r[0] for r in first + last]
        bands = [
            band - ((columns[0][i] * new[0] + columns[1][i] * new[1]) + (columns[2][i] * new[2] + columns[3][i] * new[3]))
            for i, band in enumerate(bands)
        ]
        for i in range(4):
            bands[own] = jnp.where(row_index == row + i, new[i], bands[own])
    return jnp.concatenate([band[:, n:] for band in bands], axis=0)


def last_kernel(grams_ref, start_ref, images_ref, weights_ref, residual_ref):
    n = grams_ref.shape[1] // 2
    squares, mixed = unpacked_grams(grams_ref[:, :n])
    images, cross = unpacked_grams(grams_ref[:, n:])
    solved = solve_positive(mixed, jnp.concatenate([squares, images], axis=1))
    step, carried = solved[:, :n], solved[:, n:]
    product = dot_nn(images, solved, HIGHEST)
    second = solve_positive(cross - product[:, n:], mixed - product[:, :n])
    first = jnp.transpose(step - dot_nn(carried, second, HIGHEST))
    second = jnp.transpose(second)
    both = jnp.concatenate([first, second], axis=1)
    start, images = start_ref[...], images_ref[...]
    weights_ref[...] = dot_nn(both, jnp.concatenate([start, images[:n]], axis=0), HIGHEST)
    residual_ref[...] = start - dot_nn(both, images, HIGHEST)


def last_step(grams, start, images):
    return pl.pallas_call(
        last_kernel,
        out_shape=(jax.ShapeDtypeStruct(start.shape, jnp.float32),) * 2,
        in_specs=whole_vmem(3),
        out_specs=tuple(whole_vmem(2)),
        compiler_params=pltpu.CompilerParams(vmem_limit_bytes=VMEM),
        name="last_step",
    )(grams, start, images)


def shards(innovations, obs_geometry, obs_error, tile_owner):
    tiles_axis, regions = lax.axis_size("tile"), lax.axis_size("region")
    reach = tile_owner.shape[1]
    columns, local = innovations.shape
    device = lax.axis_index(("region", "tile")).astype(jnp.int32).reshape(1)
    rounded, places, own, start, rank = sort_region(
        device,
        tile_owner,
        *halves(obs_geometry, "tile"),
        *halves(obs_error[None, :], "tile"),
        *halves(innovations, "tile"),
    )
    scale = own[3:4]
    everywhere = jnp.broadcast_to(places[None], (regions,) + places.shape)
    everywhere = lax.all_to_all(everywhere, "region", 0, 0)
    near_places, far_places = halves(everywhere, "tile")

    half_regions = regions // 2
    most = min(half_regions, 2 * reach - 1) * tiles_axis * (local // LANES)
    batches = -(-(local // ROWS) * -(-most // PAIR) * PAIR // BATCH) + 1
    capacity = -(-batches // UNROLL) * UNROLL
    plans, tiles = [], []
    for part in range(2):
        *plan, built = build_tiles(part, device, own, near_places, far_places, capacity)
        plans.append(plan)
        tiles.append(built)

    def operate(sent, block, *grams):
        building = not grams
        total = None
        for part, group in enumerate(exchange(sent, *grams)):
            if building:
                group, plans[part] = lax.optimization_barrier((group, plans[part]))
            elif part:
                group, total = lax.optimization_barrier((group, total))
            near, far = halves(group, "tile")
            results = apply_tiles(
                plans[part], near, far, tiles[part], total, (block, scale, *grams) if part else None
            )
            total = results[0]
        return results

    image, image_rounded = operate(rounded, start)
    second, _, grams = operate(image_rounded, image, first_grams(start, image))
    near, far = halves(jnp.concatenate([image, second], axis=0), "tile")
    images = jnp.concatenate([*near, *far], axis=1)
    grams, images = sum_regions(sum_tiles(grams), images)
    return last_step(grams, innovations, unsort(device, rank, images))


def solution(mesh):
    return jax.shard_map(
        shards,
        mesh=mesh,
        in_specs=(
            P(None, ("region", "tile")),
            P(None, ("region", "tile")),
            P(("region", "tile")),
            P("region", None),
        ),
        out_specs=(P(None, ("region", "tile")), P(None, ("region", "tile"))),
        check_vma=False,
    )
```

```python
import functools

import jax
import jax.numpy as jnp
from jax import lax
from jax.experimental import pallas as pl
from jax.experimental.pallas import tpu as pltpu
from jax.sharding import PartitionSpec as P

CUTOFF = 1.001
ROW_SHIFT, SKIP = 20, 1 << 19
LANES = 128
ROWS = 64
PAIR = 2
BATCH = 2 * PAIR
UNROLL = 16
VMEM = 16 * 1024 * 1024
HIGHEST = lax.Precision.HIGHEST


def whole_vmem(count):
    return [pl.BlockSpec(memory_space=pltpu.VMEM)] * count


def in_hbm(value):
    return pltpu.with_memory_space_constraint(value, pltpu.HBM)


def dot_nt(left, right, precision=None):
    return lax.dot_general(
        left, right, (((1,), (1,)), ((), ())), precision=precision, preferred_element_type=jnp.float32
    )


def dot_nn(left, right, precision=None):
    return lax.dot_general(
        left, right, (((1,), (0,)), ((), ())), precision=precision, preferred_element_type=jnp.float32
    )


def three_parts(value):
    high = value.astype(jnp.bfloat16)
    rest = value - high.astype(jnp.float32)
    middle = rest.astype(jnp.bfloat16)
    low = (rest - middle.astype(jnp.float32)).astype(jnp.bfloat16)
    return high, middle, low


def halves(block, axis):
    count = lax.axis_size(axis)
    block = block[None]
    bit = 1
    while 2 * bit < count:
        block = jnp.concatenate([block, swapped(block, axis, bit)], axis=0)
        bit *= 2
    return block, swapped(block, axis, bit)


def swapped(block, axis, bit):
    return lax.ppermute(block, axis, [(i, i ^ bit) for i in range(lax.axis_size(axis))])


def sum_tiles(block):
    bit = 1
    while bit < lax.axis_size("tile"):
        block = block + swapped(block, "tile", bit)
        bit *= 2
    return block


def swap_regions(block, even, odd):
    tiles = lax.axis_size("tile")
    route = [
        (region * tiles + tile, (region ^ (odd if tile % 2 else even)) * tiles + tile)
        for region in range(lax.axis_size("region"))
        for tile in range(tiles)
    ]
    return lax.ppermute(block, ("region", "tile"), route)


def sum_regions(block, later):
    bits, _ = region_orders(lax.axis_size("region"))
    middle = len(bits) // 2
    for step, (even, odd) in enumerate(zip(bits, bits[middle:] + bits[:middle])):
        if step == len(bits) - 1:
            block, later = lax.optimization_barrier((block, later))
        block = block + swap_regions(block, even, odd)
    return block, later


def region_orders(count):
    bits = []
    bit = count // 2
    while bit:
        bits.append(bit)
        bit //= 2
    return bits, bits[:1] + bits[-1:] + bits[1:-1] if len(bits) > 2 else bits[::-1]


def slot_offsets(count):
    table = []
    for bits in region_orders(count):
        offsets = [0]
        for bit in bits:
            offsets = offsets + [offset ^ bit for offset in offsets]
        table.append(offsets)
    return table


def exchange(block, *beside):
    regions = lax.axis_size("region")
    block = block[None]
    steps = []
    for even, odd in zip(*region_orders(regions)):
        other = swap_regions(block, even, odd)
        steps.append(other)
        if 2 * block.shape[0] == regions:
            return block, *steps[-1:-4:-1]
        other, *beside = lax.optimization_barrier((other, *beside))
        block = jnp.concatenate([block, other], axis=0)


def stacked_parts(value):
    return jnp.concatenate([part.astype(jnp.float32) for part in three_parts(value)], axis=0).astype(
        jnp.bfloat16
    )


def add_parts(value):
    rows = value.shape[0] // 3
    return (value[2 * rows :] + value[rows : 2 * rows]) + value[:rows]


def fill_order(first, rank, order_ref, row, count):
    step = 64

    def fill(block, carry):
        start = pl.multiple_of(block * step, step)
        place = first + start + lax.broadcasted_iota(jnp.int32, (step, rank.shape[1]), 0)
        order_ref[pl.ds(pl.multiple_of(row + start, step), step), :] = jnp.where(
            place == rank, 1.0, 0.0
        ).astype(jnp.bfloat16)
        return carry

    lax.fori_loop(0, count // step, fill, 0)


def sort_kernel(
    device_ref, owner_ref, near_ref, far_ref, near_error_ref, far_error_ref, block_ref, other_ref,
    rounded_out, places_out, own_out, block_out, rank_out,
    order_ref, column_ref, rank_ref, owned_ref, places_ref, errors_ref, blocks_ref, sems,
):
    columns, local = block_out.shape
    half = block_ref.shape[0]
    tile = lax.rem(device_ref[0], 2 * half)
    pairs = [(owner_ref, owned_ref)]
    for sources, target in (
        ((near_ref, far_ref), places_ref),
        ((near_error_ref, far_error_ref), errors_ref),
        ((block_ref, other_ref), blocks_ref),
    ):
        pairs += [(ref, target.at[pl.ds(part * half, half)]) for part, ref in enumerate(sources)]
    copies = [
        pltpu.make_async_copy(source, target, sems.at[index])
        for index, (source, target) in enumerate(pairs)
    ]
    for copy in copies:
        copy.start()
    for copy in copies[:5]:
        copy.wait()
    places = jnp.concatenate(
        [jnp.concatenate([places_ref[i], errors_ref[i]], axis=0) for i in range(2 * half)], axis=1
    )
    n = places.shape[1]
    step = 64
    index = jnp.concatenate(
        [
            ((tile ^ i) * local + lax.broadcasted_iota(jnp.int32, (1, local), 1)).astype(jnp.float32)
            for i in range(n // local)
        ],
        axis=1,
    )
    y_row = places[1:2, :]
    column_ref[...] = jnp.transpose(
        jnp.concatenate([y_row, index, jnp.zeros((6, n), jnp.float32)], axis=0)
    )

    def count(ties, block, total):
        start = pl.multiple_of(block * step, step)
        y_column = jnp.broadcast_to(column_ref[pl.ds(start, step), 0:1], (step, n))
        before = y_column < y_row
        if ties:
            index_column = jnp.broadcast_to(column_ref[pl.ds(start, step), 1:2], (step, n))
            before = before | ((y_column == y_row) & (index_column < index))
        return total + jnp.sum(jnp.where(before, 1.0, 0.0).reshape(step // 8, 8, n), axis=0)

    def ranks(ties):
        start = jnp.zeros((8, n), jnp.float32)
        total = lax.fori_loop(0, n // step, functools.partial(count, ties), start)
        rank_ref[...] = jnp.sum(total, axis=0, keepdims=True).astype(jnp.int32)

    ranks(False)

    @pl.when(jnp.sum(rank_ref[...]) != n * (n - 1) // 2)
    def _():
        ranks(True)

    rank = rank_ref[...]
    rank_out[...] = rank[:, :local]
    fill_order(tile * local, rank, order_ref, 0, local)
    for copy in copies[5:]:
        copy.wait()
    block = jnp.concatenate([blocks_ref[i] for i in range(2 * half)], axis=1)
    everything = jnp.concatenate(
        [
            *[part.astype(jnp.float32) for part in three_parts(block)[:2]],
            *[part.astype(jnp.float32) for part in three_parts(places)],
            jnp.zeros((4, n), jnp.float32),
        ],
        axis=0,
    ).astype(jnp.bfloat16)
    parts = dot_nt(everything, order_ref[...])
    high, low = parts[:columns], parts[columns : 2 * columns]
    rounded_out[...] = high.astype(jnp.bfloat16)
    block_out[...] = high + low
    whole = (parts[2 * columns + 8 : 2 * columns + 12] + parts[2 * columns + 4 : 2 * columns + 8]) + parts[
        2 * columns : 2 * columns + 4
    ]
    lane = lax.broadcasted_iota(jnp.int32, (1, local), 1)
    flags = jnp.zeros((1, local), jnp.float32)
    for offset in range(owner_ref.shape[1]):
        flags = jnp.where((lane == offset) & (owned_ref[0, offset] >= 0), 1.0, flags)
    own_out[...] = jnp.concatenate([whole, flags, jnp.zeros((3, local), jnp.float32)], axis=0)
    places_out[...] = jnp.concatenate([whole[:3], flags], axis=0)


def sort_region(device, tile_owner, near, far, near_error, far_error, block, other):
    local = near.shape[2]
    n = local * 2 * near.shape[0]
    columns = block.shape[1]
    smem = pl.BlockSpec(memory_space=pltpu.SMEM)
    return pl.pallas_call(
        sort_kernel,
        out_shape=(
            jax.ShapeDtypeStruct((columns, local), jnp.bfloat16),
            jax.ShapeDtypeStruct((4, local), jnp.float32),
            jax.ShapeDtypeStruct((8, local), jnp.float32),
            jax.ShapeDtypeStruct((columns, local), jnp.float32),
            jax.ShapeDtypeStruct((1, local), jnp.int32),
        ),
        in_specs=[smem] + [pl.BlockSpec(memory_space=pl.ANY)] * 7,
        out_specs=tuple(whole_vmem(5)),
        scratch_shapes=[
            pltpu.VMEM((local, n), jnp.bfloat16),
            pltpu.VMEM((n, 8), jnp.float32),
            pltpu.VMEM((1, n), jnp.int32),
            pltpu.SMEM(tile_owner.shape, jnp.int32),
            pltpu.VMEM((n // local, 3, local), jnp.float32),
            pltpu.VMEM((n // local, 1, local), jnp.float32),
            pltpu.VMEM((n // local, columns, local), jnp.float32),
            pltpu.SemaphoreType.DMA((7,)),
        ],
        compiler_params=pltpu.CompilerParams(vmem_limit_bytes=VMEM),
        cost_estimate=pl.CostEstimate(
            flops=6 * n * local * (columns + 8), bytes_accessed=4 * n * local, transcendentals=0
        ),
        name="sort_region",
    )(device, in_hbm(tile_owner), in_hbm(near), far, in_hbm(near_error), far_error, in_hbm(block), other)


def unsort_kernel(device_ref, rank_ref, block_ref, block_out, order_ref):
    n, local = order_ref.shape
    tile = lax.rem(device_ref[0], n // local)
    for slot in range(n // local):
        fill_order((tile ^ slot) * local, rank_ref[...], order_ref, slot * local, local)
    block_out[...] = add_parts(dot_nn(stacked_parts(block_ref[...]), order_ref[...]))


def unsort(device, rank, block):
    n = block.shape[1]
    local = rank.shape[1]
    return pl.pallas_call(
        unsort_kernel,
        out_shape=jax.ShapeDtypeStruct((block.shape[0], local), jnp.float32),
        in_specs=[pl.BlockSpec(memory_space=pltpu.SMEM)] + whole_vmem(2),
        out_specs=whole_vmem(1)[0],
        scratch_shapes=[pltpu.VMEM((n, local), jnp.bfloat16)],
        compiler_params=pltpu.CompilerParams(vmem_limit_bytes=VMEM),
        cost_estimate=pl.CostEstimate(
            flops=20 * n * local * block.shape[0], bytes_accessed=4 * n * local, transcendentals=0
        ),
        name="unsort",
    )(device, rank, block)


def plan_blocks(
    distance_ref, own_ref, far_ref, chunks, stage_ref, bounds_ref, ids_ref, count_ref, sem, prepare,
):
    places, local = far_ref.shape[0], own_ref.shape[1]
    blocks = local // ROWS
    lane = lax.broadcasted_iota(jnp.int32, (1, LANES), 1)

    lowest = jnp.zeros((1, LANES), jnp.float32)
    highest = lowest
    for block in range(blocks):
        here = (lane == block) | (lane == blocks + block)
        low = own_ref[1:2, block * ROWS : block * ROWS + 1]
        high = own_ref[1:2, (block + 1) * ROWS - 1 : (block + 1) * ROWS]
        lowest = jnp.where(here, 2.0 * (low - CUTOFF), lowest)
        highest = jnp.where(here, 2.0 * (high + CUTOFF), highest)
    y = far_ref[:, 1, :]
    first = jnp.zeros((places, LANES), jnp.int32)
    beyond = first
    for chunk in range(chunks):
        low = y[:, chunk * LANES : chunk * LANES + 1]
        high = y[:, (chunk + 1) * LANES - 1 : (chunk + 1) * LANES]
        first = first + (high < lowest).astype(jnp.int32)
        beyond = beyond + (low <= highest).astype(jnp.int32)
    distance = distance_ref[...]
    flags = jnp.where((lane == -distance) & (far_ref[:, 3, :LANES] > 0.0), 1.0, 0.0)
    flags = flags + jnp.where(lane == distance, own_ref[4:5, :LANES], 0.0)
    listed = jnp.sum(flags, axis=1, keepdims=True) > 0.0
    found = jnp.where(listed, jnp.maximum(beyond - first, 0), 0)
    stage_ref[...] = jnp.where(lane < blocks, first, found)
    copy = pltpu.make_async_copy(stage_ref, bounds_ref, sem)
    copy.start()
    prepare()
    copy.wait()

    count = jnp.int32(0)
    for block in range(blocks):

        def add_place(place, count, block=block):
            entry = (block << ROW_SHIFT) + place * chunks + bounds_ref[place, block]
            for chunk in range(chunks):
                ids_ref[count + chunk] = entry + chunk
            return count + bounds_ref[place, blocks + block]

        count = lax.fori_loop(0, places, add_place, count, unroll=8)
        for extra in range(PAIR - 1):
            ids_ref[count + extra] = (block << ROW_SHIFT) + SKIP
        count = lax.div(count + PAIR - 1, PAIR) * PAIR
    for extra in range(BATCH - PAIR):
        ids_ref[count + extra] = SKIP
    count_ref[0] = lax.div(count + BATCH - 1, BATCH)


def gaspari_cohn(squared):
    squared = jnp.maximum(squared, 1e-12)
    inverse = lax.rsqrt(squared)
    scaled = squared * inverse
    near = (((-3.0 * scaled + 6.0) * scaled + 7.5) * scaled - 20.0) * squared + 12.0
    left = jnp.maximum(2.0 - scaled, 0.0)
    left = left * left
    far = (left * left) * (((scaled + 2.0) * scaled - 0.5) * inverse)
    return jnp.where(scaled <= 1.0, near, far)


def locate(ids_ref, batch, part, chunk_bits):
    entry = ids_ref[batch * BATCH + part]
    lane = pl.multiple_of((entry & ((1 << chunk_bits) - 1)) * LANES, LANES)
    start = pl.multiple_of(lax.shift_right_logical(entry, ROW_SHIFT) * ROWS, ROWS)
    place = lax.shift_right_logical(entry & (SKIP - 1), chunk_bits)
    return (entry & SKIP) == 0, place, pl.ds(lane, LANES), pl.ds(start, ROWS)


def build_kernel(
    part, device_ref, own_ref, near_ref, other_ref,
    ids_ref, count_ref, tiles_ref,
    wide_ref, far_ref, stage_ref, bounds_ref, bounds_sem, distance_ref,
):
    local = own_ref.shape[1]
    places = far_ref.shape[0]
    chunk_bits = (local // LANES).bit_length() - 1
    factor = jnp.where(lax.broadcasted_iota(jnp.int32, (4, 1), 0) < 2, 2.0, 1.0 / 12.0)
    tiles, regions = 2 * near_ref.shape[0], near_ref.shape[1]
    here, tile = lax.div(device_ref[0], tiles), lax.rem(device_ref[0], tiles)
    even, odd = slot_offsets(regions)
    size = regions // 2
    for index in range(places):
        other, slot = index // size, part * size + index % size
        offset = jnp.where((tile ^ other) & 1 == 0, even[slot], odd[slot])
        region = here ^ offset
        side_ref = near_ref if 2 * other < tiles else other_ref
        far_ref[index, 0:4, :] = factor * side_ref[other % (tiles // 2), region]
        distance_ref[index : index + 1, :] = jnp.full((1, LANES), region - here, jnp.int32)

    def prepare():
        column = jnp.transpose(own_ref[...])
        for row in range(3):
            scale = 2.0 if row < 2 else 1.0
            wide_ref[row] = jnp.broadcast_to(scale * column[:, row : row + 1], (local, LANES))

    plan_blocks(
        distance_ref, own_ref, far_ref, 1 << chunk_bits,
        stage_ref, bounds_ref, ids_ref, count_ref, bounds_sem, prepare,
    )
    total = count_ref[0]

    def build_batch(batch, carry):
        for part in range(BATCH):
            real, place, lanes, rows = locate(ids_ref, batch, part, chunk_bits)
            far = far_ref[place, :, lanes]
            across_x = wide_ref[0, rows, :] - far[0:1, :]
            across_y = wide_ref[1, rows, :] - far[1:2, :]
            value = gaspari_cohn(across_x * across_x + across_y * across_y)
            spread = jnp.where(real, far[2:3, :], 0.0)
            value = wide_ref[2, rows, :] * spread * value
            tiles_ref[batch, :, part * LANES : (part + 1) * LANES] = value.astype(jnp.bfloat16)
        return carry

    lax.fori_loop(0, total, build_batch, 0)


def build_tiles(part, device, own, near, far, capacity):
    places, local = near.shape[0] * near.shape[1], own.shape[1]
    smem = pl.BlockSpec(memory_space=pltpu.SMEM)
    sizes = (capacity * BATCH + local // LANES, 1)
    shape = (capacity, ROWS, BATCH * LANES)
    scratch = [
        pltpu.VMEM((3, local, LANES), jnp.float32),
        pltpu.VMEM((places, 8, local), jnp.float32),
        pltpu.VMEM((places, LANES), jnp.int32),
        pltpu.SMEM((places, LANES), jnp.int32),
        pltpu.SemaphoreType.DMA,
        pltpu.VMEM((places, LANES), jnp.int32),
    ]
    return pl.pallas_call(
        functools.partial(build_kernel, part),
        out_shape=tuple(jax.ShapeDtypeStruct((size,), jnp.int32) for size in sizes)
        + (pltpu.VMEM(shape, jnp.bfloat16),),
        in_specs=[smem] + whole_vmem(3),
        out_specs=(smem,) * 2 + (pl.BlockSpec(memory_space=pltpu.VMEM),),
        scratch_shapes=scratch,
        compiler_params=pltpu.CompilerParams(vmem_limit_bytes=VMEM),
        cost_estimate=pl.CostEstimate(
            flops=2 * local * local * 16000, bytes_accessed=16 * local * local, transcendentals=0
        ),
        name="build_tiles",
    )(device, own, near, far)


def apply_kernel(started, last, grams, ids_ref, count_ref, near_ref, other_ref, tiles_ref, *refs):
    refs = list(refs)
    start_ref = refs.pop(0) if started else None
    if last:
        first_ref = refs.pop(2) if grams else None
        block_ref, scale_ref, out_ref, rounded_ref = refs[:4]
        total_ref = refs[-1]
    else:
        (total_ref,) = refs
    half, columns, local = near_ref.shape
    chunk_bits = (local // LANES).bit_length() - 1
    total = count_ref[0]
    groups = lax.div(total + UNROLL - 1, UNROLL)

    if started:
        total_ref[...] = start_ref[...]
    else:
        total_ref[...] = jnp.zeros(total_ref.shape, jnp.float32)

    def turn(group, carry):
        values = []
        for inner in range(UNROLL):
            batch = jnp.minimum(group * UNROLL + inner, total - 1)
            valid = group * UNROLL + inner < total
            for pair in range(BATCH // PAIR):
                sides = []
                for part in range(pair * PAIR, (pair + 1) * PAIR):
                    _, place, chunk, rows = locate(ids_ref, batch, part, chunk_bits)
                    inside = jnp.where(place < half, place, place - half)
                    sides.append(
                        jnp.where(place < half, near_ref[inside, :, chunk], other_ref[inside, :, chunk])
                    )
                side = jnp.concatenate(sides, axis=1)
                if inner:
                    side = jnp.where(valid, side, jnp.zeros_like(side))
                lanes = slice(pair * PAIR * LANES, (pair + 1) * PAIR * LANES)
                values.append((rows, dot_nt(tiles_ref[batch, :, lanes], side)))
        for rows, value in values:
            total_ref[rows, :] += value
        return carry

    lax.fori_loop(0, groups, turn, 0)
    if last:
        block = block_ref[...]
        result = jnp.transpose(total_ref[...]) + scale_ref[...] * block
        out_ref[...] = result
        rounded_ref[...] = result.astype(jnp.bfloat16)
        if grams:
            refs[4][...] = jnp.concatenate([first_ref[...], packed_grams(block, result)], axis=1)


def apply_tiles(plan, near, far, tiles, start, finish):
    near, far = [piece.reshape((-1,) + piece.shape[2:]) for piece in (near, far)]
    half, columns, local = near.shape
    last = finish is not None
    grams = last and len(finish) > 2
    smem = pl.BlockSpec(memory_space=pltpu.SMEM)
    operands = [*plan, near, far, tiles]
    in_specs = [smem] * 2 + whole_vmem(3)
    if start is not None:
        operands.append(start)
        in_specs += whole_vmem(1)
    scratch = []
    if last:
        operands += finish
        in_specs += whole_vmem(len(finish))
        out_shape = (
            jax.ShapeDtypeStruct((columns, local), jnp.float32),
            jax.ShapeDtypeStruct((columns, local), jnp.bfloat16),
        )
        if grams:
            out_shape += (jax.ShapeDtypeStruct((columns + 8, 2 * columns), jnp.float32),)
        scratch.append(pltpu.VMEM((local, columns), jnp.float32))
    else:
        out_shape = (jax.ShapeDtypeStruct((local, columns), jnp.float32),)
    return pl.pallas_call(
        functools.partial(apply_kernel, start is not None, last, grams),
        out_shape=out_shape,
        in_specs=in_specs,
        out_specs=tuple(whole_vmem(len(out_shape))),
        scratch_shapes=scratch,
        compiler_params=pltpu.CompilerParams(vmem_limit_bytes=VMEM),
        cost_estimate=pl.CostEstimate(
            flops=2 * local * local * 6000, bytes_accessed=16 * local * local, transcendentals=0
        ),
        name="apply_last" if last else "apply_first",
    )(*operands)


def packed_grams(left, right):
    n = left.shape[0]
    both = dot_nt(left, jnp.concatenate([left, right], axis=0), HIGHEST)
    square, mixed = both[:, :n], both[:, n:]
    mixed = 0.5 * (mixed + jnp.transpose(mixed))
    row, column = [lax.broadcasted_iota(jnp.int32, (n, n), axis) for axis in range(2)]
    diagonals = [
        jnp.sum(jnp.where(row == column, matrix, 0.0), axis=0, keepdims=True) for matrix in (square, mixed)
    ]
    rest = jnp.zeros((6, n), jnp.float32)
    return jnp.concatenate([jnp.where(row < column, square, mixed), *diagonals, rest], axis=0)


def unpacked_grams(packed):
    n = packed.shape[1]
    matrix = packed[:n]
    row, column = [lax.broadcasted_iota(jnp.int32, (n, n), axis) for axis in range(2)]
    upper = jnp.where(row < column, matrix, 0.0)
    lower = jnp.where(row > column, matrix, 0.0)
    diagonals = [jnp.where(row == column, packed[n + k : n + k + 1], 0.0) for k in range(2)]
    return upper + jnp.transpose(upper) + diagonals[0], lower + jnp.transpose(lower) + diagonals[1]


def grams_kernel(left_ref, right_ref, out_ref):
    out_ref[...] = packed_grams(left_ref[...], right_ref[...])


def first_grams(left, right):
    n = left.shape[0]
    return pl.pallas_call(
        grams_kernel,
        out_shape=jax.ShapeDtypeStruct((n + 8, n), jnp.float32),
        in_specs=whole_vmem(2),
        out_specs=whole_vmem(1)[0],
        compiler_params=pltpu.CompilerParams(vmem_limit_bytes=VMEM),
        cost_estimate=pl.CostEstimate(flops=2 * 10**9, bytes_accessed=8 * left.size, transcendentals=0),
        name="first_grams",
    )(left, right)


def small_product(left, right):
    return [[sum(l * r[j] for l, r in zip(row, right)) for j in range(len(right[0]))] for row in left]


def small_difference(left, right):
    return [[l - r for l, r in zip(*rows)] for rows in zip(left, right)]


def small_inverse(matrix):
    (a, b), (c, d) = matrix
    scale = 1.0 / (a * d - b * c)
    return [[d * scale, -b * scale], [-c * scale, a * scale]]


def solve_positive(matrix, target):
    n = matrix.shape[0]
    table = jnp.concatenate([0.5 * (matrix + jnp.transpose(matrix)), target], axis=1)
    bands = [table[k : k + 8, :] for k in range(0, n, 8)]
    row_index = lax.broadcasted_iota(jnp.int32, bands[0].shape, 0)
    for k in range(0, n, 4):
        own, row = k // 8, k % 8
        columns = [
            [jnp.broadcast_to(band[:, k + j : k + j + 1], band.shape) for band in bands] for j in range(4)
        ]
        pivot = [[columns[j][own][row + i : row + i + 1] for j in range(4)] for i in range(4)]
        upper, lower = pivot[:2], pivot[2:]
        top = small_inverse([r[:2] for r in upper])
        factor = small_product([r[:2] for r in lower], top)
        right = [r[2:] for r in upper]
        rest = small_inverse(small_difference([r[2:] for r in lower], small_product(factor, right)))
        rows = [[bands[own][row + i : row + i + 1]] for i in range(4)]
        last = small_product(rest, small_difference(rows[2:], small_product(factor, rows[:2])))
        first = small_product(top, small_difference(rows[:2], small_product(right, last)))
        new = [r[0] for r in first + last]
        bands = [
            band - ((columns[0][i] * new[0] + columns[1][i] * new[1]) + (columns[2][i] * new[2] + columns[3][i] * new[3]))
            for i, band in enumerate(bands)
        ]
        for i in range(4):
            bands[own] = jnp.where(row_index == row + i, new[i], bands[own])
    return jnp.concatenate([band[:, n:] for band in bands], axis=0)


def last_kernel(grams_ref, start_ref, images_ref, weights_ref, residual_ref):
    n = grams_ref.shape[1] // 2
    squares, mixed = unpacked_grams(grams_ref[:, :n])
    images, cross = unpacked_grams(grams_ref[:, n:])
    solved = solve_positive(mixed, jnp.concatenate([squares, images], axis=1))
    step, carried = solved[:, :n], solved[:, n:]
    product = dot_nn(images, solved, HIGHEST)
    second = solve_positive(cross - product[:, n:], mixed - product[:, :n])
    first = jnp.transpose(step - dot_nn(carried, second, HIGHEST))
    second = jnp.transpose(second)
    both = jnp.concatenate([first, second], axis=1)
    start, images = start_ref[...], images_ref[...]
    weights_ref[...] = dot_nn(both, jnp.concatenate([start, images[:n]], axis=0), HIGHEST)
    residual_ref[...] = start - dot_nn(both, images, HIGHEST)


def last_step(grams, start, images):
    return pl.pallas_call(
        last_kernel,
        out_shape=(jax.ShapeDtypeStruct(start.shape, jnp.float32),) * 2,
        in_specs=whole_vmem(3),
        out_specs=tuple(whole_vmem(2)),
        compiler_params=pltpu.CompilerParams(vmem_limit_bytes=VMEM),
        name="last_step",
    )(grams, start, images)


def shards(innovations, obs_geometry, obs_error, tile_owner):
    tiles_axis, regions = lax.axis_size("tile"), lax.axis_size("region")
    reach = tile_owner.shape[1]
    columns, local = innovations.shape
    device = lax.axis_index(("region", "tile")).astype(jnp.int32).reshape(1)
    rounded, places, own, start, rank = sort_region(
        device,
        tile_owner,
        *halves(obs_geometry, "tile"),
        *halves(obs_error[None, :], "tile"),
        *halves(innovations, "tile"),
    )
    scale = own[3:4]
    everywhere = jnp.broadcast_to(places[None], (regions,) + places.shape)
    everywhere = lax.all_to_all(everywhere, "region", 0, 0)
    *groups, _, before_third = exchange(rounded)
    everywhere, _ = lax.optimization_barrier((everywhere, before_third))
    near_places, far_places = halves(everywhere, "tile")

    half_regions = regions // 2
    most = min(half_regions, 2 * reach - 1) * tiles_axis * (local // LANES)
    batches = -(-(local // ROWS) * -(-most // PAIR) * PAIR // BATCH) + 1
    capacity = -(-batches // UNROLL) * UNROLL
    plans, tiles = [], []
    for part in range(2):
        *plan, built = build_tiles(part, device, own, near_places, far_places, capacity)
        plans.append(plan)
        tiles.append(built)

    def operate(groups, block, *grams):
        building = not grams
        total = None
        for part, group in enumerate(groups):
            if building:
                group, plans[part] = lax.optimization_barrier((group, plans[part]))
            elif part:
                group, total = lax.optimization_barrier((group, total))
            near, far = halves(group, "tile")
            results = apply_tiles(
                plans[part], near, far, tiles[part], total, (block, scale, *grams) if part else None
            )
            total = results[0]
        return results

    image, image_rounded = operate(groups, start)
    grams = first_grams(start, image)
    second, _, grams = operate(exchange(image_rounded, grams)[:2], image, grams)
    near, far = halves(jnp.concatenate([image, second], axis=0), "tile")
    images = jnp.concatenate([*near, *far], axis=1)
    grams, images = sum_regions(sum_tiles(grams), images)
    return last_step(grams, innovations, unsort(device, rank, images))


def solution(mesh):
    return jax.shard_map(
        shards,
        mesh=mesh,
        in_specs=(
            P(None, ("region", "tile")),
            P(None, ("region", "tile")),
            P(("region", "tile")),
            P("region", None),
        ),
        out_specs=(P(None, ("region", "tile")), P(None, ("region", "tile"))),
        check_vma=False,
    )
```
